32 devices in a mesh: seq: 8 (over z, x), tp: 4 (over y, core).
Axes of the slice: x: 2, y: 2, z: 4, core: 2. Of those that a mesh axis runs over, the one named last changes fastest.
Arguments:
- enc_input: bfloat16 [4096, 1024], P('seq'), may hold values from -6 to 6
- dec_input: bfloat16 [3, 4096, 1024], P(None, 'seq'), may hold values from -6 to 6
- enc_cotan: bfloat16 [4096, 1024], P('seq'), may hold values from -6 to 6
- dec_cotan: bfloat16 [3, 4096, 1024], P(None, 'seq'), may hold values from -6 to 6
- doc_lengths: int32 [16], replicated, may hold values from 64 to 512, as said below
- src_padding: int32 [4096], replicated, may hold values 0 or 1
- enc_qkv: bfloat16 [3, 1024, 1024], P(None, None, 'tp'), may hold values from -0.1875 to 0.1875
- enc_wout: bfloat16 [1024, 1024], P('tp'), may hold values from -1.5 to 1.5
- enc_gain: float32 [1024], replicated, may hold values from 0.1 to 1.9
- enc_bias: float32 [1024], replicated, may hold values from -2.5 to 2.5
- enc_up: bfloat16 [1024, 4096], P(None, 'tp'), may hold values from -0.1875 to 0.1875
- enc_down: bfloat16 [4096, 1024], P('tp'), may hold values from -0.1875 to 0.1875
- post_gain: float32 [1024], replicated, may hold values from 0.1 to 1.9
- post_bias: float32 [1024], replicated, may hold values from -2.5 to 2.5
- self_qkv: bfloat16 [3, 1024, 1024], P(None, None, 'tp'), may hold values from -0.1875 to 0.1875
- self_rel: bfloat16 [1024, 512], P(None, 'tp'), may hold values from -0.1875 to 0.1875
- self_wout: bfloat16 [1024, 1024], P('tp'), may hold values from -1.5 to 1.5
- self_gain: float32 [1024], replicated, may hold values from 0.1 to 1.9
- self_bias: float32 [1024], replicated, may hold values from -2.5 to 2.5
- cross_wq: bfloat16 [1024, 1024], P(None, 'tp'), may hold values from -0.1875 to 0.1875
- cross_wkv: bfloat16 [2, 1024, 1024], P(None, None, 'tp'), may hold values from -0.1875 to 0.1875
- cross_wout: bfloat16 [1024, 1024], P('tp'), may hold values from -1.5 to 1.5
- cross_gain: float32 [1024], replicated, may hold values from 0.1 to 1.9
- cross_bias: float32 [1024], replicated, may hold values from -2.5 to 2.5
- ffn_up: bfloat16 [1024, 4096], P(None, 'tp'), may hold values from -0.1875 to 0.1875
- ffn_down: bfloat16 [4096, 1024], P('tp'), may hold values from -0.1875 to 0.1875
- ffn_gain: float32 [1024], replicated, may hold values from 0.1 to 1.9
- ffn_bias: float32 [1024], replicated, may hold values from -2.5 to 2.5
Outputs:
- enc_output: bfloat16 [4096, 1024], P('seq')
- dec_output: bfloat16 [3, 4096, 1024], P(None, 'seq')
- enc_grad: bfloat16 [4096, 1024], P('seq')
- dec_grad: bfloat16 [3, 4096, 1024], P(None, 'seq')
- grad_enc_qkv: float32 [3, 1024, 1024], P(None, None, 'tp')
- grad_enc_wout: float32 [1024, 1024], P('tp')
- grad_enc_gain: float32 [1024], replicated
- grad_enc_bias: float32 [1024], replicated
- grad_enc_up: float32 [1024, 4096], P(None, 'tp')
- grad_enc_down: float32 [4096, 1024], P('tp')
- grad_post_gain: float32 [1024], replicated
- grad_post_bias: float32 [1024], replicated
- grad_self_qkv: float32 [3, 1024, 1024], P(None, None, 'tp')
- grad_self_rel: float32 [1024, 512], P(None, 'tp')
- grad_self_wout: float32 [1024, 1024], P('tp')
- grad_self_gain: float32 [1024], replicated
- grad_self_bias: float32 [1024], replicated
- grad_cross_wq: float32 [1024, 1024], P(None, 'tp')
- grad_cross_wkv: float32 [2, 1024, 1024], P(None, None, 'tp')
- grad_cross_wout: float32 [1024, 1024], P('tp')
- grad_cross_gain: float32 [1024], replicated
- grad_cross_bias: float32 [1024], replicated
- grad_ffn_up: float32 [1024, 4096], P(None, 'tp')
- grad_ffn_down: float32 [4096, 1024], P('tp')
- grad_ffn_gain: float32 [1024], replicated
- grad_ffn_bias: float32 [1024], replicated
The draws below stay inside these ranges and needn't reach their ends.
Inputs may be any that keep to these rules, and one draw needn't show every extreme that they name: `doc_lengths`: the lengths of the 16 documents in pack order; they sum to 4096, one is exactly 512 and one exactly 64.
All inputs are finite; a program needn't handle non-finite values.
Results may differ from the reference program's by a relative error of at most 0.03.
Values may be sent and summed in bfloat16 or wider, within the bound.
A program may use at most 384 MiB of HBM per device.

```python
import math
import jax
import jax.numpy as jnp
from jax import lax

D = 1024
HEADS = 16
HD = 64
FF = 4096
BUCKETS = 32
STREAMS = 3
DOC_MAX = 512
DOC_MIN = 64
TOK_DEV = 512
TOKENS = 4096


def draw_doc_lengths(key, part):
    key = jax.random.fold_in(key, 7)
    doc_count = TOKENS // (DOC_MAX // 2)
    middle = DOC_MAX // 2
    quarter = DOC_MAX // 4
    pair_count = (doc_count - 4) // 2
    shuffle = jax.random.permutation(jax.random.fold_in(key, 1), doc_count)
    transfers = jax.random.randint(jax.random.fold_in(key, 2), (pair_count,), 0, middle - DOC_MIN + 1)
    transfers = transfers.at[0].set(middle - DOC_MIN)
    planted = jnp.array([2 * quarter, -quarter, -quarter, 0], jnp.int32)
    change = jnp.concatenate([planted, jnp.stack([transfers, -transfers], 1).reshape(-1).astype(jnp.int32)])
    lengths = jnp.full((doc_count,), middle, jnp.int32).at[shuffle].add(change)
    return lengths.astype(jnp.int32)


def touch_ends(values, stream_key, low, top_value):
    extent = values.shape
    index_at = [jax.random.randint(jax.random.fold_in(stream_key, axis), (), 0, extent[axis]) for axis in range(len(extent))]
    values = values.at[tuple(index_at)].set(low)
    longest = extent.index(max(extent))
    index_at[longest] = (index_at[longest] + 1) % extent[longest]
    return values.at[tuple(index_at)].set(top_value)


def shard_levels(key, extent, shards, least, largest):
    level, own = 1.0, jax.random.fold_in(key, 6)
    for position, shards_of in shards:
        heights = jnp.exp(jax.random.uniform(jax.random.fold_in(own, position), (shards_of,), jnp.float32, least / len(shards), largest / len(shards)))
        level = level * jnp.repeat(heights, extent[position] // shards_of).reshape([-1 if axis == position else 1 for axis in range(len(extent))])
    return level


def normal_values(rng, shape, scale, reach, shards=(), kind=jnp.bfloat16):
    values = jax.random.normal(rng, shape, jnp.float32) * scale
    if len(shards) > 0:
        values = shard_levels(rng, shape, shards, -0.22, 0.18) * values
    return jnp.clip(values, min=-reach, max=reach).astype(kind)


def setup_inputs(seed: int = 0) -> dict:
    arg_keys = jax.random.split(jax.random.key(seed), 29)
    enc_input = normal_values(arg_keys[0], (TOKENS, D), 1.0, 6.0, ((0, 8),))
    dec_input = normal_values(arg_keys[1], (STREAMS, TOKENS, D), 1.0, 6.0, ((1, 8),))
    enc_cotan = normal_values(arg_keys[2], (TOKENS, D), 1.0, 6.0, ((0, 8),))
    dec_cotan = normal_values(arg_keys[3], (STREAMS, TOKENS, D), 1.0, 6.0, ((1, 8),))
    doc_lengths = draw_doc_lengths(jax.random.fold_in(arg_keys[28], 71), 0)
    src_padding = touch_ends((jax.random.randint(arg_keys[5], (TOKENS,), 0, 8) < 7).astype(jnp.int32), jax.random.fold_in(arg_keys[5], 1), 0, 1)
    enc_qkv = normal_values(arg_keys[6], (3, D, D), D ** -0.5, 0.1875, ((2, 4),))
    enc_wout = normal_values(arg_keys[7], (D, D), (D // 64) ** -0.5, 1.5, ((0, 4),))
    enc_gain = jnp.clip(1.0 + 0.18 * jax.random.normal(arg_keys[8], (D,), jnp.float32), 0.1, 1.9)
    enc_bias = normal_values(arg_keys[9], (D,), 0.5, 2.5, (), jnp.float32)
    enc_up = normal_values(arg_keys[10], (D, FF), D ** -0.5, 0.1875, ((1, 4),))
    enc_down = normal_values(arg_keys[11], (FF, D), (FF // 4) ** -0.5, 0.1875, ((0, 4),))
    post_gain = jnp.clip(1.0 + 0.18 * jax.random.normal(arg_keys[12], (D,), jnp.float32), 0.1, 1.9)
    post_bias = normal_values(arg_keys[13], (D,), 0.5, 2.5, (), jnp.float32)
    self_qkv = normal_values(arg_keys[14], (3, D, D), D ** -0.5, 0.1875, ((2, 4),))
    self_rel = normal_values(arg_keys[15], (D, HEADS * BUCKETS), D ** -0.5, 0.1875, ((1, 4),))
    self_wout = normal_values(arg_keys[16], (D, D), (D // 64) ** -0.5, 1.5, ((0, 4),))
    self_gain = jnp.clip(1.0 + 0.18 * jax.random.normal(arg_keys[17], (D,), jnp.float32), 0.1, 1.9)
    self_bias = normal_values(arg_keys[18], (D,), 0.5, 2.5, (), jnp.float32)
    cross_wq = normal_values(arg_keys[19], (D, D), D ** -0.5, 0.1875, ((1, 4),))
    cross_wkv = normal_values(arg_keys[20], (2, D, D), D ** -0.5, 0.1875, ((2, 4),))
    cross_wout = normal_values(arg_keys[21], (D, D), (D // 64) ** -0.5, 1.5, ((0, 4),))
    cross_gain = jnp.clip(1.0 + 0.18 * jax.random.normal(arg_keys[22], (D,), jnp.float32), 0.1, 1.9)
    cross_bias = normal_values(arg_keys[23], (D,), 0.5, 2.5, (), jnp.float32)
    ffn_up = normal_values(arg_keys[24], (D, FF), D ** -0.5, 0.1875, ((1, 4),))
    ffn_down = normal_values(arg_keys[25], (FF, D), (FF // 4) ** -0.5, 0.1875, ((0, 4),))
    ffn_gain = jnp.clip(1.0 + 0.18 * jax.random.normal(arg_keys[26], (D,), jnp.float32), 0.1, 1.9)
    ffn_bias = normal_values(arg_keys[27], (D,), 0.5, 2.5, (), jnp.float32)
    return dict(enc_input=enc_input, dec_input=dec_input, enc_cotan=enc_cotan, dec_cotan=dec_cotan, doc_lengths=doc_lengths, src_padding=src_padding, enc_qkv=enc_qkv, enc_wout=enc_wout, enc_gain=enc_gain, enc_bias=enc_bias, enc_up=enc_up, enc_down=enc_down, post_gain=post_gain, post_bias=post_bias, self_qkv=self_qkv, self_rel=self_rel, self_wout=self_wout, self_gain=self_gain, self_bias=self_bias, cross_wq=cross_wq, cross_wkv=cross_wkv, cross_wout=cross_wout, cross_gain=cross_gain, cross_bias=cross_bias, ffn_up=ffn_up, ffn_down=ffn_down, ffn_gain=ffn_gain, ffn_bias=ffn_bias)


@jax.custom_vjp
def low(v):
    return lax.optimization_barrier(v.astype(jnp.bfloat16)).astype(jnp.float32)

@jax.custom_vjp
def low_back(v):
    return v

def low_keep(v):
    return (low(v), None)

def low_pass(kept, grad):
    return (grad,)

def back_keep(v):
    return (v, None)

def back_low(kept, grad):
    return (low(grad),)
low.defvjp(low_keep, low_pass)
low_back.defvjp(back_keep, back_low)

def matmul(left, right):
    return jnp.dot(left, right, precision=lax.Precision.HIGHEST, preferred_element_type=jnp.float32)

def round_both(value):
    return low(low_back(value))

def bucket_of(offset):
    exact = BUCKETS // 2
    total = jnp.zeros(offset.shape, jnp.int32)
    for level in range(1, BUCKETS):
        if level < exact:
            bound = level
        else:
            bound = int(math.ceil(exact * (128.0 / exact) ** ((level - exact) / exact)))
        total = total + (offset >= bound).astype(jnp.int32)
    return total

def doc_index(positions, ends):
    return lax.optimization_barrier(jnp.sum((positions[:, None] >= ends[None, :]).astype(jnp.int32), 1))

def first_of(positions, starts, ends):
    owner = doc_index(positions, ends)
    match = owner[:, None] == jnp.arange(ends.shape[0], dtype=jnp.int32)[None, :]
    return lax.optimization_barrier(jnp.sum(jnp.where(match, starts[None, :], 0), 1)).astype(jnp.int32)

def gather_bias(table, buckets):
    heads = table.shape[1]
    spread = jnp.broadcast_to(buckets[None], (heads,) + buckets.shape)
    return jnp.take_along_axis(jnp.transpose(table, (1, 0, 2)), spread, axis=2)

def layer_norm(resid, gain, shift):
    mean = lax.optimization_barrier(jnp.mean(resid, -1, keepdims=True))
    centred = resid - mean
    variance = lax.optimization_barrier(jnp.mean(centred * centred, -1, keepdims=True))
    return centred * lax.rsqrt(variance + 1e-05) * gain + shift

def attend_block(queries, keys, values, bias, allowed, own_score, own_value):
    scale = queries.shape[-1] ** (-0.5)
    raw = jnp.einsum('qhe,khe->hqk', queries, keys, precision=lax.Precision.HIGHEST) * scale
    scores = low_back(raw)
    if bias is not None:
        scores = scores + bias
    scores = jnp.where(allowed[None], scores, -1e+30)
    if own_score is not None:
        scores = jnp.concatenate([scores, own_score[:, :, None]], 2)
    weights = low(jax.nn.softmax(scores, axis=-1))
    count = keys.shape[0]
    result = jnp.einsum('hqk,khe->qhe', weights[:, :, :count], values, precision=lax.Precision.HIGHEST)
    if own_value is not None:
        result = result + weights[:, :, count].T[:, :, None] * own_value
    return result

def attend_pack(queries, keys, values, table, kind, context, own_keys, own_values):
    ends, starts, padding = context
    width = DOC_MAX - 1
    block = TOK_DEV
    heads = queries.shape[1]
    wide_keys = jnp.pad(keys, ((width, width), (0, 0), (0, 0)))
    wide_values = jnp.pad(values, ((width, width), (0, 0), (0, 0)))
    wide_padding = jnp.pad(padding, (width, width))

    def one_block(index):
        start = (index * block).astype(jnp.int32)
        query_pos = start + jnp.arange(block, dtype=jnp.int32)
        key_pos = start - width + jnp.arange(block + 2 * width, dtype=jnp.int32)
        key_valid = (key_pos >= 0) & (key_pos < TOKENS)
        key_doc = jnp.where(key_valid, doc_index(key_pos, ends), -1)
        same = doc_index(query_pos, ends)[:, None] == key_doc[None, :]
        key_pad = lax.dynamic_slice_in_dim(wide_padding, start, block + 2 * width) == 1
        if kind == 'encoder':
            allowed = same & (key_pad[None, :] | (key_pos[None, :] == query_pos[:, None]))
        elif kind == 'cross':
            key_first = key_pos == first_of(key_pos, starts, ends)
            allowed = same & (key_pad[None, :] | key_first[None, :])
        elif kind == 'main':
            allowed = same & (key_pos[None, :] <= query_pos[:, None])
        else:
            allowed = same & (key_pos[None, :] < query_pos[:, None])
        block_queries = lax.dynamic_slice_in_dim(queries, start, block)
        block_keys = lax.dynamic_slice_in_dim(wide_keys, start, block + 2 * width)
        block_values = lax.dynamic_slice_in_dim(wide_values, start, block + 2 * width)
        bias = None
        own_score = None
        own_value = None
        if table is not None:
            block_table = lax.dynamic_slice_in_dim(table, start, block)
            bias = gather_bias(block_table, bucket_of(query_pos[:, None] - key_pos[None, :]))
            if own_keys is not None:
                block_own = lax.dynamic_slice_in_dim(own_keys, start, block)
                own_value = lax.dynamic_slice_in_dim(own_values, start, block)
                own_raw = lax.optimization_barrier(jnp.sum(block_queries * block_own, -1)) * block_queries.shape[-1] ** (-0.5)
                own_score = low_back(own_raw).T + block_table[:, :, 0].T
        return attend_block(block_queries, block_keys, block_values, bias, allowed, own_score, own_value)
    result = lax.map(jax.checkpoint(one_block), jnp.arange(TOKENS // block, dtype=jnp.int32))
    return result.reshape(TOKENS, heads, -1)

def forward(enc_input, dec_input, enc_qkv, enc_wout, enc_gain, enc_bias, enc_up, enc_down, post_gain, post_bias, self_qkv, self_rel, self_wout, self_gain, self_bias, cross_wq, cross_wkv, cross_wout, cross_gain, cross_bias, ffn_up, ffn_down, ffn_gain, ffn_bias, context):

    def split(flat):
        return flat.reshape(TOKENS, HEADS, HD)
    enc_low = low(enc_input)
    enc_queries = split(round_both(matmul(enc_low, enc_qkv[0])))
    enc_keys = split(round_both(matmul(enc_low, enc_qkv[1])))
    enc_values = split(round_both(matmul(enc_low, enc_qkv[2])))
    enc_att = attend_pack(enc_queries, enc_keys, enc_values, None, 'encoder', context, None, None)
    branch = low_back(matmul(round_both(enc_att.reshape(TOKENS, D)), enc_wout))
    enc_mid = layer_norm(enc_input + branch, enc_gain, enc_bias)
    hidden = low_back(matmul(low(enc_mid), enc_up))
    branch = low_back(matmul(low(jax.nn.gelu(hidden, approximate=False)), enc_down))
    enc_state = layer_norm(enc_mid + branch, post_gain, post_bias)
    dec_low = low(dec_input)
    queries = [split(round_both(matmul(dec_low[stream], self_qkv[0]))) for stream in range(STREAMS)]
    keys = [split(round_both(matmul(dec_low[stream], self_qkv[1]))) for stream in range(STREAMS)]
    values = [split(round_both(matmul(dec_low[stream], self_qkv[2]))) for stream in range(STREAMS)]
    tables = [low_back(matmul(dec_low[stream], self_rel)).reshape(TOKENS, HEADS, BUCKETS) for stream in range(STREAMS)]
    results = [attend_pack(queries[0], keys[0], values[0], tables[0], 'main', context, None, None)]
    for stream in range(1, STREAMS):
        results.append(attend_pack(queries[stream], keys[0], values[0], tables[stream], 'predict', context, keys[stream], values[stream]))
    self_att = jnp.stack(results).reshape(STREAMS, TOKENS, D)
    branch = low_back(matmul(round_both(self_att), self_wout))
    dec_first = layer_norm(dec_input + branch, self_gain, self_bias)
    enc_final_low = low(enc_state)
    cross_keys = split(round_both(matmul(enc_final_low, cross_wkv[0])))
    cross_values = split(round_both(matmul(enc_final_low, cross_wkv[1])))
    cross_queries = round_both(matmul(low(dec_first), cross_wq))
    results = [attend_pack(split(cross_queries[stream]), cross_keys, cross_values, None, 'cross', context, None, None) for stream in range(STREAMS)]
    cross_att = jnp.stack(results).reshape(STREAMS, TOKENS, D)
    branch = low_back(matmul(round_both(cross_att), cross_wout))
    dec_second = layer_norm(dec_first + branch, cross_gain, cross_bias)
    hidden = low_back(matmul(low(dec_second), ffn_up))
    branch = low_back(matmul(low(jax.nn.gelu(hidden, approximate=False)), ffn_down))
    dec_state = layer_norm(dec_second + branch, ffn_gain, ffn_bias)
    return (enc_state, dec_state)

def reference(enc_input, dec_input, enc_cotan, dec_cotan, doc_lengths, src_padding, enc_qkv, enc_wout, enc_gain, enc_bias, enc_up, enc_down, post_gain, post_bias, self_qkv, self_rel, self_wout, self_gain, self_bias, cross_wq, cross_wkv, cross_wout, cross_gain, cross_bias, ffn_up, ffn_down, ffn_gain, ffn_bias):
    ends = jnp.cumsum(doc_lengths).astype(jnp.int32)
    starts = (ends - doc_lengths).astype(jnp.int32)
    context = (ends, starts, src_padding)
    floats = [item.astype(jnp.float32) for item in (enc_input, dec_input, enc_qkv, enc_wout, enc_gain, enc_bias, enc_up, enc_down, post_gain, post_bias, self_qkv, self_rel, self_wout, self_gain, self_bias, cross_wq, cross_wkv, cross_wout, cross_gain, cross_bias, ffn_up, ffn_down, ffn_gain, ffn_bias)]

    def run(*values):
        return forward(*values, context)
    outputs, pull = jax.vjp(run, *floats)
    grads = pull((enc_cotan.astype(jnp.float32), dec_cotan.astype(jnp.float32)))
    return (outputs[0].astype(jnp.bfloat16), outputs[1].astype(jnp.bfloat16), grads[0].astype(jnp.bfloat16), grads[1].astype(jnp.bfloat16), grads[2], grads[3], grads[4], grads[5], grads[6], grads[7], grads[8], grads[9], grads[10], grads[11], grads[12], grads[13], grads[14], grads[15], grads[16], grads[17], grads[18], grads[19], grads[20], grads[21], grads[22], grads[23])
```

```python
import functools
import math

import jax
import jax.numpy as jnp
import numpy as np
from jax import lax
from jax.experimental import pallas as pl
from jax.experimental.pallas import tpu as pltpu
from jax.sharding import PartitionSpec as P

HD = 64
BUCKETS = 32
DOC_MAX = 512
PAIR = 2 * HD
BQ = 128
BK = 256
NEG = -1e30
VMEM_BYTES = 40 * 1024 * 1024

LOW = jnp.bfloat16
WIDE = jnp.float32


def bucket_bounds():
    exact = BUCKETS // 2
    bounds = []
    for level in range(1, BUCKETS):
        if level < exact:
            bounds.append(level)
        else:
            bounds.append(int(math.ceil(exact * (128.0 / exact) ** ((level - exact) / exact))))
    return bounds


def bucket_table(offsets):
    return sum((offsets >= bound).astype(np.int32) for bound in bucket_bounds())


def dot_nt(left, right):
    return lax.dot_general(left, right, (((1,), (1,)), ((), ())), preferred_element_type=WIDE)


def dot_nn(left, right):
    return lax.dot_general(left, right, (((1,), (0,)), ((), ())), preferred_element_type=WIDE)


def stack_heads(cells):
    lane = lax.broadcasted_iota(jnp.int32, cells.shape, 1)
    wide = cells.astype(WIDE)
    first = jnp.where(lane < HD, wide, 0.0)
    return jnp.concatenate([first, wide - first], 0)


def merge_heads(cells):
    half = cells.shape[0] // 2
    lane = lax.broadcasted_iota(jnp.int32, (half, cells.shape[1]), 1)
    return jnp.where(lane < HD, cells[:half], cells[half:])


def both_heads(mask, cells):
    return jnp.where(mask[None], cells.reshape(2, BQ, cells.shape[1]), NEG).reshape(cells.shape)


def pair_columns(cells, pair):
    return jnp.concatenate([cells[:, 2 * pair : 2 * pair + 1], cells[:, 2 * pair + 1 : 2 * pair + 2]], 0)


def put_columns(store, pair, column):
    lane = lax.broadcasted_iota(jnp.int32, store.shape, 1)
    store = jnp.where(lane == 2 * pair, column[:BQ], store)
    return jnp.where(lane == 2 * pair + 1, column[BQ:], store)


def fill_window(window, parts):
    rows = parts[0].shape[1]
    for place, part in enumerate(parts):
        window[:, place * rows : (place + 1) * rows, :] = part[...]


def full_mask(with_self, qdoc, kdoc_ref, block, query_at):
    allowed = qdoc == kdoc_ref[block]
    if with_self:
        row = lax.broadcasted_iota(jnp.int32, allowed.shape, 0) + query_at
        column = lax.broadcasted_iota(jnp.int32, allowed.shape, 1) + block * BK
        allowed = allowed | (row == column)
    return allowed


def full_forward_kernel(
    with_self,
    bounds_ref,
    q_ref,
    before_ref,
    here_ref,
    after_ref,
    qdoc_ref,
    kdoc_ref,
    att_ref,
    wide_ref,
    lse_ref,
    window,
    scores,
    top,
    total,
    gathered,
):
    stream, step = pl.program_id(0), pl.program_id(1)
    rows = here_ref.shape[1]
    pairs = here_ref.shape[2] // PAIR

    @pl.when((stream == 0) & (step == 0))
    def _():
        fill_window(window, (before_ref, here_ref, after_ref))

    low_block, high_block = bounds_ref[0, step], bounds_ref[1, step]
    qdoc = qdoc_ref[...]
    queries = [
        (stack_heads(q_ref[:, pair * PAIR : (pair + 1) * PAIR]) * HD**-0.5).astype(LOW)
        for pair in range(pairs)
    ]
    top[...] = jnp.full(top.shape, NEG, WIDE)
    total[...] = jnp.zeros(total.shape, WIDE)
    gathered[...] = jnp.zeros(gathered.shape, WIDE)

    def score_step(block, carry):
        allowed = full_mask(with_self, qdoc, kdoc_ref, block, rows + step * BQ)
        at = pl.ds(pl.multiple_of(block * BK, BK), BK)
        for pair in range(pairs):
            keys = window[0, at, pair * PAIR : (pair + 1) * PAIR]
            found = both_heads(allowed, dot_nt(queries[pair], keys))
            scores[block, pair] = found
            top[pair] = jnp.maximum(top[pair], jnp.maximum(found[:, :128], found[:, 128:]))
        return carry

    lax.fori_loop(low_block, high_block, score_step, 0)
    peaks = [jnp.max(top[pair], 1, keepdims=True) for pair in range(pairs)]

    def value_step(block, carry):
        at = pl.ds(pl.multiple_of(block * BK, BK), BK)
        for pair in range(pairs):
            values = window[1, at, pair * PAIR : (pair + 1) * PAIR]
            weights = jnp.exp(scores[block, pair] - peaks[pair])
            total[pair] += weights[:, :128] + weights[:, 128:]
            gathered[pair] += dot_nn(weights.astype(LOW), values)
        return carry

    lax.fori_loop(low_block, high_block, value_step, 0)
    lse = jnp.zeros((BQ, 128), WIDE)
    for pair in range(pairs):
        weight = jnp.sum(total[pair], 1, keepdims=True)
        result = merge_heads(gathered[pair] / weight)
        att_ref[:, pair * PAIR : (pair + 1) * PAIR] = result.astype(LOW)
        wide_ref[:, pair * PAIR : (pair + 1) * PAIR] = result
        lse = put_columns(lse, pair, peaks[pair] + jnp.log(weight))
    lse_ref[...] = lse


def full_backward_kernel(
    with_self,
    bounds_ref,
    q_ref,
    grad_ref,
    att_ref,
    lse_ref,
    before_ref,
    here_ref,
    after_ref,
    qdoc_ref,
    kdoc_ref,
    qgrad_ref,
    gbefore_ref,
    ghere_ref,
    gafter_ref,
    window,
    wgrad,
    qgrad,
):
    stream, step = pl.program_id(0), pl.program_id(1)
    rows = here_ref.shape[1]
    pairs = here_ref.shape[2] // PAIR

    @pl.when((stream == 0) & (step == 0))
    def _():
        fill_window(window, (before_ref, here_ref, after_ref))
        wgrad[...] = jnp.zeros(wgrad.shape, WIDE)

    low_block, high_block = bounds_ref[0, step], bounds_ref[1, step]
    qdoc = qdoc_ref[...]
    lse_all = lse_ref[...]
    queries, grads, queries_t, grads_t, deltas, logs = [], [], [], [], [], []
    for pair in range(pairs):
        cut = slice(pair * PAIR, (pair + 1) * PAIR)
        query = stack_heads(q_ref[:, cut]) * HD**-0.5
        grad = stack_heads(grad_ref[:, cut])
        att = att_ref[:, cut]
        deltas.append(jnp.sum(grad * jnp.concatenate([att, att], 0), 1, keepdims=True))
        logs.append(pair_columns(lse_all, pair))
        queries.append(query.astype(LOW))
        grads.append(grad.astype(LOW))
        queries_t.append(query.T.astype(LOW))
        grads_t.append(grad.T.astype(LOW))
    qgrad[...] = jnp.zeros(qgrad.shape, WIDE)

    def block_step(block, carry):
        allowed = full_mask(with_self, qdoc, kdoc_ref, block, rows + step * BQ)
        at = pl.ds(pl.multiple_of(block * BK, BK), BK)
        for pair in range(pairs):
            cut = slice(pair * PAIR, (pair + 1) * PAIR)
            keys = window[0, at, cut]
            values = window[1, at, cut]
            probs = jnp.exp(both_heads(allowed, dot_nt(queries[pair], keys)) - logs[pair])
            slopes = probs * (dot_nt(grads[pair], values) - deltas[pair])
            slopes = slopes.astype(LOW)
            qgrad[pair] += dot_nn(slopes, keys)
            wgrad[0, cut, at] += dot_nn(queries_t[pair], slopes)
            wgrad[1, cut, at] += dot_nn(grads_t[pair], probs.astype(LOW))
        return carry

    lax.fori_loop(low_block, high_block, block_step, 0)
    for pair in range(pairs):
        qgrad_ref[:, pair * PAIR : (pair + 1) * PAIR] = (
            merge_heads(qgrad[pair]) * HD**-0.5
        ).astype(LOW)

    @pl.when((stream == pl.num_programs(0) - 1) & (step == pl.num_programs(1) - 1))
    def _():
        gbefore_ref[...] = wgrad[:, :, :rows].astype(LOW)
        ghere_ref[...] = wgrad[:, :, rows : 2 * rows]
        gafter_ref[...] = wgrad[:, :, 2 * rows :].astype(LOW)


def causal_parts(own, table, gidx, pair):
    lane = lax.broadcasted_iota(jnp.int32, (BQ, 128), 1)
    row = lax.broadcasted_iota(jnp.int32, (BQ, 128), 0)
    near, far = [], []
    for head in (2 * pair, 2 * pair + 1):
        spread = jnp.take_along_axis(
            table, gidx + head * BUCKETS, axis=1, mode="promise_in_bounds"
        )
        last = table[:, head * BUCKETS + BUCKETS - 1 : head * BUCKETS + BUCKETS]
        near.append((jnp.where(lane > row, spread, last), spread))
        far.append(last)
    bias_before = jnp.concatenate([near[0][0], near[1][0]], 0)
    bias_here = jnp.concatenate([near[0][1], near[1][1]], 0)
    return bias_before, bias_here, jnp.concatenate(far, 0)


def own_column(table, pair):
    first, second = 2 * pair * BUCKETS, (2 * pair + 1) * BUCKETS
    return jnp.concatenate([table[:, first : first + 1], table[:, second : second + 1]], 0)


def causal_masks(own, qdoc, kdoc_ref, near):
    lane = lax.broadcasted_iota(jnp.int32, (BQ, 128), 1)
    row = lax.broadcasted_iota(jnp.int32, (BQ, 128), 0)
    earlier = (lane < row) if own else (lane <= row)
    return qdoc == kdoc_ref[near - 1], (qdoc == kdoc_ref[near]) & earlier


def causal_forward_kernel(own, *refs):
    bounds_ref, q_ref, before_ref, here_ref, qdoc_ref, kdoc_ref, table_ref, gidx_ref = refs[:8]
    refs = refs[8:]
    if own:
        own_ref, refs = refs[0], refs[1:]
    att_ref, wide_ref, lse_ref, window, scores, top, total, gathered = refs
    stream, step = pl.program_id(0), pl.program_id(1)
    rows = here_ref.shape[1]
    pairs = here_ref.shape[2] // PAIR

    @pl.when((stream == 0) & (step == 0))
    def _():
        fill_window(window, (before_ref, here_ref))

    near = rows // 128 + step
    low_block = bounds_ref[step]
    qdoc = qdoc_ref[...]
    table = table_ref[...]
    gidx = gidx_ref[...]
    queries, fars, peaks, owns = [], [], [], []
    mask_before, mask_here = causal_masks(own, qdoc, kdoc_ref, near)
    near_at = pl.ds(pl.multiple_of((near - 1) * 128, 128), 256)
    for pair in range(pairs):
        cut = slice(pair * PAIR, (pair + 1) * PAIR)
        query = stack_heads(q_ref[:, cut]) * HD**-0.5
        queries.append(query.astype(LOW))
        bias_before, bias_here, far = causal_parts(own, table, gidx, pair)
        fars.append(far)
        found = dot_nt(queries[pair], window[0, near_at, cut])
        found_before = both_heads(mask_before, found[:, :128] + bias_before)
        found_here = both_heads(mask_here, found[:, 128:] + bias_here)
        scores[near - 1, pair] = found_before
        scores[near, pair] = found_here
        top[pair] = jnp.maximum(found_before, found_here)
        if own:
            keys = own_ref[0, :, cut].astype(WIDE)
            owns.append(
                jnp.sum(query * jnp.concatenate([keys, keys], 0), 1, keepdims=True)
                + own_column(table, pair)
            )

    def score_step(block, carry):
        allowed = qdoc == kdoc_ref[block]
        at = pl.ds(pl.multiple_of(block * 128, 128), 128)
        for pair in range(pairs):
            keys = window[0, at, pair * PAIR : (pair + 1) * PAIR]
            found = both_heads(allowed, dot_nt(queries[pair], keys) + fars[pair])
            scores[block, pair] = found
            top[pair] = jnp.maximum(top[pair], found)
        return carry

    lax.fori_loop(low_block, near - 1, score_step, 0)
    for pair in range(pairs):
        cut = slice(pair * PAIR, (pair + 1) * PAIR)
        peak = jnp.max(top[pair], 1, keepdims=True)
        if own:
            peak = jnp.maximum(peak, owns[pair])
        peaks.append(peak)
        weights_before = jnp.exp(scores[near - 1, pair] - peak)
        weights_here = jnp.exp(scores[near, pair] - peak)
        total[pair] = weights_before + weights_here
        weights = jnp.concatenate([weights_before, weights_here], 1).astype(LOW)
        gathered[pair] = dot_nn(weights, window[1, near_at, cut])

    def value_step(block, carry):
        at = pl.ds(pl.multiple_of(block * 128, 128), 128)
        for pair in range(pairs):
            values = window[1, at, pair * PAIR : (pair + 1) * PAIR]
            weights = jnp.exp(scores[block, pair] - peaks[pair])
            total[pair] += weights
            gathered[pair] += dot_nn(weights.astype(LOW), values)
        return carry

    lax.fori_loop(low_block, near - 1, value_step, 0)
    lse = jnp.zeros((BQ, 128), WIDE)
    for pair in range(pairs):
        cut = slice(pair * PAIR, (pair + 1) * PAIR)
        weight = jnp.sum(total[pair], 1, keepdims=True)
        result = gathered[pair]
        if own:
            own_weight = jnp.exp(owns[pair] - peaks[pair])
            weight = weight + own_weight
            values = own_ref[1, :, cut].astype(WIDE)
            result = result + own_weight * jnp.concatenate([values, values], 0)
        result = merge_heads(result / weight)
        att_ref[:, cut] = result.astype(LOW)
        wide_ref[:, cut] = result
        lse = put_columns(lse, pair, peaks[pair] + jnp.log(weight))
    lse_ref[...] = lse


def causal_backward_kernel(own, *refs):
    bounds_ref, q_ref, grad_ref, att_ref, lse_ref, before_ref, here_ref = refs[:7]
    qdoc_ref, kdoc_ref, table_ref, gidx_ref, sidx_ref, hot_ref = refs[7:13]
    refs = refs[13:]
    if own:
        own_ref, refs = refs[0], refs[1:]
    qgrad_ref, tgrad_ref, gbefore_ref, ghere_ref = refs[:4]
    refs = refs[4:]
    if own:
        ograd_ref, refs = refs[0], refs[1:]
    window, wgrad, qgrad, farsum = refs
    stream, step = pl.program_id(0), pl.program_id(1)
    rows = here_ref.shape[1]
    pairs = here_ref.shape[2] // PAIR

    @pl.when((stream == 0) & (step == 0))
    def _():
        fill_window(window, (before_ref, here_ref))
        wgrad[...] = jnp.zeros(wgrad.shape, WIDE)

    near = rows // 128 + step
    low_block = bounds_ref[step]
    qdoc = qdoc_ref[...]
    table = table_ref[...]
    gidx = gidx_ref[...]
    sidx = sidx_ref[...]
    lse_all = lse_ref[...]
    lane = lax.broadcasted_iota(jnp.int32, (BQ, 128), 1)
    row = lax.broadcasted_iota(jnp.int32, (BQ, 128), 0)
    mask_before, mask_here = causal_masks(own, qdoc, kdoc_ref, near)
    near_at = pl.ds(pl.multiple_of((near - 1) * 128, 128), 256)
    queries, grads, queries_t, grads_t, deltas, logs, fars = [], [], [], [], [], [], []
    tgrad = jnp.zeros((BQ, 128), WIDE)
    for pair in range(pairs):
        cut = slice(pair * PAIR, (pair + 1) * PAIR)
        query = stack_heads(q_ref[:, cut]) * HD**-0.5
        grad = stack_heads(grad_ref[:, cut])
        att = att_ref[:, cut]
        delta = jnp.sum(grad * jnp.concatenate([att, att], 0), 1, keepdims=True)
        log_total = pair_columns(lse_all, pair)
        deltas.append(delta)
        logs.append(log_total)
        queries.append(query.astype(LOW))
        grads.append(grad.astype(LOW))
        queries_t.append(query.T.astype(LOW))
        grads_t.append(grad.T.astype(LOW))
        bias_before, bias_here, far = causal_parts(own, table, gidx, pair)
        fars.append(far)
        keys = window[0, near_at, cut]
        values = window[1, near_at, cut]
        found = dot_nt(queries[pair], keys)
        found_before = both_heads(mask_before, found[:, :128] + bias_before)
        found_here = both_heads(mask_here, found[:, 128:] + bias_here)
        probs = jnp.exp(jnp.concatenate([found_before, found_here], 1) - log_total)
        slopes = probs * (dot_nt(grads[pair], values) - delta)
        slopes_low = slopes.astype(LOW)
        qgrad[pair] = dot_nn(slopes_low, keys)
        wgrad[0, cut, near_at] += dot_nn(queries_t[pair], slopes_low)
        wgrad[1, cut, near_at] += dot_nn(grads_t[pair], probs.astype(LOW))
        rest = []
        for side in range(2):
            part_before = slopes[side * BQ : (side + 1) * BQ, :128]
            part_here = slopes[side * BQ : (side + 1) * BQ, 128:]
            merged = jnp.where(lane <= row, part_here, part_before)
            skewed = jnp.take_along_axis(merged, sidx, axis=1, mode="promise_in_bounds")
            tgrad = tgrad + dot_nn(skewed.astype(LOW), hot_ref[2 * pair + side])
            rest.append(jnp.where(lane <= row, part_before, 0.0))
        farsum[pair] = jnp.concatenate(rest, 0)
        if own:
            own_keys = own_ref[0, :, cut].astype(WIDE)
            own_values = own_ref[1, :, cut].astype(WIDE)
            own_keys = jnp.concatenate([own_keys, own_keys], 0)
            own_values = jnp.concatenate([own_values, own_values], 0)
            own_score = jnp.sum(query * own_keys, 1, keepdims=True) + own_column(table, pair)
            own_prob = jnp.exp(own_score - log_total)
            own_slope = own_prob * (jnp.sum(grad * own_values, 1, keepdims=True) - delta)
            qgrad[pair] += own_slope * own_keys
            key_part = own_slope * query
            value_part = own_prob * grad
            ograd_ref[0, :, cut] = (key_part[:BQ] + key_part[BQ:]).astype(LOW)
            ograd_ref[1, :, cut] = (value_part[:BQ] + value_part[BQ:]).astype(LOW)
            for side in range(2):
                place = (2 * pair + side) * BUCKETS
                tgrad = tgrad + jnp.where(lane == place, own_slope[side * BQ : (side + 1) * BQ], 0.0)

    def block_step(block, carry):
        allowed = qdoc == kdoc_ref[block]
        at = pl.ds(pl.multiple_of(block * 128, 128), 128)
        for pair in range(pairs):
            cut = slice(pair * PAIR, (pair + 1) * PAIR)
            keys = window[0, at, cut]
            values = window[1, at, cut]
            found = both_heads(allowed, dot_nt(queries[pair], keys) + fars[pair])
            probs = jnp.exp(found - logs[pair])
            slopes = probs * (dot_nt(grads[pair], values) - deltas[pair])
            farsum[pair] += slopes
            slopes = slopes.astype(LOW)
            qgrad[pair] += dot_nn(slopes, keys)
            wgrad[0, cut, at] += dot_nn(queries_t[pair], slopes)
            wgrad[1, cut, at] += dot_nn(grads_t[pair], probs.astype(LOW))
        return carry

    lax.fori_loop(low_block, near - 1, block_step, 0)
    for pair in range(pairs):
        qgrad_ref[:, pair * PAIR : (pair + 1) * PAIR] = (
            merge_heads(qgrad[pair]) * HD**-0.5
        ).astype(LOW)
        rest = jnp.sum(farsum[pair], 1, keepdims=True)
        for side in range(2):
            place = (2 * pair + side) * BUCKETS + BUCKETS - 1
            tgrad = tgrad + jnp.where(lane == place, rest[side * BQ : (side + 1) * BQ], 0.0)
    tgrad_ref[...] = tgrad.astype(LOW)

    @pl.when((stream == pl.num_programs(0) - 1) & (step == pl.num_programs(1) - 1))
    def _():
        gbefore_ref[...] = wgrad[:, :, :rows].astype(LOW)
        ghere_ref[...] = wgrad[:, :, rows:]


def whole_spec(shape):
    return pl.BlockSpec(shape, lambda stream, step, bounds: (0,) * len(shape))


def rows_spec(width):
    return pl.BlockSpec((None, BQ, width), lambda stream, step, bounds: (stream, step, 0))


def pair_rows_spec(width):
    return pl.BlockSpec((None, 2, BQ, width), lambda stream, step, bounds: (stream, 0, step, 0))


QDOC_SPEC = pl.BlockSpec((BQ, 1), lambda stream, step, bounds: (step, 0))


def shaped(shape, dtype):
    return jax.ShapeDtypeStruct(shape, dtype)


def local_call(kernel, grid, in_specs, out_specs, out_shape, scratch, cost):
    return pl.pallas_call(
        kernel,
        grid_spec=pltpu.PrefetchScalarGridSpec(
            num_scalar_prefetch=1,
            grid=grid,
            in_specs=in_specs,
            out_specs=out_specs,
            scratch_shapes=scratch,
        ),
        out_shape=out_shape,
        compiler_params=pltpu.CompilerParams(
            vmem_limit_bytes=VMEM_BYTES, dimension_semantics=("arbitrary", "arbitrary")
        ),
        cost_estimate=pl.CostEstimate(
            flops=int(cost), bytes_accessed=4 * 1024 * 1024, transcendentals=0
        ),
    )


def full_forward(with_self, bounds, queries, before, here, after, qdoc, kdoc):
    streams, rows, width = queries.shape
    pairs = width // PAIR
    blocks = 3 * rows // BK
    kv_spec = whole_spec((2, rows, width))
    return local_call(
        functools.partial(full_forward_kernel, with_self),
        (streams, rows // BQ),
        [rows_spec(width), kv_spec, kv_spec, kv_spec, QDOC_SPEC, whole_spec((blocks, 1, BK))],
        [rows_spec(width), rows_spec(width), rows_spec(128)],
        [
            shaped((streams, rows, width), LOW),
            shaped((streams, rows, width), WIDE),
            shaped((streams, rows, 128), WIDE),
        ],
        [
            pltpu.VMEM((2, 3 * rows, width), LOW),
            pltpu.VMEM((blocks, pairs, 2 * BQ, BK), WIDE),
            pltpu.VMEM((pairs, 2 * BQ, 128), WIDE),
            pltpu.VMEM((pairs, 2 * BQ, 128), WIDE),
            pltpu.VMEM((pairs, 2 * BQ, 128), WIDE),
        ],
        streams * 4e9,
    )(bounds, queries, before, here, after, qdoc, kdoc)


def full_backward(with_self, bounds, queries, grads, att, lse, before, here, after, qdoc, kdoc):
    streams, rows, width = queries.shape
    pairs = width // PAIR
    blocks = 3 * rows // BK
    kv_spec = whole_spec((2, rows, width))
    grad_spec = whole_spec((2, width, rows))
    return local_call(
        functools.partial(full_backward_kernel, with_self),
        (streams, rows // BQ),
        [rows_spec(width)] * 3
        + [rows_spec(128), kv_spec, kv_spec, kv_spec, QDOC_SPEC, whole_spec((blocks, 1, BK))],
        [rows_spec(width), grad_spec, grad_spec, grad_spec],
        [
            shaped((streams, rows, width), LOW),
            shaped((2, width, rows), LOW),
            shaped((2, width, rows), WIDE),
            shaped((2, width, rows), LOW),
        ],
        [
            pltpu.VMEM((2, 3 * rows, width), LOW),
            pltpu.VMEM((2, width, 3 * rows), WIDE),
            pltpu.VMEM((pairs, 2 * BQ, 128), WIDE),
        ],
        streams * 8e9,
    )(bounds, queries, grads, att, lse, before, here, after, qdoc, kdoc)


def spread_index():
    row, lane = np.arange(BQ)[:, None], np.arange(128)[None, :]
    return bucket_table((row - lane) % 128).astype(np.int32)


def skew_index():
    row, lane = np.arange(BQ)[:, None], np.arange(128)[None, :]
    return ((row - lane) % 128).astype(np.int32)


def bucket_hot(heads):
    offsets = np.arange(128)
    hot = np.zeros((heads, 128, 128), np.float32)
    for head in range(heads):
        hot[head, offsets, head * BUCKETS + bucket_table(offsets)] = 1.0
    return hot


def causal_forward(own, bounds, queries, before, here, qdoc, kdoc, tables, own_pair):
    streams, rows, width = queries.shape
    pairs = width // PAIR
    blocks = 2 * rows // 128
    kv_spec = whole_spec((2, rows, width))
    specs = [rows_spec(width), kv_spec, kv_spec, QDOC_SPEC, whole_spec((blocks, 1, 128))]
    specs += [rows_spec(128), whole_spec((BQ, 128))]
    operands = [bounds, queries, before, here, qdoc, kdoc, tables, jnp.asarray(spread_index())]
    if own:
        specs.append(pair_rows_spec(width))
        operands.append(own_pair)
    return local_call(
        functools.partial(causal_forward_kernel, own),
        (streams, rows // BQ),
        specs,
        [rows_spec(width), rows_spec(width), rows_spec(128)],
        [
            shaped((streams, rows, width), LOW),
            shaped((streams, rows, width), WIDE),
            shaped((streams, rows, 128), WIDE),
        ],
        [
            pltpu.VMEM((2, 2 * rows, width), LOW),
            pltpu.VMEM((blocks, pairs, 2 * BQ, 128), WIDE),
            pltpu.VMEM((pairs, 2 * BQ, 128), WIDE),
            pltpu.VMEM((pairs, 2 * BQ, 128), WIDE),
            pltpu.VMEM((pairs, 2 * BQ, 128), WIDE),
        ],
        streams * 4e9,
    )(*operands)


def causal_backward(
    own, bounds, queries, grads, att, lse, before, here, qdoc, kdoc, tables, own_pair
):
    streams, rows, width = queries.shape
    pairs = width // PAIR
    blocks = 2 * rows // 128
    kv_spec = whole_spec((2, rows, width))
    grad_spec = whole_spec((2, width, rows))
    specs = [rows_spec(width)] * 3 + [rows_spec(128), kv_spec, kv_spec, QDOC_SPEC]
    specs += [whole_spec((blocks, 1, 128)), rows_spec(128), whole_spec((BQ, 128))]
    specs += [whole_spec((BQ, 128)), whole_spec((2 * pairs, 128, 128))]
    operands = [bounds, queries, grads, att, lse, before, here, qdoc, kdoc, tables]
    operands += [jnp.asarray(spread_index()), jnp.asarray(skew_index())]
    operands += [jnp.asarray(bucket_hot(2 * pairs), LOW)]
    out_specs = [rows_spec(width), rows_spec(128), grad_spec, grad_spec]
    out_shape = [
        shaped((streams, rows, width), LOW),
        shaped((streams, rows, 128), LOW),
        shaped((2, width, rows), LOW),
        shaped((2, width, rows), WIDE),
    ]
    if own:
        specs.append(pair_rows_spec(width))
        operands.append(own_pair)
        out_specs.append(pair_rows_spec(width))
        out_shape.append(shaped((streams, 2, rows, width), LOW))
    return local_call(
        functools.partial(causal_backward_kernel, own),
        (streams, rows // BQ),
        specs,
        out_specs,
        out_shape,
        [
            pltpu.VMEM((2, 2 * rows, width), LOW),
            pltpu.VMEM((2, width, 2 * rows), WIDE),
            pltpu.VMEM((pairs, 2 * BQ, 128), WIDE),
            pltpu.VMEM((pairs, 2 * BQ, 128), WIDE),
        ],
        streams * 8e9,
    )(*operands)


def swap_core(value):
    count = lax.axis_size("tp")
    return lax.ppermute(value, "tp", [(place, place ^ 1) for place in range(count)])


def sum_chips(value):
    count = lax.axis_size("tp")
    hop = 2
    while hop < count:
        low = value.astype(LOW)
        value = low.astype(WIDE) + lax.ppermute(
            low, "tp", [(place, place ^ hop) for place in range(count)]
        ).astype(WIDE)
        hop *= 2
    return value


def core_index():
    return lax.rem(lax.axis_index("tp"), 2)


def half_rows(rows, mine):
    half = rows.shape[1] // 2
    core = core_index() if mine else 1 - core_index()
    return lax.dynamic_slice_in_dim(rows, core * half, half, 1)


def natural_rows(mine, other):
    first = core_index() == 0
    return jnp.concatenate([jnp.where(first, mine, other), jnp.where(first, other, mine)], 1)


def project(rows, weight):
    return jnp.einsum("gsd,df->gsf", rows, weight, preferred_element_type=WIDE)


def back_project(grads, weight):
    return jnp.einsum("gsf,df->gsd", grads, weight, preferred_element_type=WIDE)


def weight_grad(rows, grads):
    return jnp.einsum("gsd,gsf->df", rows, grads, preferred_element_type=WIDE)


def summed_rows(mine, other):
    return sum_chips(mine + swap_core(other.astype(LOW)).astype(WIDE))


def norm_forward(resid, gain, shift):
    mean = jnp.mean(resid, -1, keepdims=True)
    centred = resid - mean
    inverse = lax.rsqrt(jnp.mean(centred * centred, -1, keepdims=True) + 1e-05)
    normed = centred * inverse
    return (normed * gain + shift, normed, inverse)


def close_branch(resid, mine, other, gain, shift):
    output, normed, inverse = norm_forward(resid + summed_rows(mine, other), gain, shift)
    low = output.astype(LOW)
    return (output, low, swap_core(low), (normed, inverse))


def open_branch(grad_out, saved, gain):
    normed, inverse = saved
    grad_normed = grad_out * gain
    grad_resid = inverse * (
        grad_normed
        - jnp.mean(grad_normed, -1, keepdims=True)
        - normed * jnp.mean(grad_normed * normed, -1, keepdims=True)
    )
    low = grad_resid.astype(LOW)
    sums = jnp.stack([jnp.sum(grad_out * normed, (0, 1)), jnp.sum(grad_out, (0, 1))])
    return (grad_resid, low, swap_core(low), sums)


def gelu_both(hidden):
    scaled = hidden * (0.5**0.5)
    half = 0.5 * lax.erf(scaled) + 0.5
    slope = half + hidden * jnp.exp(-(scaled * scaled)) * ((2.0 * math.pi) ** -0.5)
    return ((hidden * half).astype(LOW), slope.astype(LOW))


def passed_along(value, steps):
    count = lax.axis_size("seq")
    if steps > 0:
        pairs = [(place, place + 1) for place in range(count - 1)]
    else:
        pairs = [(place + 1, place) for place in range(count - 1)]
    return lax.ppermute(value, "seq", pairs)


def doc_index(positions, ends):
    return jnp.sum((positions[:, None] >= ends[None, :]).astype(jnp.int32), 1)


def pick(owner, values):
    match = owner[:, None] == jnp.arange(values.shape[0], dtype=jnp.int32)[None, :]
    return jnp.sum(jnp.where(match, values[None, :], 0), 1)


def sum_seq(values, earlier):
    low = tuple(value.astype(LOW) for value in values)
    if earlier is not None:
        low, earlier = lax.optimization_barrier((low, earlier))
    return lax.psum(low, "seq")


def pad_tables(tables):
    missing = 128 - tables.shape[-1]
    return jnp.pad(tables, ((0, 0), (0, 0), (0, missing))) if missing else tables


def per_device(
    enc_input,
    dec_input,
    enc_cotan,
    dec_cotan,
    doc_lengths,
    src_padding,
    enc_qkv,
    enc_wout,
    enc_gain,
    enc_bias,
    enc_up,
    enc_down,
    post_gain,
    post_bias,
    self_qkv,
    self_rel,
    self_wout,
    self_gain,
    self_bias,
    cross_wq,
    cross_wkv,
    cross_wout,
    cross_gain,
    cross_bias,
    ffn_up,
    ffn_down,
    ffn_gain,
    ffn_bias,
):
    rows = enc_input.shape[0]
    half = rows // 2
    streams = dec_input.shape[0]
    table_width = self_rel.shape[1]
    base = lax.axis_index("seq") * rows
    total_rows = rows * lax.axis_size("seq")
    ends = jnp.cumsum(doc_lengths)
    starts = ends - doc_lengths
    key_pos = base - rows + jnp.arange(3 * rows, dtype=jnp.int32)
    key_valid = (key_pos >= 0) & (key_pos < total_rows)
    key_owner = doc_index(key_pos, ends)
    key_doc = jnp.where(key_valid, key_owner, -1)
    key_pad = (
        lax.dynamic_slice_in_dim(jnp.pad(src_padding, (rows, rows)), base, 3 * rows) == 1
    )
    key_first = key_pos == pick(key_owner, starts)
    qdoc = key_doc[rows : 2 * rows][:, None]
    enc_kdoc = jnp.where(key_pad, key_doc, -1).reshape(-1, 1, BK)
    cross_kdoc = jnp.where(key_pad | key_first, key_doc, -1).reshape(-1, 1, BK)
    self_kdoc = key_doc[: 2 * rows].reshape(-1, 1, 128)
    owners = key_owner[rows : 2 * rows]
    block_first = pick(owners[::BQ], starts) - base + rows
    block_end = pick(owners[BQ - 1 :: BQ], ends) - base + rows
    full_bounds = jnp.stack([block_first // BK, (block_end + BK - 1) // BK])
    self_bounds = block_first // 128

    enc_rows = enc_input[None]
    enc_proj = jnp.einsum("sd,cdf->csf", enc_input, enc_qkv, preferred_element_type=WIDE).astype(LOW)
    enc_pair = enc_proj[1:]
    enc_query = enc_proj[:1]
    enc_before = passed_along(enc_pair, 1)
    enc_after = passed_along(enc_pair, -1)
    dec_proj = [
        jnp.einsum("sd,cdf->csf", dec_input[stream], self_qkv, preferred_element_type=WIDE).astype(LOW)
        for stream in range(streams)
    ]
    main_pair = dec_proj[0][1:]
    main_before = passed_along(main_pair, 1)
    tables = pad_tables(project(dec_input, self_rel))

    enc_att, enc_wide, enc_lse = full_forward(
        True, full_bounds, enc_query, enc_before, enc_pair, enc_after, qdoc, enc_kdoc
    )
    enc_resid, enc_mine, enc_other, enc_saved_attn = close_branch(
        half_rows(enc_rows, True).astype(WIDE),
        project(half_rows(enc_att, True), enc_wout),
        project(half_rows(enc_att, False), enc_wout),
        enc_gain,
        enc_bias,
    )
    enc_middle = jnp.concatenate([enc_mine, enc_other], 1)
    enc_act, enc_slope = gelu_both(project(enc_middle, enc_up))

    self_att, self_wide, self_lse = [], [], []
    for stream in range(streams):
        own = stream > 0
        att, wide, lse = causal_forward(
            own,
            self_bounds,
            dec_proj[stream][:1],
            main_before,
            main_pair,
            qdoc,
            self_kdoc,
            tables[stream : stream + 1],
            dec_proj[stream][1:][None] if own else None,
        )
        self_att.append(att)
        self_wide.append(wide)
        self_lse.append(lse)

    enc_resid, enc_mine, enc_other, enc_saved_ffn = close_branch(
        enc_resid,
        project(enc_act[:, :half], enc_down),
        project(enc_act[:, half:], enc_down),
        post_gain,
        post_bias,
    )
    enc_final = natural_rows(enc_mine, enc_other)
    cross_pair = jnp.einsum(
        "sd,cdf->csf", enc_final[0], cross_wkv, preferred_element_type=WIDE
    ).astype(LOW)
    cross_before = passed_along(cross_pair, 1)
    cross_after = passed_along(cross_pair, -1)

    groups = [(stream, stream + 1) for stream in range(streams)]
    first_saved, first_rows, first_resid = [], [], []
    for stream in range(streams):
        resid, mine, other, saved = close_branch(
            half_rows(dec_input[stream][None], True).astype(WIDE),
            project(half_rows(self_att[stream], True), self_wout),
            project(half_rows(self_att[stream], False), self_wout),
            self_gain,
            self_bias,
        )
        first_resid.append(resid)
        first_saved.append(saved)
        first_rows.append((mine, other))
    cross_query, cross_att, cross_wide, cross_lse = [], [], [], []
    for stream in range(streams):
        mine, other = first_rows[stream]
        query = natural_rows(
            project(mine, cross_wq).astype(LOW), project(other, cross_wq).astype(LOW)
        )
        att, wide, lse = full_forward(
            False, full_bounds, query, cross_before, cross_pair, cross_after, qdoc, cross_kdoc
        )
        cross_query.append(query)
        cross_att.append(att)
        cross_wide.append(wide)
        cross_lse.append(lse)
    second_saved, second_rows, second_resid = [], [], []
    for stream in range(streams):
        resid, mine, other, saved = close_branch(
            first_resid[stream],
            project(half_rows(cross_att[stream], True), cross_wout),
            project(half_rows(cross_att[stream], False), cross_wout),
            cross_gain,
            cross_bias,
        )
        second_resid.append(resid)
        second_saved.append(saved)
        second_rows.append(jnp.concatenate([mine, other], 1))
    dec_act, dec_slope = [], []
    dec_final, grad, ffn_grad_rows, ffn_sums = [], [], [], []
    for stream in range(streams):
        act, slope = gelu_both(project(second_rows[stream], ffn_up))
        dec_act.append(act)
        dec_slope.append(slope)
        resid, mine, other, saved = close_branch(
            second_resid[stream],
            project(act[:, :half], ffn_down),
            project(act[:, half:], ffn_down),
            ffn_gain,
            ffn_bias,
        )
        dec_final.append(natural_rows(mine, other))
        grad_out = half_rows(dec_cotan[stream][None], True).astype(WIDE)
        resid_grad, mine, other, sums = open_branch(grad_out, saved, ffn_gain)
        grad.append(resid_grad)
        ffn_grad_rows.append(jnp.concatenate([mine, other], 1))
        ffn_sums.append(sums)
    dec_final = jnp.concatenate(dec_final, 0)

    cross_sums, cross_grad_rows, hidden_grads = [], [], []
    for stream in range(streams):
        grad_act = jnp.einsum(
            "gsd,fd->gsf", ffn_grad_rows[stream], ffn_down, preferred_element_type=WIDE
        )
        hidden_grad = (grad_act * dec_slope[stream].astype(WIDE)).astype(LOW)
        hidden_grads.append(hidden_grad)
        grad[stream] = grad[stream] + summed_rows(
            back_project(hidden_grad[:, :half], ffn_up), back_project(hidden_grad[:, half:], ffn_up)
        )
        resid_grad, mine, other, sums = open_branch(grad[stream], second_saved[stream], cross_gain)
        grad[stream] = resid_grad
        cross_grad_rows.append((mine, other))
        cross_sums.append(sums)
    ffn_down_grad = weight_grad(jnp.concatenate(dec_act), jnp.concatenate(ffn_grad_rows))
    ffn_up_grad = weight_grad(jnp.concatenate(second_rows), jnp.concatenate(hidden_grads))
    ffn_sum = sum_seq([ffn_down_grad, ffn_up_grad], None)

    def att_grad(mine, other, weight):
        return natural_rows(
            jnp.einsum("gsd,fd->gsf", mine, weight, preferred_element_type=WIDE).astype(LOW),
            jnp.einsum("gsd,fd->gsf", other, weight, preferred_element_type=WIDE).astype(LOW),
        )

    def att_weight_grad(atts, grads):
        lefts, rights = [], []
        for att, (mine, other) in zip(atts, grads):
            lefts += [half_rows(att, True), half_rows(att, False)]
            rights += [mine, other]
        return weight_grad(jnp.concatenate(lefts, 1), jnp.concatenate(rights, 1))

    cross_query_grads, cross_parts = [], []
    for stream in range(streams):
        cross_att_grad = att_grad(*cross_grad_rows[stream], cross_wout)
        query_grad, *parts = full_backward(
            False,
            full_bounds,
            cross_query[stream],
            cross_att_grad,
            cross_wide[stream],
            cross_lse[stream],
            cross_before,
            cross_pair,
            cross_after,
            qdoc,
            cross_kdoc,
        )
        cross_query_grads.append(query_grad)
        cross_parts.append(parts)

    def fold_pair(parts, after):
        to_before = sum(part[0].astype(WIDE) for part in parts).astype(LOW)
        here = sum(part[1] for part in parts) + passed_along(to_before, -1).astype(WIDE)
        if after:
            to_after = sum(part[2].astype(WIDE) for part in parts).astype(LOW)
            here = here + passed_along(to_after, 1).astype(WIDE)
        return here.astype(LOW)

    cross_pair_grad = fold_pair(cross_parts, True)
    enc_extra = jnp.einsum("cfs,cdf->sd", cross_pair_grad, cross_wkv, preferred_element_type=WIDE)[None]
    enc_grad = half_rows(enc_cotan[None], True).astype(WIDE) + summed_rows(
        half_rows(enc_extra, True), half_rows(enc_extra, False)
    )
    enc_grad, mine, other, post_sums = open_branch(enc_grad, enc_saved_ffn, post_gain)
    enc_ffn_rows = jnp.concatenate([mine, other], 1)

    self_sums, self_grad_rows = [], []
    for stream in range(streams):
        query_grad = cross_query_grads[stream]
        grad[stream] = grad[stream] + summed_rows(
            back_project(half_rows(query_grad, True), cross_wq),
            back_project(half_rows(query_grad, False), cross_wq),
        )
        resid_grad, mine, other, sums = open_branch(grad[stream], first_saved[stream], self_gain)
        grad[stream] = resid_grad
        self_grad_rows.append((mine, other))
        self_sums.append(sums)
    cross_wout_grad = att_weight_grad(cross_att, cross_grad_rows)
    cross_wq_grad = att_weight_grad(cross_query_grads, first_rows).T
    cross_wkv_grad = jnp.einsum("sd,cfs->cdf", enc_final[0], cross_pair_grad, preferred_element_type=WIDE)
    cross_sum = sum_seq([cross_wout_grad, cross_wq_grad, cross_wkv_grad], ffn_sum)

    grad_act = jnp.einsum("gsd,fd->gsf", enc_ffn_rows, enc_down, preferred_element_type=WIDE)
    hidden_grad = (grad_act * enc_slope.astype(WIDE)).astype(LOW)
    enc_grad = enc_grad + summed_rows(
        back_project(hidden_grad[:, :half], enc_up), back_project(hidden_grad[:, half:], enc_up)
    )
    enc_sum = sum_seq(
        [weight_grad(enc_act, enc_ffn_rows), weight_grad(enc_middle, hidden_grad)], cross_sum
    )
    enc_grad, mine, other, enc_sums = open_branch(enc_grad, enc_saved_attn, enc_gain)
    enc_grad_rows = (mine, other)

    self_proj_grads, self_parts, table_grads = [], [], []
    for stream in range(streams):
        own = stream > 0
        self_att_grad = att_grad(*self_grad_rows[stream], self_wout)
        query_grad, table_grad, *parts = causal_backward(
            own,
            self_bounds,
            dec_proj[stream][:1],
            self_att_grad,
            self_wide[stream],
            self_lse[stream],
            main_before,
            main_pair,
            qdoc,
            self_kdoc,
            tables[stream : stream + 1],
            dec_proj[stream][1:][None] if own else None,
        )
        self_parts.append(parts[:2])
        table_grads.append(table_grad[:, :, :table_width])
        own_grad = parts[2][0] if own else None
        self_proj_grads.append([query_grad, own_grad])
    main_grad = fold_pair(self_parts, False)
    main_grad = jnp.swapaxes(main_grad, 1, 2)
    dec_grad = []
    full_proj_grads = []
    for stream in range(streams):
        query_grad, own_grad = self_proj_grads[stream]
        pair_grad = main_grad if stream == 0 else own_grad
        proj_grad = jnp.concatenate([query_grad, pair_grad], 0)
        full_proj_grads.append(proj_grad)
        partial_value = (
            jnp.einsum("csf,cdf->sd", proj_grad, self_qkv, preferred_element_type=WIDE)[None]
            + back_project(table_grads[stream], self_rel)
        )
        total = grad[stream] + summed_rows(
            half_rows(partial_value, True), half_rows(partial_value, False)
        )
        low = total.astype(LOW)
        dec_grad.append(natural_rows(low, swap_core(low)))
    dec_grad = jnp.concatenate(dec_grad, 0)
    self_qkv_grad = jnp.einsum(
        "gsd,gcsf->cdf", dec_input, jnp.stack(full_proj_grads), preferred_element_type=WIDE
    )
    self_rel_grad = weight_grad(dec_input, jnp.concatenate(table_grads, 0))
    self_wout_grad = att_weight_grad(self_att, self_grad_rows)

    enc_att_grad = att_grad(*enc_grad_rows, enc_wout)
    query_grad, *parts = full_backward(
        True,
        full_bounds,
        enc_query,
        enc_att_grad,
        enc_wide,
        enc_lse,
        enc_before,
        enc_pair,
        enc_after,
        qdoc,
        enc_kdoc,
    )
    pair_grad = jnp.swapaxes(fold_pair([parts], True), 1, 2)
    enc_proj_grad = jnp.concatenate([query_grad, pair_grad], 0)
    enc_qkv_grad = jnp.einsum("sd,csf->cdf", enc_input, enc_proj_grad, preferred_element_type=WIDE)
    partial_value = jnp.einsum(
        "csf,cdf->sd", enc_proj_grad, enc_qkv, preferred_element_type=WIDE
    )[None]
    enc_grad = enc_grad + summed_rows(
        half_rows(partial_value, True), half_rows(partial_value, False)
    )
    low = enc_grad.astype(LOW)
    enc_grad = natural_rows(low, swap_core(low))[0]
    enc_wout_grad = att_weight_grad([enc_att], [enc_grad_rows])

    sums = jnp.concatenate(
        [enc_sums, post_sums, sum(self_sums), sum(cross_sums), sum(ffn_sums)], 0
    )
    sums = sums + swap_core(sums)
    last_sum = sum_seq(
        [self_qkv_grad, self_rel_grad, self_wout_grad, enc_qkv_grad, enc_wout_grad, sums], enc_sum
    )
    ffn_down_grad, ffn_up_grad = [value.astype(WIDE) for value in ffn_sum]
    cross_wout_grad, cross_wq_grad, cross_wkv_grad = [value.astype(WIDE) for value in cross_sum]
    enc_down_grad, enc_up_grad = [value.astype(WIDE) for value in enc_sum]
    self_qkv_grad, self_rel_grad, self_wout_grad, enc_qkv_grad, enc_wout_grad, sums = [
        value.astype(WIDE) for value in last_sum
    ]
    return (
        enc_final[0],
        dec_final,
        enc_grad,
        dec_grad,
        enc_qkv_grad,
        enc_wout_grad,
        sums[0],
        sums[1],
        enc_up_grad,
        enc_down_grad,
        sums[2],
        sums[3],
        self_qkv_grad,
        self_rel_grad,
        self_wout_grad,
        sums[4],
        sums[5],
        cross_wq_grad,
        cross_wkv_grad,
        cross_wout_grad,
        sums[6],
        sums[7],
        ffn_up_grad,
        ffn_down_grad,
        sums[8],
        sums[9],
    )


def solution(mesh):
    in_specs = (
        P("seq", None),
        P(None, "seq", None),
        P("seq", None),
        P(None, "seq", None),
        P(),
        P(),
        P(None, None, "tp"),
        P("tp", None),
        P(),
        P(),
        P(None, "tp"),
        P("tp", None),
        P(),
        P(),
        P(None, None, "tp"),
        P(None, "tp"),
        P("tp", None),
        P(),
        P(),
        P(None, "tp"),
        P(None, None, "tp"),
        P("tp", None),
        P(),
        P(),
        P(None, "tp"),
        P("tp", None),
        P(),
        P(),
    )
    out_specs = (
        P("seq", None),
        P(None, "seq", None),
        P("seq", None),
        P(None, "seq", None),
        P(None, None, "tp"),
        P("tp", None),
        P(),
        P(),
        P(None, "tp"),
        P("tp", None),
        P(),
        P(),
        P(None, None, "tp"),
        P(None, "tp"),
        P("tp", None),
        P(),
        P(),
        P(None, "tp"),
        P(None, None, "tp"),
        P("tp", None),
        P(),
        P(),
        P(None, "tp"),
        P("tp", None),
        P(),
        P(),
    )
    return jax.shard_map(
        per_device, mesh=mesh, in_specs=in_specs, out_specs=out_specs, check_vma=False
    )
```

```python
import functools
import math

import jax
import jax.numpy as jnp
import numpy as np
from jax import lax
from jax.experimental import pallas as pl
from jax.experimental.pallas import tpu as pltpu
from jax.sharding import PartitionSpec as P

HD = 64
BUCKETS = 32
DOC_MAX = 512
PAIR = 2 * HD
BQ = 128
BK = 256
NEG = -1e30
VMEM_BYTES = 40 * 1024 * 1024

LOW = jnp.bfloat16
WIDE = jnp.float32


def bucket_bounds():
    exact = BUCKETS // 2
    bounds = []
    for level in range(1, BUCKETS):
        if level < exact:
            bounds.append(level)
        else:
            bounds.append(int(math.ceil(exact * (128.0 / exact) ** ((level - exact) / exact))))
    return bounds


def bucket_table(offsets):
    return sum((offsets >= bound).astype(np.int32) for bound in bucket_bounds())


def dot_nt(left, right):
    return lax.dot_general(left, right, (((1,), (1,)), ((), ())), preferred_element_type=WIDE)


def dot_nn(left, right):
    return lax.dot_general(left, right, (((1,), (0,)), ((), ())), preferred_element_type=WIDE)


def stack_heads(cells):
    lane = lax.broadcasted_iota(jnp.int32, cells.shape, 1)
    wide = cells.astype(WIDE)
    first = jnp.where(lane < HD, wide, 0.0)
    return jnp.concatenate([first, wide - first], 0)


def merge_heads(cells):
    half = cells.shape[0] // 2
    lane = lax.broadcasted_iota(jnp.int32, (half, cells.shape[1]), 1)
    return jnp.where(lane < HD, cells[:half], cells[half:])


def both_heads(mask, cells):
    return jnp.where(mask[None], cells.reshape(2, BQ, cells.shape[1]), NEG).reshape(cells.shape)


def pair_columns(cells, pair):
    return jnp.concatenate([cells[:, 2 * pair : 2 * pair + 1], cells[:, 2 * pair + 1 : 2 * pair + 2]], 0)


def put_columns(store, pair, column):
    lane = lax.broadcasted_iota(jnp.int32, store.shape, 1)
    store = jnp.where(lane == 2 * pair, column[:BQ], store)
    return jnp.where(lane == 2 * pair + 1, column[BQ:], store)


def fill_window(window, parts):
    rows = parts[0].shape[1]
    for place, part in enumerate(parts):
        window[:, place * rows : (place + 1) * rows, :] = part[...]


def full_mask(with_self, qdoc, kdoc_ref, block, query_at):
    allowed = qdoc == kdoc_ref[block]
    if with_self:
        row = lax.broadcasted_iota(jnp.int32, allowed.shape, 0) + query_at
        column = lax.broadcasted_iota(jnp.int32, allowed.shape, 1) + block * BK
        allowed = allowed | (row == column)
    return allowed


def full_forward_kernel(
    with_self,
    bounds_ref,
    q_ref,
    before_ref,
    here_ref,
    after_ref,
    qdoc_ref,
    kdoc_ref,
    att_ref,
    wide_ref,
    lse_ref,
    window,
    scores,
    top,
    total,
    gathered,
):
    stream, step = pl.program_id(0), pl.program_id(1)
    rows = here_ref.shape[1]
    pairs = here_ref.shape[2] // PAIR

    @pl.when((stream == 0) & (step == 0))
    def _():
        fill_window(window, (before_ref, here_ref, after_ref))

    low_block, high_block = bounds_ref[0, step], bounds_ref[1, step]
    qdoc = qdoc_ref[...]
    queries = [
        (stack_heads(q_ref[:, pair * PAIR : (pair + 1) * PAIR]) * HD**-0.5).astype(LOW)
        for pair in range(pairs)
    ]
    top[...] = jnp.full(top.shape, NEG, WIDE)
    total[...] = jnp.zeros(total.shape, WIDE)
    gathered[...] = jnp.zeros(gathered.shape, WIDE)

    def score_step(block, carry):
        allowed = full_mask(with_self, qdoc, kdoc_ref, block, rows + step * BQ)
        at = pl.ds(pl.multiple_of(block * BK, BK), BK)
        for pair in range(pairs):
            keys = window[0, at, pair * PAIR : (pair + 1) * PAIR]
            found = both_heads(allowed, dot_nt(queries[pair], keys))
            scores[block, pair] = found
            top[pair] = jnp.maximum(top[pair], jnp.maximum(found[:, :128], found[:, 128:]))
        return carry

    lax.fori_loop(low_block, high_block, score_step, 0)
    peaks = [jnp.max(top[pair], 1, keepdims=True) for pair in range(pairs)]

    def value_step(block, carry):
        at = pl.ds(pl.multiple_of(block * BK, BK), BK)
        for pair in range(pairs):
            values = window[1, at, pair * PAIR : (pair + 1) * PAIR]
            weights = jnp.exp(scores[block, pair] - peaks[pair])
            total[pair] += weights[:, :128] + weights[:, 128:]
            gathered[pair] += dot_nn(weights.astype(LOW), values)
        return carry

    lax.fori_loop(low_block, high_block, value_step, 0)
    lse = jnp.zeros((BQ, 128), WIDE)
    for pair in range(pairs):
        weight = jnp.sum(total[pair], 1, keepdims=True)
        result = merge_heads(gathered[pair] / weight)
        att_ref[:, pair * PAIR : (pair + 1) * PAIR] = result.astype(LOW)
        wide_ref[:, pair * PAIR : (pair + 1) * PAIR] = result
        lse = put_columns(lse, pair, peaks[pair] + jnp.log(weight))
    lse_ref[...] = lse


def full_backward_kernel(
    with_self,
    bounds_ref,
    q_ref,
    grad_ref,
    att_ref,
    lse_ref,
    before_ref,
    here_ref,
    after_ref,
    qdoc_ref,
    kdoc_ref,
    qgrad_ref,
    gbefore_ref,
    ghere_ref,
    gafter_ref,
    window,
    wgrad,
    qgrad,
):
    stream, step = pl.program_id(0), pl.program_id(1)
    rows = here_ref.shape[1]
    pairs = here_ref.shape[2] // PAIR

    @pl.when((stream == 0) & (step == 0))
    def _():
        fill_window(window, (before_ref, here_ref, after_ref))
        wgrad[...] = jnp.zeros(wgrad.shape, WIDE)

    low_block, high_block = bounds_ref[0, step], bounds_ref[1, step]
    qdoc = qdoc_ref[...]
    lse_all = lse_ref[...]
    queries, grads, queries_t, grads_t, deltas, logs = [], [], [], [], [], []
    for pair in range(pairs):
        cut = slice(pair * PAIR, (pair + 1) * PAIR)
        query = stack_heads(q_ref[:, cut]) * HD**-0.5
        grad = stack_heads(grad_ref[:, cut])
        att = att_ref[:, cut]
        deltas.append(jnp.sum(grad * jnp.concatenate([att, att], 0), 1, keepdims=True))
        logs.append(pair_columns(lse_all, pair))
        queries.append(query.astype(LOW))
        grads.append(grad.astype(LOW))
        queries_t.append(query.T.astype(LOW))
        grads_t.append(grad.T.astype(LOW))
    qgrad[...] = jnp.zeros(qgrad.shape, WIDE)

    def block_step(block, carry):
        allowed = full_mask(with_self, qdoc, kdoc_ref, block, rows + step * BQ)
        at = pl.ds(pl.multiple_of(block * BK, BK), BK)
        for pair in range(pairs):
            cut = slice(pair * PAIR, (pair + 1) * PAIR)
            keys = window[0, at, cut]
            values = window[1, at, cut]
            probs = jnp.exp(both_heads(allowed, dot_nt(queries[pair], keys)) - logs[pair])
            slopes = probs * (dot_nt(grads[pair], values) - deltas[pair])
            slopes = slopes.astype(LOW)
            qgrad[pair] += dot_nn(slopes, keys)
            wgrad[0, cut, at] += dot_nn(queries_t[pair], slopes)
            wgrad[1, cut, at] += dot_nn(grads_t[pair], probs.astype(LOW))
        return carry

    lax.fori_loop(low_block, high_block, block_step, 0)
    for pair in range(pairs):
        qgrad_ref[:, pair * PAIR : (pair + 1) * PAIR] = (
            merge_heads(qgrad[pair]) * HD**-0.5
        ).astype(LOW)

    @pl.when((stream == pl.num_programs(0) - 1) & (step == pl.num_programs(1) - 1))
    def _():
        for side in range(2):
            gbefore_ref[side] = wgrad[side, :, :rows].T.astype(LOW)
            ghere_ref[side] = wgrad[side, :, rows : 2 * rows].T
            gafter_ref[side] = wgrad[side, :, 2 * rows :].T.astype(LOW)


def causal_parts(own, table, gidx, pair):
    lane = lax.broadcasted_iota(jnp.int32, (BQ, 128), 1)
    row = lax.broadcasted_iota(jnp.int32, (BQ, 128), 0)
    near, far = [], []
    for head in (2 * pair, 2 * pair + 1):
        spread = jnp.take_along_axis(
            table, gidx + head * BUCKETS, axis=1, mode="promise_in_bounds"
        )
        last = table[:, head * BUCKETS + BUCKETS - 1 : head * BUCKETS + BUCKETS]
        near.append((jnp.where(lane > row, spread, last), spread))
        far.append(last)
    bias_before = jnp.concatenate([near[0][0], near[1][0]], 0)
    bias_here = jnp.concatenate([near[0][1], near[1][1]], 0)
    return bias_before, bias_here, jnp.concatenate(far, 0)


def own_column(table, pair):
    first, second = 2 * pair * BUCKETS, (2 * pair + 1) * BUCKETS
    return jnp.concatenate([table[:, first : first + 1], table[:, second : second + 1]], 0)


def causal_masks(own, qdoc, kdoc_ref, near):
    lane = lax.broadcasted_iota(jnp.int32, (BQ, 128), 1)
    row = lax.broadcasted_iota(jnp.int32, (BQ, 128), 0)
    earlier = (lane < row) if own else (lane <= row)
    return qdoc == kdoc_ref[near - 1], (qdoc == kdoc_ref[near]) & earlier


def causal_forward_kernel(own, *refs):
    bounds_ref, q_ref, before_ref, here_ref, qdoc_ref, kdoc_ref, table_ref, gidx_ref = refs[:8]
    refs = refs[8:]
    if own:
        own_ref, refs = refs[0], refs[1:]
    att_ref, wide_ref, lse_ref, window, scores, top, total, gathered = refs
    stream, step = pl.program_id(0), pl.program_id(1)
    rows = here_ref.shape[1]
    pairs = here_ref.shape[2] // PAIR

    @pl.when((stream == 0) & (step == 0))
    def _():
        fill_window(window, (before_ref, here_ref))

    near = rows // 128 + step
    low_block = bounds_ref[step]
    qdoc = qdoc_ref[...]
    table = table_ref[...]
    gidx = gidx_ref[...]
    queries, fars, peaks, owns = [], [], [], []
    mask_before, mask_here = causal_masks(own, qdoc, kdoc_ref, near)
    near_at = pl.ds(pl.multiple_of((near - 1) * 128, 128), 256)
    for pair in range(pairs):
        cut = slice(pair * PAIR, (pair + 1) * PAIR)
        query = stack_heads(q_ref[:, cut]) * HD**-0.5
        queries.append(query.astype(LOW))
        bias_before, bias_here, far = causal_parts(own, table, gidx, pair)
        fars.append(far)
        found = dot_nt(queries[pair], window[0, near_at, cut])
        found_before = both_heads(mask_before, found[:, :128] + bias_before)
        found_here = both_heads(mask_here, found[:, 128:] + bias_here)
        scores[near - 1, pair] = found_before
        scores[near, pair] = found_here
        top[pair] = jnp.maximum(found_before, found_here)
        if own:
            keys = own_ref[0, :, cut].astype(WIDE)
            owns.append(
                jnp.sum(query * jnp.concatenate([keys, keys], 0), 1, keepdims=True)
                + own_column(table, pair)
            )

    def score_step(block, carry):
        allowed = qdoc == kdoc_ref[block]
        at = pl.ds(pl.multiple_of(block * 128, 128), 128)
        for pair in range(pairs):
            keys = window[0, at, pair * PAIR : (pair + 1) * PAIR]
            found = both_heads(allowed, dot_nt(queries[pair], keys) + fars[pair])
            scores[block, pair] = found
            top[pair] = jnp.maximum(top[pair], found)
        return carry

    lax.fori_loop(low_block, near - 1, score_step, 0)
    for pair in range(pairs):
        cut = slice(pair * PAIR, (pair + 1) * PAIR)
        peak = jnp.max(top[pair], 1, keepdims=True)
        if own:
            peak = jnp.maximum(peak, owns[pair])
        peaks.append(peak)
        weights_before = jnp.exp(scores[near - 1, pair] - peak)
        weights_here = jnp.exp(scores[near, pair] - peak)
        total[pair] = weights_before + weights_here
        weights = jnp.concatenate([weights_before, weights_here], 1).astype(LOW)
        gathered[pair] = dot_nn(weights, window[1, near_at, cut])

    def value_step(block, carry):
        at = pl.ds(pl.multiple_of(block * 128, 128), 128)
        for pair in range(pairs):
            values = window[1, at, pair * PAIR : (pair + 1) * PAIR]
            weights = jnp.exp(scores[block, pair] - peaks[pair])
            total[pair] += weights
            gathered[pair] += dot_nn(weights.astype(LOW), values)
        return carry

    lax.fori_loop(low_block, near - 1, value_step, 0)
    lse = jnp.zeros((BQ, 128), WIDE)
    for pair in range(pairs):
        cut = slice(pair * PAIR, (pair + 1) * PAIR)
        weight = jnp.sum(total[pair], 1, keepdims=True)
        result = gathered[pair]
        if own:
            own_weight = jnp.exp(owns[pair] - peaks[pair])
            weight = weight + own_weight
            values = own_ref[1, :, cut].astype(WIDE)
            result = result + own_weight * jnp.concatenate([values, values], 0)
        result = merge_heads(result / weight)
        att_ref[:, cut] = result.astype(LOW)
        wide_ref[:, cut] = result
        lse = put_columns(lse, pair, peaks[pair] + jnp.log(weight))
    lse_ref[...] = lse


def causal_backward_kernel(own, *refs):
    bounds_ref, q_ref, grad_ref, att_ref, lse_ref, before_ref, here_ref = refs[:7]
    qdoc_ref, kdoc_ref, table_ref, gidx_ref, sidx_ref, hot_ref = refs[7:13]
    refs = refs[13:]
    if own:
        own_ref, refs = refs[0], refs[1:]
    qgrad_ref, tgrad_ref, gbefore_ref, ghere_ref = refs[:4]
    refs = refs[4:]
    if own:
        ograd_ref, refs = refs[0], refs[1:]
    window, wgrad, qgrad, farsum = refs
    stream, step = pl.program_id(0), pl.program_id(1)
    rows = here_ref.shape[1]
    pairs = here_ref.shape[2] // PAIR

    @pl.when((stream == 0) & (step == 0))
    def _():
        fill_window(window, (before_ref, here_ref))
        wgrad[...] = jnp.zeros(wgrad.shape, WIDE)

    near = rows // 128 + step
    low_block = bounds_ref[step]
    qdoc = qdoc_ref[...]
    table = table_ref[...]
    gidx = gidx_ref[...]
    sidx = sidx_ref[...]
    lse_all = lse_ref[...]
    lane = lax.broadcasted_iota(jnp.int32, (BQ, 128), 1)
    row = lax.broadcasted_iota(jnp.int32, (BQ, 128), 0)
    mask_before, mask_here = causal_masks(own, qdoc, kdoc_ref, near)
    near_at = pl.ds(pl.multiple_of((near - 1) * 128, 128), 256)
    queries, grads, queries_t, grads_t, deltas, logs, fars = [], [], [], [], [], [], []
    tgrad = jnp.zeros((BQ, 128), WIDE)
    for pair in range(pairs):
        cut = slice(pair * PAIR, (pair + 1) * PAIR)
        query = stack_heads(q_ref[:, cut]) * HD**-0.5
        grad = stack_heads(grad_ref[:, cut])
        att = att_ref[:, cut]
        delta = jnp.sum(grad * jnp.concatenate([att, att], 0), 1, keepdims=True)
        log_total = pair_columns(lse_all, pair)
        deltas.append(delta)
        logs.append(log_total)
        queries.append(query.astype(LOW))
        grads.append(grad.astype(LOW))
        queries_t.append(query.T.astype(LOW))
        grads_t.append(grad.T.astype(LOW))
        bias_before, bias_here, far = causal_parts(own, table, gidx, pair)
        fars.append(far)
        keys = window[0, near_at, cut]
        values = window[1, near_at, cut]
        found = dot_nt(queries[pair], keys)
        found_before = both_heads(mask_before, found[:, :128] + bias_before)
        found_here = both_heads(mask_here, found[:, 128:] + bias_here)
        probs = jnp.exp(jnp.concatenate([found_before, found_here], 1) - log_total)
        slopes = probs * (dot_nt(grads[pair], values) - delta)
        slopes_low = slopes.astype(LOW)
        qgrad[pair] = dot_nn(slopes_low, keys)
        wgrad[0, cut, near_at] += dot_nn(queries_t[pair], slopes_low)
        wgrad[1, cut, near_at] += dot_nn(grads_t[pair], probs.astype(LOW))
        rest = []
        for side in range(2):
            part_before = slopes[side * BQ : (side + 1) * BQ, :128]
            part_here = slopes[side * BQ : (side + 1) * BQ, 128:]
            merged = jnp.where(lane <= row, part_here, part_before)
            skewed = jnp.take_along_axis(merged, sidx, axis=1, mode="promise_in_bounds")
            tgrad = tgrad + dot_nn(skewed.astype(LOW), hot_ref[2 * pair + side])
            rest.append(jnp.where(lane <= row, part_before, 0.0))
        farsum[pair] = jnp.concatenate(rest, 0)
        if own:
            own_keys = own_ref[0, :, cut].astype(WIDE)
            own_values = own_ref[1, :, cut].astype(WIDE)
            own_keys = jnp.concatenate([own_keys, own_keys], 0)
            own_values = jnp.concatenate([own_values, own_values], 0)
            own_score = jnp.sum(query * own_keys, 1, keepdims=True) + own_column(table, pair)
            own_prob = jnp.exp(own_score - log_total)
            own_slope = own_prob * (jnp.sum(grad * own_values, 1, keepdims=True) - delta)
            qgrad[pair] += own_slope * own_keys
            key_part = own_slope * query
            value_part = own_prob * grad
            ograd_ref[0, :, cut] = (key_part[:BQ] + key_part[BQ:]).astype(LOW)
            ograd_ref[1, :, cut] = (value_part[:BQ] + value_part[BQ:]).astype(LOW)
            for side in range(2):
                place = (2 * pair + side) * BUCKETS
                tgrad = tgrad + jnp.where(lane == place, own_slope[side * BQ : (side + 1) * BQ], 0.0)

    def block_step(block, carry):
        allowed = qdoc == kdoc_ref[block]
        at = pl.ds(pl.multiple_of(block * 128, 128), 128)
        for pair in range(pairs):
            cut = slice(pair * PAIR, (pair + 1) * PAIR)
            keys = window[0, at, cut]
            values = window[1, at, cut]
            found = both_heads(allowed, dot_nt(queries[pair], keys) + fars[pair])
            probs = jnp.exp(found - logs[pair])
            slopes = probs * (dot_nt(grads[pair], values) - deltas[pair])
            farsum[pair] += slopes
            slopes = slopes.astype(LOW)
            qgrad[pair] += dot_nn(slopes, keys)
            wgrad[0, cut, at] += dot_nn(queries_t[pair], slopes)
            wgrad[1, cut, at] += dot_nn(grads_t[pair], probs.astype(LOW))
        return carry

    lax.fori_loop(low_block, near - 1, block_step, 0)
    for pair in range(pairs):
        qgrad_ref[:, pair * PAIR : (pair + 1) * PAIR] = (
            merge_heads(qgrad[pair]) * HD**-0.5
        ).astype(LOW)
        rest = jnp.sum(farsum[pair], 1, keepdims=True)
        for side in range(2):
            place = (2 * pair + side) * BUCKETS + BUCKETS - 1
            tgrad = tgrad + jnp.where(lane == place, rest[side * BQ : (side + 1) * BQ], 0.0)
    tgrad_ref[...] = tgrad.astype(LOW)

    @pl.when((stream == pl.num_programs(0) - 1) & (step == pl.num_programs(1) - 1))
    def _():
        for side in range(2):
            gbefore_ref[side] = wgrad[side, :, :rows].T.astype(LOW)
            ghere_ref[side] = wgrad[side, :, rows:].T


def whole_spec(shape):
    return pl.BlockSpec(shape, lambda stream, step, bounds: (0,) * len(shape))


def rows_spec(width):
    return pl.BlockSpec((None, BQ, width), lambda stream, step, bounds: (stream, step, 0))


def pair_rows_spec(width):
    return pl.BlockSpec((None, 2, BQ, width), lambda stream, step, bounds: (stream, 0, step, 0))


QDOC_SPEC = pl.BlockSpec((BQ, 1), lambda stream, step, bounds: (step, 0))


def shaped(shape, dtype):
    return jax.ShapeDtypeStruct(shape, dtype)


def local_call(kernel, grid, in_specs, out_specs, out_shape, scratch, cost):
    return pl.pallas_call(
        kernel,
        grid_spec=pltpu.PrefetchScalarGridSpec(
            num_scalar_prefetch=1,
            grid=grid,
            in_specs=in_specs,
            out_specs=out_specs,
            scratch_shapes=scratch,
        ),
        out_shape=out_shape,
        compiler_params=pltpu.CompilerParams(
            vmem_limit_bytes=VMEM_BYTES, dimension_semantics=("arbitrary", "arbitrary")
        ),
        cost_estimate=pl.CostEstimate(
            flops=int(cost), bytes_accessed=int(cost), transcendentals=0
        ),
    )


def full_forward(with_self, bounds, queries, before, here, after, qdoc, kdoc):
    streams, rows, width = queries.shape
    pairs = width // PAIR
    blocks = 3 * rows // BK
    kv_spec = whole_spec((2, rows, width))
    return local_call(
        functools.partial(full_forward_kernel, with_self),
        (streams, rows // BQ),
        [rows_spec(width), kv_spec, kv_spec, kv_spec, QDOC_SPEC, whole_spec((blocks, 1, BK))],
        [rows_spec(width), rows_spec(width), rows_spec(128)],
        [
            shaped((streams, rows, width), LOW),
            shaped((streams, rows, width), WIDE),
            shaped((streams, rows, 128), WIDE),
        ],
        [
            pltpu.VMEM((2, 3 * rows, width), LOW),
            pltpu.VMEM((blocks, pairs, 2 * BQ, BK), WIDE),
            pltpu.VMEM((pairs, 2 * BQ, 128), WIDE),
            pltpu.VMEM((pairs, 2 * BQ, 128), WIDE),
            pltpu.VMEM((pairs, 2 * BQ, 128), WIDE),
        ],
        1000,
    )(bounds, queries, before, here, after, qdoc, kdoc)


def full_backward(with_self, bounds, queries, grads, att, lse, before, here, after, qdoc, kdoc):
    streams, rows, width = queries.shape
    pairs = width // PAIR
    blocks = 3 * rows // BK
    kv_spec = whole_spec((2, rows, width))
    grad_spec = whole_spec((2, rows, width))
    return local_call(
        functools.partial(full_backward_kernel, with_self),
        (streams, rows // BQ),
        [rows_spec(width)] * 3
        + [rows_spec(128), kv_spec, kv_spec, kv_spec, QDOC_SPEC, whole_spec((blocks, 1, BK))],
        [rows_spec(width), grad_spec, grad_spec, grad_spec],
        [
            shaped((streams, rows, width), LOW),
            shaped((2, rows, width), LOW),
            shaped((2, rows, width), WIDE),
            shaped((2, rows, width), LOW),
        ],
        [
            pltpu.VMEM((2, 3 * rows, width), LOW),
            pltpu.VMEM((2, width, 3 * rows), WIDE),
            pltpu.VMEM((pairs, 2 * BQ, 128), WIDE),
        ],
        1000,
    )(bounds, queries, grads, att, lse, before, here, after, qdoc, kdoc)


def spread_index():
    row, lane = np.arange(BQ)[:, None], np.arange(128)[None, :]
    return bucket_table((row - lane) % 128).astype(np.int32)


def skew_index():
    row, lane = np.arange(BQ)[:, None], np.arange(128)[None, :]
    return ((row - lane) % 128).astype(np.int32)


def bucket_hot(heads):
    offsets = np.arange(128)
    hot = np.zeros((heads, 128, 128), np.float32)
    for head in range(heads):
        hot[head, offsets, head * BUCKETS + bucket_table(offsets)] = 1.0
    return hot


def causal_forward(own, bounds, queries, before, here, qdoc, kdoc, tables, own_pair):
    streams, rows, width = queries.shape
    pairs = width // PAIR
    blocks = 2 * rows // 128
    kv_spec = whole_spec((2, rows, width))
    specs = [rows_spec(width), kv_spec, kv_spec, QDOC_SPEC, whole_spec((blocks, 1, 128))]
    specs += [rows_spec(128), whole_spec((BQ, 128))]
    operands = [bounds, queries, before, here, qdoc, kdoc, tables, jnp.asarray(spread_index())]
    if own:
        specs.append(pair_rows_spec(width))
        operands.append(own_pair)
    return local_call(
        functools.partial(causal_forward_kernel, own),
        (streams, rows // BQ),
        specs,
        [rows_spec(width), rows_spec(width), rows_spec(128)],
        [
            shaped((streams, rows, width), LOW),
            shaped((streams, rows, width), WIDE),
            shaped((streams, rows, 128), WIDE),
        ],
        [
            pltpu.VMEM((2, 2 * rows, width), LOW),
            pltpu.VMEM((blocks, pairs, 2 * BQ, 128), WIDE),
            pltpu.VMEM((pairs, 2 * BQ, 128), WIDE),
            pltpu.VMEM((pairs, 2 * BQ, 128), WIDE),
            pltpu.VMEM((pairs, 2 * BQ, 128), WIDE),
        ],
        1000,
    )(*operands)


def causal_backward(
    own, bounds, queries, grads, att, lse, before, here, qdoc, kdoc, tables, own_pair
):
    streams, rows, width = queries.shape
    pairs = width // PAIR
    blocks = 2 * rows // 128
    kv_spec = whole_spec((2, rows, width))
    grad_spec = whole_spec((2, rows, width))
    specs = [rows_spec(width)] * 3 + [rows_spec(128), kv_spec, kv_spec, QDOC_SPEC]
    specs += [whole_spec((blocks, 1, 128)), rows_spec(128), whole_spec((BQ, 128))]
    specs += [whole_spec((BQ, 128)), whole_spec((2 * pairs, 128, 128))]
    operands = [bounds, queries, grads, att, lse, before, here, qdoc, kdoc, tables]
    operands += [jnp.asarray(spread_index()), jnp.asarray(skew_index())]
    operands += [jnp.asarray(bucket_hot(2 * pairs), LOW)]
    out_specs = [rows_spec(width), rows_spec(128), grad_spec, grad_spec]
    out_shape = [
        shaped((streams, rows, width), LOW),
        shaped((streams, rows, 128), LOW),
        shaped((2, rows, width), LOW),
        shaped((2, rows, width), WIDE),
    ]
    if own:
        specs.append(pair_rows_spec(width))
        operands.append(own_pair)
        out_specs.append(pair_rows_spec(width))
        out_shape.append(shaped((streams, 2, rows, width), LOW))
    return local_call(
        functools.partial(causal_backward_kernel, own),
        (streams, rows // BQ),
        specs,
        out_specs,
        out_shape,
        [
            pltpu.VMEM((2, 2 * rows, width), LOW),
            pltpu.VMEM((2, width, 2 * rows), WIDE),
            pltpu.VMEM((pairs, 2 * BQ, 128), WIDE),
            pltpu.VMEM((pairs, 2 * BQ, 128), WIDE),
        ],
        1000,
    )(*operands)


SUM_ROWS = 64
SUM_WIDTH = 1024
SUM_DELAY = 3
MESH = pl.DeviceIdType.MESH


def tree_kernel(count, *refs):
    out_ref, x_ref, total, part, landed, sent_up, came_up, sent_down, came_down, filled = refs[-10:]
    chunks = x_ref.shape[0]
    fills, at = [], 0
    for place, piece in enumerate(refs[:-10]):
        size = piece.shape[0]
        fills.append(
            pltpu.make_async_copy(piece, x_ref.at[pl.ds(at, size)], filled.at[place])
        )
        at += size
    for fill in fills:
        fill.start()
    ring = part.shape[0]
    tall = count // 2
    place = lax.axis_index("seq")
    column = lax.rem(place, 2)
    row = place // 2
    beside = place + 1 - 2 * column

    def everyone(act):
        act(beside, None)
        act(place - 2, row > 0)
        act(place + 2, row < tall - 1)

    barrier = pltpu.get_barrier_semaphore()

    def greet(device, there):
        def signal():
            pl.semaphore_signal(barrier, inc=1, device_id={"seq": device}, device_id_type=MESH)

        if there is None:
            signal()
        else:
            pl.when(there)(signal)

    everyone(greet)
    friends = 1 + (row > 0).astype(jnp.int32) + (row < tall - 1).astype(jnp.int32)
    pl.semaphore_wait(barrier, friends)

    def role(chunk):
        kind = lax.rem(chunk, 6 + tall)
        spine = kind < 6
        top = jnp.where(spine, tall // 2 - 1 + lax.rem(kind // 2, 2), kind - 6)
        main = column == lax.rem(kind, 2)
        walks = main | jnp.logical_not(spine)
        here = row == top
        children = (
            main & (spine | here),
            walks & (row > 0) & (row <= top),
            walks & (row < tall - 1) & (row >= top),
        )
        reach = jnp.where(row < top, row, tall - 1 - row)
        reach = jnp.where(here, jnp.maximum(top, tall - 1 - top), reach)
        level = jnp.where(
            spine, jnp.where(main, 1 + reach, 0), reach + (here & main).astype(jnp.int32)
        )
        depth = jnp.abs(row - top) + jnp.logical_not(main).astype(jnp.int32)
        sideways = jnp.logical_not(main) & (spine | here)
        return children, level, depth, main & here, sideways, row < top

    devices = (beside, place - 2, place + 2)

    def up_copy(chunk, slot, device):
        at = lax.rem(chunk, ring)
        return pltpu.make_async_remote_copy(
            src_ref=part.at[at],
            dst_ref=landed.at[at, slot],
            send_sem=sent_up.at[at],
            recv_sem=came_up.at[at, slot],
            device_id={"seq": device},
            device_id_type=MESH,
        )

    def down_copy(chunk, slot, device):
        at = lax.rem(chunk, ring)
        return pltpu.make_async_remote_copy(
            src_ref=out_ref.at[chunk],
            dst_ref=out_ref.at[chunk],
            send_sem=sent_down.at[at, slot],
            recv_sem=came_down.at[at],
            device_id={"seq": device},
            device_id_type=MESH,
        )

    def spread(chunk, children):
        for slot, child in enumerate(children):

            @pl.when(child)
            def _():
                down_copy(chunk, slot, devices[slot]).start()

    def climb(chunk, children, root, sideways, rising):
        at = lax.rem(chunk, ring)
        total[...] = x_ref[chunk].astype(WIDE)
        for slot, child in enumerate(children):

            @pl.when(child)
            def _():
                up_copy(chunk, slot, devices[slot]).wait_recv()
                total[...] += landed[at, slot].astype(WIDE)

        @pl.when(root)
        def _():
            out_ref[chunk] = total[...].astype(LOW)
            spread(chunk, children)

        @pl.when(jnp.logical_not(root))
        def _():
            part[at] = total[...].astype(LOW)

            @pl.when(sideways)
            def _():
                up_copy(chunk, 0, beside).start()

            @pl.when(jnp.logical_not(sideways) & rising)
            def _():
                up_copy(chunk, 1, place + 2).start()

            @pl.when(jnp.logical_not(sideways) & jnp.logical_not(rising))
            def _():
                up_copy(chunk, 2, place - 2).start()

    def fall(chunk, children):
        down_copy(chunk, 0, beside).wait_recv()
        up_copy(chunk, 0, beside).wait_send()
        spread(chunk, children)

    def finish(chunk, children):
        for slot, child in enumerate(children):

            @pl.when(child)
            def _():
                down_copy(chunk, slot, devices[slot]).wait_send()

    levels = tall + 1
    for fill in fills:
        fill.wait()

    def period(time, carry):
        def at_level(place_in_line, act):
            chunk = time - SUM_DELAY * place_in_line

            @pl.when((chunk >= 0) & (chunk < chunks))
            def _():
                act(chunk)

        def finish_step(chunk):
            finish(chunk, role(chunk)[0])

        at_level(2 * levels + 1, finish_step)
        for depth_now in range(levels, 0, -1):

            def fall_step(chunk, depth_now=depth_now):
                children, _, depth, root, _, _ = role(chunk)

                @pl.when((depth == depth_now) & jnp.logical_not(root))
                def _():
                    fall(chunk, children)

            at_level(levels + depth_now, fall_step)
        for level_now in range(levels - 1, -1, -1):

            def climb_step(chunk, level_now=level_now):
                children, level, _, root, sideways, rising = role(chunk)

                @pl.when(level == level_now)
                def _():
                    climb(chunk, children, root, sideways, rising)

            at_level(level_now, climb_step)
        return carry

    lax.fori_loop(0, chunks + SUM_DELAY * (2 * levels + 1), period, 0)


def link_sum(pieces, count):
    levels = count // 2 + 1
    chunks = sum(piece.shape[0] for piece in pieces)
    ring = min(chunks, SUM_DELAY * (2 * levels + 1) + 1)
    block = (SUM_ROWS, SUM_WIDTH)
    return pl.pallas_call(
        functools.partial(tree_kernel, count),
        in_specs=[pl.BlockSpec(memory_space=pl.ANY)] * len(pieces),
        out_specs=pl.BlockSpec(memory_space=pltpu.VMEM),
        out_shape=shaped((chunks,) + block, LOW),
        scratch_shapes=[
            pltpu.VMEM((chunks,) + block, LOW),
            pltpu.VMEM(block, WIDE),
            pltpu.VMEM((ring,) + block, LOW),
            pltpu.VMEM((ring, 3) + block, LOW),
            pltpu.SemaphoreType.DMA((ring,)),
            pltpu.SemaphoreType.DMA((ring, 3)),
            pltpu.SemaphoreType.DMA((ring, 3)),
            pltpu.SemaphoreType.DMA((ring,)),
            pltpu.SemaphoreType.DMA((len(pieces),)),
        ],
        compiler_params=pltpu.CompilerParams(
            collective_id=0, has_side_effects=True, vmem_limit_bytes=56 * 1024 * 1024
        ),
        cost_estimate=pl.CostEstimate(flops=1000, bytes_accessed=1000, transcendentals=0),
    )(*pieces)


PLAN = (
    "e012ee0eee10ee20102010112122020101212020",
    "101212F020011212e200Ce1e11Ce2eGe202ee100",
    "S122D00eeWWee",
)


class Kept:
    pass


class Order:
    def __init__(self):
        self.token = None

    def enter(self, *values):
        if self.token is None:
            return values
        values, _ = lax.optimization_barrier((values, self.token))
        return values

    def leave(self, value):
        self.token = value


def swap_core(value):
    count = lax.axis_size("tp")
    return lax.ppermute(value, "tp", [(place, place ^ 1) for place in range(count)])


def swap_chip(low):
    count = lax.axis_size("tp")
    hop = 2
    got = lax.ppermute(low, "tp", [(place, place ^ hop) for place in range(count)])
    while 2 * hop < count:
        hop *= 2
        low = (low.astype(WIDE) + got.astype(WIDE)).astype(LOW)
        got = lax.ppermute(low, "tp", [(place, place ^ hop) for place in range(count)])
    return low, got


def core_index():
    return lax.rem(lax.axis_index("tp"), 2)


def half_rows(rows, mine):
    half = rows.shape[1] // 2
    core = core_index() if mine else 1 - core_index()
    return lax.dynamic_slice_in_dim(rows, core * half, half, 1)


def natural_rows(mine, other):
    first = core_index() == 0
    return jnp.concatenate([jnp.where(first, mine, other), jnp.where(first, other, mine)], 1)


def project(rows, weight):
    return jnp.einsum("gsd,df->gsf", rows, weight, preferred_element_type=WIDE)


def back_project(grads, weight):
    return jnp.einsum("gsf,df->gsd", grads, weight, preferred_element_type=WIDE)


def weight_grad(rows, grads):
    return jnp.einsum("gsd,gsf->df", rows, grads, preferred_element_type=WIDE)


def split_rows(cells):
    if isinstance(cells, tuple):
        return list(cells)
    return [half_rows(cells, True), half_rows(cells, False)]


def rows_weight_grad(lefts, rights):
    lefts = [part for cells in lefts for part in split_rows(cells)]
    rights = [part for cells in rights for part in split_rows(cells)]
    return weight_grad(jnp.concatenate(lefts, 1), jnp.concatenate(rights, 1))


def norm_forward(resid, gain, shift):
    mean = jnp.mean(resid, -1, keepdims=True)
    centred = resid - mean
    inverse = lax.rsqrt(jnp.mean(centred * centred, -1, keepdims=True) + 1e-05)
    normed = centred * inverse
    return (normed * gain + shift, normed, inverse)


def norm_backward(grad_out, saved, gain):
    normed, inverse = saved
    grad_normed = grad_out * gain
    grad_resid = inverse * (
        grad_normed
        - jnp.mean(grad_normed, -1, keepdims=True)
        - normed * jnp.mean(grad_normed * normed, -1, keepdims=True)
    )
    sums = jnp.stack([jnp.sum(grad_out * normed, (0, 1)), jnp.sum(grad_out, (0, 1))])
    return (grad_resid, sums)


def gelu_both(hidden):
    scaled = hidden * (0.5**0.5)
    half = 0.5 * lax.erf(scaled) + 0.5
    slope = half + hidden * jnp.exp(-(scaled * scaled)) * ((2.0 * math.pi) ** -0.5)
    return ((hidden * half).astype(LOW), slope.astype(LOW))


def passed_along(value, steps):
    count = lax.axis_size("seq")
    if steps > 0:
        pairs = [(place, place + 1) for place in range(count - 1)]
    else:
        pairs = [(place + 1, place) for place in range(count - 1)]
    return lax.ppermute(value, "seq", pairs)


def doc_index(positions, ends):
    return jnp.sum((positions[:, None] >= ends[None, :]).astype(jnp.int32), 1)


def pick(owner, values):
    match = owner[:, None] == jnp.arange(values.shape[0], dtype=jnp.int32)[None, :]
    return jnp.sum(jnp.where(match, values[None, :], 0), 1)


def pad_tables(tables):
    missing = 128 - tables.shape[-1]
    return jnp.pad(tables, ((0, 0), (0, 0), (0, missing))) if missing else tables


def sum_seq(values, turn):
    places = list(range(lax.axis_size("seq")))
    return lax.psum(tuple(values), "seq", axis_index_groups=[places[turn:] + places[:turn]])


def per_device(
    enc_input,
    dec_input,
    enc_cotan,
    dec_cotan,
    doc_lengths,
    src_padding,
    enc_qkv,
    enc_wout,
    enc_gain,
    enc_bias,
    enc_up,
    enc_down,
    post_gain,
    post_bias,
    self_qkv,
    self_rel,
    self_wout,
    self_gain,
    self_bias,
    cross_wq,
    cross_wkv,
    cross_wout,
    cross_gain,
    cross_bias,
    ffn_up,
    ffn_down,
    ffn_gain,
    ffn_bias,
):
    rows = enc_input.shape[0]
    half = rows // 2
    streams = dec_input.shape[0]
    table_width = self_rel.shape[1]
    base = lax.axis_index("seq") * rows
    total_rows = rows * lax.axis_size("seq")
    ends = jnp.cumsum(doc_lengths)
    starts = ends - doc_lengths
    key_pos = base - rows + jnp.arange(3 * rows, dtype=jnp.int32)
    key_valid = (key_pos >= 0) & (key_pos < total_rows)
    key_owner = doc_index(key_pos, ends)
    key_doc = jnp.where(key_valid, key_owner, -1)
    key_pad = (
        lax.dynamic_slice_in_dim(jnp.pad(src_padding, (rows, rows)), base, 3 * rows) == 1
    )
    key_first = key_pos == pick(key_owner, starts)
    qdoc = key_doc[rows : 2 * rows][:, None]
    enc_kdoc = jnp.where(key_pad, key_doc, -1).reshape(-1, 1, BK)
    cross_kdoc = jnp.where(key_pad | key_first, key_doc, -1).reshape(-1, 1, BK)
    self_kdoc = key_doc[: 2 * rows].reshape(-1, 1, 128)
    owners = key_owner[rows : 2 * rows]
    block_first = pick(owners[::BQ], starts) - base + rows
    block_end = pick(owners[BQ - 1 :: BQ], ends) - base + rows
    full_bounds = jnp.stack([block_first // BK, (block_end + BK - 1) // BK])
    self_bounds = block_first // 128

    order = Order()
    enter, leave = order.enter, order.leave
    enc, cross = Kept(), Kept()
    dec = [Kept() for _ in range(streams)]
    straight_rows = enc_input[None]

    def halves(att, weight):
        other = project(half_rows(att, False), weight).astype(LOW)
        mine = project(half_rows(att, True), weight)
        return mine, other

    def back_halves(grads, weight):
        other = back_project(half_rows(grads, False), weight).astype(LOW)
        mine = back_project(half_rows(grads, True), weight)
        return mine, other

    def exchange(mine, other):
        got = swap_core(other)
        yield
        mine, got = enter(mine, got)
        low = (mine + got.astype(WIDE)).astype(LOW)
        leave(low)
        low, got = swap_chip(low)
        yield
        low, got = enter(low, got)
        return low.astype(WIDE) + got.astype(WIDE)

    def close_branch(resid, mine, other, gain, shift):
        total = yield from exchange(mine, other)
        output, normed, inverse = norm_forward(resid + total, gain, shift)
        low = output.astype(LOW)
        leave(low)
        return output, low, swap_core(low), (normed, inverse)

    def open_branch(grad, saved, gain):
        grad, sums = norm_backward(grad, saved, gain)
        low = grad.astype(LOW)
        leave(low)
        return grad, low, swap_core(low), sums

    def encoder():
        (enc_rows,) = enter(enc_input)
        pair = jnp.einsum("sd,cdf->csf", enc_rows, enc_qkv[1:], preferred_element_type=WIDE).astype(LOW)
        enc.pair = pair
        enc.before = passed_along(pair, 1)
        enc.after = passed_along(pair, -1)
        enc.query = project(enc_rows[None], enc_qkv[0]).astype(LOW)
        leave(enc.query)
        yield
        query, before, after = enter(enc.query, enc.before, enc.after)
        enc.query, enc.before, enc.after = query, before, after
        att, wide, lse = full_forward(
            True, full_bounds, query, before, enc.pair, after, qdoc, enc_kdoc
        )
        enc.att, enc.wide, enc.lse = att, wide, lse
        mine, other = halves(att, enc_wout)
        leave(mine)
        resid = half_rows(straight_rows, True).astype(WIDE)
        resid, mine, got, enc.saved_att = yield from close_branch(
            resid, mine, other, enc_gain, enc_bias
        )
        yield
        mine, got = enter(mine, got)
        middle = jnp.concatenate([mine, got], 1)
        act, slope = gelu_both(project(middle, enc_up))
        enc.middle, enc.act, enc.slope = middle, act, slope
        other = project(act[:, half:], enc_down).astype(LOW)
        mine = project(act[:, :half], enc_down)
        leave(mine)
        resid, mine, got, enc.saved_ffn = yield from close_branch(
            resid, mine, other, post_gain, post_bias
        )
        yield
        mine, got = enter(mine, got)
        enc.final = natural_rows(mine, got)
        pair = jnp.einsum(
            "sd,cdf->csf", enc.final[0], cross_wkv, preferred_element_type=WIDE
        ).astype(LOW)
        leave(pair)
        cross.pair = pair
        cross.before = passed_along(pair, 1)
        cross.after = passed_along(pair, -1)
        yield
        parts = enter(*[dec[stream].cross_parts for stream in range(streams)])
        to_before = sum(part[0].astype(WIDE) for part in parts).astype(LOW)
        to_after = sum(part[2].astype(WIDE) for part in parts).astype(LOW)
        here = sum(part[1] for part in parts)
        leave(to_after)
        from_next = passed_along(to_before, -1)
        from_last = passed_along(to_after, 1)
        yield
        here, from_next, from_last = enter(here, from_next, from_last)
        pair_grad = (here + from_next.astype(WIDE) + from_last.astype(WIDE)).astype(LOW)
        cross.pair_grad = pair_grad
        extra = jnp.einsum("csf,cdf->sd", pair_grad, cross_wkv, preferred_element_type=WIDE)[None]
        mine, other = half_rows(extra, True), half_rows(extra, False).astype(LOW)
        leave(other)
        total = yield from exchange(mine, other)
        grad = half_rows(enc_cotan[None], True).astype(WIDE) + total
        grad, mine, got, enc.post_sums = open_branch(grad, enc.saved_ffn, post_gain)
        yield
        mine, got = enter(mine, got)
        ffn_rows = jnp.concatenate([mine, got], 1)
        grad_act = jnp.einsum("gsd,fd->gsf", ffn_rows, enc_down, preferred_element_type=WIDE)
        hidden_grad = (grad_act * enc.slope.astype(WIDE)).astype(LOW)
        enc.ffn_rows, enc.hidden_grad = ffn_rows, hidden_grad
        other = back_project(hidden_grad[:, half:], enc_up).astype(LOW)
        mine = back_project(hidden_grad[:, :half], enc_up)
        leave(mine)
        total = yield from exchange(mine, other)
        grad, mine, got, enc.att_sums = open_branch(grad + total, enc.saved_att, enc_gain)
        yield
        mine, got = enter(mine, got)
        enc.att_rows = (mine, got)
        query_grad, to_before, here, to_after = full_backward(
            True,
            full_bounds,
            enc.query,
            att_grad(mine, got, enc_wout),
            enc.wide,
            enc.lse,
            enc.before,
            enc.pair,
            enc.after,
            qdoc,
            enc_kdoc,
        )
        leave(query_grad)
        from_next = passed_along(to_before, -1)
        from_last = passed_along(to_after, 1)
        yield
        here, from_next, from_last = enter(here, from_next, from_last)
        pair_grad = (here + from_next.astype(WIDE) + from_last.astype(WIDE)).astype(LOW)
        enc.query_grad, enc.pair_grad = query_grad, pair_grad
        partial_value = back_project(query_grad, enc_qkv[0]) + jnp.einsum(
            "csf,cdf->sd", pair_grad, enc_qkv[1:], preferred_element_type=WIDE
        )
        mine, other = half_rows(partial_value, True), half_rows(partial_value, False).astype(LOW)
        leave(other)
        total = yield from exchange(mine, other)
        low = (grad + total).astype(LOW)
        leave(low)
        got = swap_core(low)
        yield
        low, got = enter(low, got)
        enc.grad = natural_rows(low, got)[0]
        leave(enc.grad)
        yield

    def att_grad(mine, other, weight):
        return natural_rows(
            jnp.einsum("gsd,fd->gsf", mine, weight, preferred_element_type=WIDE).astype(LOW),
            jnp.einsum("gsd,fd->gsf", other, weight, preferred_element_type=WIDE).astype(LOW),
        )

    def decoder(stream):
        own = stream > 0
        kept = dec[stream]
        (dec_rows,) = enter(dec_input[stream : stream + 1])
        pair = jnp.einsum(
            "gsd,cdf->gcsf", dec_rows, self_qkv[1:], preferred_element_type=WIDE
        ).astype(LOW)
        query = project(dec_rows, self_qkv[0]).astype(LOW)
        table = pad_tables(project(dec_rows, self_rel))
        leave((pair, query, table))
        if stream == 0:
            cross.main = pair[0]
            cross.main_before = passed_along(pair[0], 1)
        yield
        main = cross.main
        query, main_before = enter(query, cross.main_before)
        cross.main_before = main_before
        own_pair = pair if own else None
        att, wide, lse = causal_forward(
            own, self_bounds, query, main_before, main, qdoc, self_kdoc, table, own_pair
        )
        kept.self_att = att
        mine, other = halves(att, self_wout)
        leave(mine)
        resid, mine, got, saved_self = yield from close_branch(
            half_rows(dec_rows, True).astype(WIDE), mine, other, self_gain, self_bias
        )
        yield
        mine, got = enter(mine, got)
        kept.first = (mine, got)
        cross_query = natural_rows(
            project(mine, cross_wq).astype(LOW), project(got, cross_wq).astype(LOW)
        )
        leave(cross_query)
        yield
        cross_query, before, after = enter(cross_query, cross.before, cross.after)
        cross.before, cross.after = before, after
        cross_att, cross_wide, cross_lse = full_forward(
            False, full_bounds, cross_query, before, cross.pair, after, qdoc, cross_kdoc
        )
        kept.cross_att = cross_att
        mine, other = halves(cross_att, cross_wout)
        leave(mine)
        resid, mine, got, saved_cross = yield from close_branch(
            resid, mine, other, cross_gain, cross_bias
        )
        yield
        mine, got = enter(mine, got)
        second = jnp.concatenate([mine, got], 1)
        act, slope = gelu_both(project(second, ffn_up))
        kept.second, kept.act = second, act
        other = project(act[:, half:], ffn_down).astype(LOW)
        mine = project(act[:, :half], ffn_down)
        leave(mine)
        total = yield from exchange(mine, other)
        output, normed, inverse = norm_forward(resid + total, ffn_gain, ffn_bias)
        final_mine = output.astype(LOW)
        final_got = swap_core(final_mine)
        grad = half_rows(dec_cotan[stream : stream + 1], True).astype(WIDE)
        grad, mine, got, kept.ffn_sums = open_branch(grad, (normed, inverse), ffn_gain)
        yield
        mine, got = enter(mine, got)
        ffn_rows = jnp.concatenate([mine, got], 1)
        grad_act = jnp.einsum("gsd,fd->gsf", ffn_rows, ffn_down, preferred_element_type=WIDE)
        hidden_grad = (grad_act * slope.astype(WIDE)).astype(LOW)
        kept.ffn_rows, kept.hidden_grad = ffn_rows, hidden_grad
        other = back_project(hidden_grad[:, half:], ffn_up).astype(LOW)
        mine = back_project(hidden_grad[:, :half], ffn_up)
        leave(mine)
        total = yield from exchange(mine, other)
        grad, mine, got, kept.cross_sums = open_branch(grad + total, saved_cross, cross_gain)
        kept.final = natural_rows(final_mine, final_got)
        yield
        mine, got = enter(mine, got)
        kept.cross_rows = (mine, got)
        query_grad, *kept.cross_parts = full_backward(
            False,
            full_bounds,
            cross_query,
            att_grad(mine, got, cross_wout),
            cross_wide,
            cross_lse,
            cross.before,
            cross.pair,
            cross.after,
            qdoc,
            cross_kdoc,
        )
        kept.cross_query_grad = query_grad
        mine, other = back_halves(query_grad, cross_wq)
        leave(mine)
        total = yield from exchange(mine, other)
        grad, mine, got, kept.self_sums = open_branch(grad + total, saved_self, self_gain)
        yield
        mine, got = enter(mine, got)
        kept.self_rows = (mine, got)
        query_grad, table_grad, to_before, here, *own_grad = causal_backward(
            own,
            self_bounds,
            query,
            att_grad(mine, got, self_wout),
            wide,
            lse,
            main_before,
            main,
            qdoc,
            self_kdoc,
            table,
            own_pair,
        )
        table_grad = table_grad[:, :, :table_width]
        kept.table_grad = table_grad
        kept.self_parts = (to_before, here)
        leave(query_grad)
        if own:
            pair_grad = own_grad[0][0]
        else:
            yield
            parts = enter(*[dec[item].self_parts for item in range(streams)])
            to_before = sum(part[0].astype(WIDE) for part in parts).astype(LOW)
            here = sum(part[1] for part in parts)
            leave(to_before)
            from_next = passed_along(to_before, -1)
            yield
            here, from_next = enter(here, from_next)
            pair_grad = (here + from_next.astype(WIDE)).astype(LOW)
        kept.query_grad, kept.pair_grad = query_grad, pair_grad
        partial_value = (
            back_project(query_grad, self_qkv[0])
            + jnp.einsum("csf,cdf->sd", pair_grad, self_qkv[1:], preferred_element_type=WIDE)
            + back_project(table_grad, self_rel)
        )
        mine, other = half_rows(partial_value, True), half_rows(partial_value, False).astype(LOW)
        leave(other)
        total = yield from exchange(mine, other)
        low = (grad + total).astype(LOW)
        leave(low)
        got = swap_core(low)
        yield
        low, got = enter(low, got)
        kept.grad = natural_rows(low, got)
        leave(kept.grad)
        yield

    weights = Kept()

    def ffn_weights():
        acts, grads = enter([kept.act for kept in dec], [kept.ffn_rows for kept in dec])
        down = weight_grad(jnp.concatenate(acts), jnp.concatenate(grads)).astype(LOW)
        seconds, grads = [kept.second for kept in dec], [kept.hidden_grad for kept in dec]
        up = weight_grad(jnp.concatenate(seconds), jnp.concatenate(grads)).astype(LOW)
        leave((down, up))
        weights.ffn = sum_seq((down, up), 0)
        yield

    def cross_weights():
        atts, grads = enter([kept.cross_att for kept in dec], [kept.cross_rows for kept in dec])
        wout = rows_weight_grad(atts, grads).astype(LOW)
        firsts = [kept.first for kept in dec]
        wq = rows_weight_grad(firsts, [kept.cross_query_grad for kept in dec]).astype(LOW)
        leave((wout, wq))
        weights.cross = (wout, wq)
        yield
        (final,) = enter(enc.final)
        wkv = jnp.einsum(
            "sd,csf->cdf", final[0], cross.pair_grad, preferred_element_type=WIDE
        ).astype(LOW)
        leave(wkv)
        weights.cross = sum_seq(weights.cross + (wkv,), 1)
        yield

    def enc_ffn_weights():
        act, grads = enter(enc.act, enc.ffn_rows)
        down = weight_grad(act, grads).astype(LOW)
        up = weight_grad(enc.middle, enc.hidden_grad).astype(LOW)
        leave((down, up))
        weights.enc = [down, up]
        yield

    def turned(cells):
        return jnp.swapaxes(cells, -1, -2)

    def self_weights():
        atts, grads = enter([kept.self_att for kept in dec], [kept.self_rows for kept in dec])
        wout = rows_weight_grad(atts, grads).astype(LOW)
        tables = jnp.concatenate([kept.table_grad for kept in dec], 0)
        rel = weight_grad(tables, dec_input).astype(LOW)
        queries = jnp.concatenate([kept.query_grad for kept in dec])
        query = weight_grad(queries, dec_input).astype(LOW)
        pairs = jnp.stack([kept.pair_grad for kept in dec])
        pair = jnp.einsum(
            "gsd,gcsf->cfd", dec_input, pairs, preferred_element_type=WIDE
        ).astype(LOW)
        leave((wout, rel, query, pair))
        weights.self = [wout, rel, query, pair]
        yield

    def finished():
        (finals,) = enter([kept.final for kept in dec])
        weights.final = jnp.concatenate(finals, 0)
        leave(weights.final)
        yield

    def enc_weights():
        query_grad, pair_grad, grads = enter(enc.query_grad, enc.pair_grad, enc.att_rows)
        query = weight_grad(query_grad, straight_rows).astype(LOW)
        pair = jnp.einsum(
            "sd,csf->cfd", enc_input, pair_grad, preferred_element_type=WIDE
        ).astype(LOW)
        wout = rows_weight_grad([enc.att], [grads]).astype(LOW)
        sums = jnp.concatenate(
            [
                enc.att_sums,
                enc.post_sums,
                sum(kept.self_sums for kept in dec),
                sum(kept.cross_sums for kept in dec),
                sum(kept.ffn_sums for kept in dec),
            ],
            0,
        )
        sums = (sums + swap_core(sums)).astype(LOW).reshape(-1, SUM_WIDTH)
        padded = jnp.pad(sums, ((0, -sums.shape[0] % SUM_ROWS), (0, 0)))
        parts = weights.enc + weights.self + [wout, query, pair]
        pieces = [part.reshape(-1, SUM_ROWS, SUM_WIDTH) for part in parts + [padded]]
        parts.append(sums)
        leave((wout, query, pair, padded))
        yield
        pieces = enter(*pieces)
        summed = link_sum(pieces, lax.axis_size("seq"))
        leave(summed)
        weights.ffn, weights.cross = enter(weights.ffn, weights.cross)
        summed = summed.reshape(-1, SUM_WIDTH)
        found, at = [], 0
        for part in parts:
            size = part.size // SUM_WIDTH
            found.append(summed[at : at + size].astype(WIDE).reshape(part.shape))
            at += size
        weights.last = found
        yield

    tasks = {"e": encoder(), "F": ffn_weights(), "C": cross_weights()}
    tasks.update({"D": finished(), "G": enc_ffn_weights(), "S": self_weights(), "W": enc_weights()})
    tasks.update({str(stream): decoder(stream) for stream in range(streams)})
    for item in "".join(PLAN):
        next(tasks[item], None)
    for task in tasks.values():
        for _ in task:
            pass

    ffn_down_grad, ffn_up_grad = [value.astype(WIDE) for value in weights.ffn]
    cross_wout_grad, cross_wq_grad, cross_wkv_grad = [
        value.astype(WIDE) for value in weights.cross
    ]
    enc_down_grad, enc_up_grad, *found = weights.last
    self_wout_grad, self_rel_grad, query, pair, *found = found
    self_qkv_grad = jnp.concatenate([turned(query)[None], turned(pair)], 0)
    enc_wout_grad, query, pair, sums = found
    enc_qkv_grad = jnp.concatenate([turned(query)[None], turned(pair)], 0)
    sums = sums.reshape(-1, enc_input.shape[1])
    return (
        enc.final[0],
        weights.final,
        enc.grad,
        jnp.concatenate([kept.grad for kept in dec], 0),
        enc_qkv_grad,
        enc_wout_grad,
        sums[0],
        sums[1],
        enc_up_grad,
        enc_down_grad,
        sums[2],
        sums[3],
        self_qkv_grad,
        self_rel_grad.T,
        self_wout_grad,
        sums[4],
        sums[5],
        cross_wq_grad,
        cross_wkv_grad,
        cross_wout_grad,
        sums[6],
        sums[7],
        ffn_up_grad,
        ffn_down_grad,
        sums[8],
        sums[9],
    )


def solution(mesh):
    in_specs = (
        P("seq", None),
        P(None, "seq", None),
        P("seq", None),
        P(None, "seq", None),
        P(),
        P(),
        P(None, None, "tp"),
        P("tp", None),
        P(),
        P(),
        P(None, "tp"),
        P("tp", None),
        P(),
        P(),
        P(None, None, "tp"),
        P(None, "tp"),
        P("tp", None),
        P(),
        P(),
        P(None, "tp"),
        P(None, None, "tp"),
        P("tp", None),
        P(),
        P(),
        P(None, "tp"),
        P("tp", None),
        P(),
        P(),
    )
    out_specs = (
        P("seq", None),
        P(None, "seq", None),
        P("seq", None),
        P(None, "seq", None),
        P(None, None, "tp"),
        P("tp", None),
        P(),
        P(),
        P(None, "tp"),
        P("tp", None),
        P(),
        P(),
        P(None, None, "tp"),
        P(None, "tp"),
        P("tp", None),
        P(),
        P(),
        P(None, "tp"),
        P(None, None, "tp"),
        P("tp", None),
        P(),
        P(),
        P(None, "tp"),
        P("tp", None),
        P(),
        P(),
    )
    return jax.shard_map(
        per_device, mesh=mesh, in_specs=in_specs, out_specs=out_specs, check_vma=False
    )
```

```python
import functools
import math

import jax
import jax.numpy as jnp
import numpy as np
from jax import lax
from jax.experimental import pallas as pl
from jax.experimental.pallas import tpu as pltpu
from jax.sharding import PartitionSpec as P

HD = 64
BUCKETS = 32
DOC_MAX = 512
PAIR = 2 * HD
BQ = 128
BK = 256
NEG = -1e30
VMEM_BYTES = 40 * 1024 * 1024

LOW = jnp.bfloat16
WIDE = jnp.float32


def bucket_bounds():
    exact = BUCKETS // 2
    bounds = []
    for level in range(1, BUCKETS):
        if level < exact:
            bounds.append(level)
        else:
            bounds.append(int(math.ceil(exact * (128.0 / exact) ** ((level - exact) / exact))))
    return bounds


def bucket_table(offsets):
    return sum((offsets >= bound).astype(np.int32) for bound in bucket_bounds())


def dot_nt(left, right):
    return lax.dot_general(left, right, (((1,), (1,)), ((), ())), preferred_element_type=WIDE)


def dot_nn(left, right):
    return lax.dot_general(left, right, (((1,), (0,)), ((), ())), preferred_element_type=WIDE)


def stack_heads(cells):
    lane = lax.broadcasted_iota(jnp.int32, cells.shape, 1)
    wide = cells.astype(WIDE)
    first = jnp.where(lane < HD, wide, 0.0)
    return jnp.concatenate([first, wide - first], 0)


def merge_heads(cells):
    half = cells.shape[0] // 2
    lane = lax.broadcasted_iota(jnp.int32, (half, cells.shape[1]), 1)
    return jnp.where(lane < HD, cells[:half], cells[half:])


def both_heads(mask, cells):
    return jnp.where(mask[None], cells.reshape(2, BQ, cells.shape[1]), NEG).reshape(cells.shape)


def pair_columns(cells, pair):
    return jnp.concatenate([cells[:, 2 * pair : 2 * pair + 1], cells[:, 2 * pair + 1 : 2 * pair + 2]], 0)


def put_columns(store, pair, column):
    lane = lax.broadcasted_iota(jnp.int32, store.shape, 1)
    store = jnp.where(lane == 2 * pair, column[:BQ], store)
    return jnp.where(lane == 2 * pair + 1, column[BQ:], store)


def fill_window(window, parts):
    rows = parts[0].shape[1]
    for place, part in enumerate(parts):
        window[:, place * rows : (place + 1) * rows, :] = part[...]


def full_mask(with_self, qdoc, kdoc_ref, block, query_at):
    allowed = qdoc == kdoc_ref[block]
    if with_self:
        row = lax.broadcasted_iota(jnp.int32, allowed.shape, 0) + query_at
        column = lax.broadcasted_iota(jnp.int32, allowed.shape, 1) + block * BK
        allowed = allowed | (row == column)
    return allowed


def full_forward_kernel(
    with_self,
    bounds_ref,
    q_ref,
    before_ref,
    here_ref,
    after_ref,
    qdoc_ref,
    kdoc_ref,
    att_ref,
    wide_ref,
    lse_ref,
    window,
    scores,
    top,
    total,
    gathered,
):
    stream, step = pl.program_id(0), pl.program_id(1)
    rows = here_ref.shape[1]
    pairs = here_ref.shape[2] // PAIR

    @pl.when((stream == 0) & (step == 0))
    def _():
        fill_window(window, (before_ref, here_ref, after_ref))

    low_block, high_block = bounds_ref[0, step], bounds_ref[1, step]
    qdoc = qdoc_ref[...]
    queries = [
        (stack_heads(q_ref[:, pair * PAIR : (pair + 1) * PAIR]) * HD**-0.5).astype(LOW)
        for pair in range(pairs)
    ]
    top[...] = jnp.full(top.shape, NEG, WIDE)
    total[...] = jnp.zeros(total.shape, WIDE)
    gathered[...] = jnp.zeros(gathered.shape, WIDE)

    def score_step(block, carry):
        allowed = full_mask(with_self, qdoc, kdoc_ref, block, rows + step * BQ)
        at = pl.ds(pl.multiple_of(block * BK, BK), BK)
        for pair in range(pairs):
            keys = window[0, at, pair * PAIR : (pair + 1) * PAIR]
            found = both_heads(allowed, dot_nt(queries[pair], keys))
            scores[block, pair] = found
            top[pair] = jnp.maximum(top[pair], jnp.maximum(found[:, :128], found[:, 128:]))
        return carry

    lax.fori_loop(low_block, high_block, score_step, 0)
    peaks = [jnp.max(top[pair], 1, keepdims=True) for pair in range(pairs)]

    def value_step(block, carry):
        at = pl.ds(pl.multiple_of(block * BK, BK), BK)
        for pair in range(pairs):
            values = window[1, at, pair * PAIR : (pair + 1) * PAIR]
            weights = jnp.exp(scores[block, pair] - peaks[pair])
            total[pair] += weights[:, :128] + weights[:, 128:]
            gathered[pair] += dot_nn(weights.astype(LOW), values)
        return carry

    lax.fori_loop(low_block, high_block, value_step, 0)
    lse = jnp.zeros((BQ, 128), WIDE)
    for pair in range(pairs):
        weight = jnp.sum(total[pair], 1, keepdims=True)
        result = merge_heads(gathered[pair] / weight)
        att_ref[:, pair * PAIR : (pair + 1) * PAIR] = result.astype(LOW)
        wide_ref[:, pair * PAIR : (pair + 1) * PAIR] = result
        lse = put_columns(lse, pair, peaks[pair] + jnp.log(weight))
    lse_ref[...] = lse


def full_backward_kernel(
    with_self,
    bounds_ref,
    q_ref,
    grad_ref,
    att_ref,
    lse_ref,
    before_ref,
    here_ref,
    after_ref,
    qdoc_ref,
    kdoc_ref,
    qgrad_ref,
    gbefore_ref,
    ghere_ref,
    gafter_ref,
    window,
    wgrad,
    qgrad,
):
    stream, step = pl.program_id(0), pl.program_id(1)
    rows = here_ref.shape[1]
    pairs = here_ref.shape[2] // PAIR

    @pl.when((stream == 0) & (step == 0))
    def _():
        fill_window(window, (before_ref, here_ref, after_ref))
        wgrad[...] = jnp.zeros(wgrad.shape, WIDE)

    low_block, high_block = bounds_ref[0, step], bounds_ref[1, step]
    qdoc = qdoc_ref[...]
    lse_all = lse_ref[...]
    queries, grads, queries_t, grads_t, deltas, logs = [], [], [], [], [], []
    for pair in range(pairs):
        cut = slice(pair * PAIR, (pair + 1) * PAIR)
        query = stack_heads(q_ref[:, cut]) * HD**-0.5
        grad = stack_heads(grad_ref[:, cut])
        att = att_ref[:, cut]
        deltas.append(jnp.sum(grad * jnp.concatenate([att, att], 0), 1, keepdims=True))
        logs.append(pair_columns(lse_all, pair))
        queries.append(query.astype(LOW))
        grads.append(grad.astype(LOW))
        queries_t.append(query.T.astype(LOW))
        grads_t.append(grad.T.astype(LOW))
    qgrad[...] = jnp.zeros(qgrad.shape, WIDE)

    def block_step(block, carry):
        allowed = full_mask(with_self, qdoc, kdoc_ref, block, rows + step * BQ)
        at = pl.ds(pl.multiple_of(block * BK, BK), BK)
        for pair in range(pairs):
            cut = slice(pair * PAIR, (pair + 1) * PAIR)
            keys = window[0, at, cut]
            values = window[1, at, cut]
            probs = jnp.exp(both_heads(allowed, dot_nt(queries[pair], keys)) - logs[pair])
            slopes = probs * (dot_nt(grads[pair], values) - deltas[pair])
            slopes = slopes.astype(LOW)
            qgrad[pair] += dot_nn(slopes, keys)
            wgrad[0, cut, at] += dot_nn(queries_t[pair], slopes)
            wgrad[1, cut, at] += dot_nn(grads_t[pair], probs.astype(LOW))
        return carry

    lax.fori_loop(low_block, high_block, block_step, 0)
    for pair in range(pairs):
        qgrad_ref[:, pair * PAIR : (pair + 1) * PAIR] = (
            merge_heads(qgrad[pair]) * HD**-0.5
        ).astype(LOW)

    @pl.when((stream == pl.num_programs(0) - 1) & (step == pl.num_programs(1) - 1))
    def _():
        for side in range(2):
            gbefore_ref[side] = wgrad[side, :, :rows].T.astype(LOW)
            ghere_ref[side] = wgrad[side, :, rows : 2 * rows].T
            gafter_ref[side] = wgrad[side, :, 2 * rows :].T.astype(LOW)


def causal_parts(own, table, gidx, pair):
    lane = lax.broadcasted_iota(jnp.int32, (BQ, 128), 1)
    row = lax.broadcasted_iota(jnp.int32, (BQ, 128), 0)
    near, far = [], []
    for head in (2 * pair, 2 * pair + 1):
        spread = jnp.take_along_axis(
            table, gidx + head * BUCKETS, axis=1, mode="promise_in_bounds"
        )
        last = table[:, head * BUCKETS + BUCKETS - 1 : head * BUCKETS + BUCKETS]
        near.append((jnp.where(lane > row, spread, last), spread))
        far.append(last)
    bias_before = jnp.concatenate([near[0][0], near[1][0]], 0)
    bias_here = jnp.concatenate([near[0][1], near[1][1]], 0)
    return bias_before, bias_here, jnp.concatenate(far, 0)


def own_column(table, pair):
    first, second = 2 * pair * BUCKETS, (2 * pair + 1) * BUCKETS
    return jnp.concatenate([table[:, first : first + 1], table[:, second : second + 1]], 0)


def causal_masks(own, qdoc, kdoc_ref, near):
    lane = lax.broadcasted_iota(jnp.int32, (BQ, 128), 1)
    row = lax.broadcasted_iota(jnp.int32, (BQ, 128), 0)
    earlier = (lane < row) if own else (lane <= row)
    return qdoc == kdoc_ref[near - 1], (qdoc == kdoc_ref[near]) & earlier


def causal_forward_kernel(own, *refs):
    bounds_ref, q_ref, before_ref, here_ref, qdoc_ref, kdoc_ref, table_ref, gidx_ref = refs[:8]
    refs = refs[8:]
    if own:
        own_ref, refs = refs[0], refs[1:]
    att_ref, wide_ref, lse_ref, window, scores, top, total, gathered = refs
    stream, step = pl.program_id(0), pl.program_id(1)
    rows = here_ref.shape[1]
    pairs = here_ref.shape[2] // PAIR

    @pl.when((stream == 0) & (step == 0))
    def _():
        fill_window(window, (before_ref, here_ref))

    near = rows // 128 + step
    low_block = bounds_ref[step]
    qdoc = qdoc_ref[...]
    table = table_ref[...]
    gidx = gidx_ref[...]
    queries, fars, peaks, owns = [], [], [], []
    mask_before, mask_here = causal_masks(own, qdoc, kdoc_ref, near)
    near_at = pl.ds(pl.multiple_of((near - 1) * 128, 128), 256)
    for pair in range(pairs):
        cut = slice(pair * PAIR, (pair + 1) * PAIR)
        query = stack_heads(q_ref[:, cut]) * HD**-0.5
        queries.append(query.astype(LOW))
        bias_before, bias_here, far = causal_parts(own, table, gidx, pair)
        fars.append(far)
        found = dot_nt(queries[pair], window[0, near_at, cut])
        found_before = both_heads(mask_before, found[:, :128] + bias_before)
        found_here = both_heads(mask_here, found[:, 128:] + bias_here)
        scores[near - 1, pair] = found_before
        scores[near, pair] = found_here
        top[pair] = jnp.maximum(found_before, found_here)
        if own:
            keys = own_ref[0, :, cut].astype(WIDE)
            owns.append(
                jnp.sum(query * jnp.concatenate([keys, keys], 0), 1, keepdims=True)
                + own_column(table, pair)
            )

    def score_step(block, carry):
        allowed = qdoc == kdoc_ref[block]
        at = pl.ds(pl.multiple_of(block * 128, 128), 128)
        for pair in range(pairs):
            keys = window[0, at, pair * PAIR : (pair + 1) * PAIR]
            found = both_heads(allowed, dot_nt(queries[pair], keys) + fars[pair])
            scores[block, pair] = found
            top[pair] = jnp.maximum(top[pair], found)
        return carry

    lax.fori_loop(low_block, near - 1, score_step, 0)
    for pair in range(pairs):
        cut = slice(pair * PAIR, (pair + 1) * PAIR)
        peak = jnp.max(top[pair], 1, keepdims=True)
        if own:
            peak = jnp.maximum(peak, owns[pair])
        peaks.append(peak)
        weights_before = jnp.exp(scores[near - 1, pair] - peak)
        weights_here = jnp.exp(scores[near, pair] - peak)
        total[pair] = weights_before + weights_here
        weights = jnp.concatenate([weights_before, weights_here], 1).astype(LOW)
        gathered[pair] = dot_nn(weights, window[1, near_at, cut])

    def value_step(block, carry):
        at = pl.ds(pl.multiple_of(block * 128, 128), 128)
        for pair in range(pairs):
            values = window[1, at, pair * PAIR : (pair + 1) * PAIR]
            weights = jnp.exp(scores[block, pair] - peaks[pair])
            total[pair] += weights
            gathered[pair] += dot_nn(weights.astype(LOW), values)
        return carry

    lax.fori_loop(low_block, near - 1, value_step, 0)
    lse = jnp.zeros((BQ, 128), WIDE)
    for pair in range(pairs):
        cut = slice(pair * PAIR, (pair + 1) * PAIR)
        weight = jnp.sum(total[pair], 1, keepdims=True)
        result = gathered[pair]
        if own:
            own_weight = jnp.exp(owns[pair] - peaks[pair])
            weight = weight + own_weight
            values = own_ref[1, :, cut].astype(WIDE)
            result = result + own_weight * jnp.concatenate([values, values], 0)
        result = merge_heads(result / weight)
        att_ref[:, cut] = result.astype(LOW)
        wide_ref[:, cut] = result
        lse = put_columns(lse, pair, peaks[pair] + jnp.log(weight))
    lse_ref[...] = lse


def causal_backward_kernel(own, *refs):
    bounds_ref, q_ref, grad_ref, att_ref, lse_ref, before_ref, here_ref = refs[:7]
    qdoc_ref, kdoc_ref, table_ref, gidx_ref, sidx_ref, hot_ref = refs[7:13]
    refs = refs[13:]
    if own:
        own_ref, refs = refs[0], refs[1:]
    qgrad_ref, tgrad_ref, gbefore_ref, ghere_ref = refs[:4]
    refs = refs[4:]
    if own:
        ograd_ref, refs = refs[0], refs[1:]
    window, wgrad, qgrad, farsum = refs
    stream, step = pl.program_id(0), pl.program_id(1)
    rows = here_ref.shape[1]
    pairs = here_ref.shape[2] // PAIR

    @pl.when((stream == 0) & (step == 0))
    def _():
        fill_window(window, (before_ref, here_ref))
        wgrad[...] = jnp.zeros(wgrad.shape, WIDE)

    near = rows // 128 + step
    low_block = bounds_ref[step]
    qdoc = qdoc_ref[...]
    table = table_ref[...]
    gidx = gidx_ref[...]
    sidx = sidx_ref[...]
    lse_all = lse_ref[...]
    lane = lax.broadcasted_iota(jnp.int32, (BQ, 128), 1)
    row = lax.broadcasted_iota(jnp.int32, (BQ, 128), 0)
    mask_before, mask_here = causal_masks(own, qdoc, kdoc_ref, near)
    near_at = pl.ds(pl.multiple_of((near - 1) * 128, 128), 256)
    queries, grads, queries_t, grads_t, deltas, logs, fars = [], [], [], [], [], [], []
    tgrad = jnp.zeros((BQ, 128), WIDE)
    for pair in range(pairs):
        cut = slice(pair * PAIR, (pair + 1) * PAIR)
        query = stack_heads(q_ref[:, cut]) * HD**-0.5
        grad = stack_heads(grad_ref[:, cut])
        att = att_ref[:, cut]
        delta = jnp.sum(grad * jnp.concatenate([att, att], 0), 1, keepdims=True)
        log_total = pair_columns(lse_all, pair)
        deltas.append(delta)
        logs.append(log_total)
        queries.append(query.astype(LOW))
        grads.append(grad.astype(LOW))
        queries_t.append(query.T.astype(LOW))
        grads_t.append(grad.T.astype(LOW))
        bias_before, bias_here, far = causal_parts(own, table, gidx, pair)
        fars.append(far)
        keys = window[0, near_at, cut]
        values = window[1, near_at, cut]
        found = dot_nt(queries[pair], keys)
        found_before = both_heads(mask_before, found[:, :128] + bias_before)
        found_here = both_heads(mask_here, found[:, 128:] + bias_here)
        probs = jnp.exp(jnp.concatenate([found_before, found_here], 1) - log_total)
        slopes = probs * (dot_nt(grads[pair], values) - delta)
        slopes_low = slopes.astype(LOW)
        qgrad[pair] = dot_nn(slopes_low, keys)
        wgrad[0, cut, near_at] += dot_nn(queries_t[pair], slopes_low)
        wgrad[1, cut, near_at] += dot_nn(grads_t[pair], probs.astype(LOW))
        rest = []
        for side in range(2):
            part_before = slopes[side * BQ : (side + 1) * BQ, :128]
            part_here = slopes[side * BQ : (side + 1) * BQ, 128:]
            merged = jnp.where(lane <= row, part_here, part_before)
            skewed = jnp.take_along_axis(merged, sidx, axis=1, mode="promise_in_bounds")
            tgrad = tgrad + dot_nn(skewed.astype(LOW), hot_ref[2 * pair + side])
            rest.append(jnp.where(lane <= row, part_before, 0.0))
        farsum[pair] = jnp.concatenate(rest, 0)
        if own:
            own_keys = own_ref[0, :, cut].astype(WIDE)
            own_values = own_ref[1, :, cut].astype(WIDE)
            own_keys = jnp.concatenate([own_keys, own_keys], 0)
            own_values = jnp.concatenate([own_values, own_values], 0)
            own_score = jnp.sum(query * own_keys, 1, keepdims=True) + own_column(table, pair)
            own_prob = jnp.exp(own_score - log_total)
            own_slope = own_prob * (jnp.sum(grad * own_values, 1, keepdims=True) - delta)
            qgrad[pair] += own_slope * own_keys
            key_part = own_slope * query
            value_part = own_prob * grad
            ograd_ref[0, :, cut] = (key_part[:BQ] + key_part[BQ:]).astype(LOW)
            ograd_ref[1, :, cut] = (value_part[:BQ] + value_part[BQ:]).astype(LOW)
            for side in range(2):
                place = (2 * pair + side) * BUCKETS
                tgrad = tgrad + jnp.where(lane == place, own_slope[side * BQ : (side + 1) * BQ], 0.0)

    def block_step(block, carry):
        allowed = qdoc == kdoc_ref[block]
        at = pl.ds(pl.multiple_of(block * 128, 128), 128)
        for pair in range(pairs):
            cut = slice(pair * PAIR, (pair + 1) * PAIR)
            keys = window[0, at, cut]
            values = window[1, at, cut]
            found = both_heads(allowed, dot_nt(queries[pair], keys) + fars[pair])
            probs = jnp.exp(found - logs[pair])
            slopes = probs * (dot_nt(grads[pair], values) - deltas[pair])
            farsum[pair] += slopes
            slopes = slopes.astype(LOW)
            qgrad[pair] += dot_nn(slopes, keys)
            wgrad[0, cut, at] += dot_nn(queries_t[pair], slopes)
            wgrad[1, cut, at] += dot_nn(grads_t[pair], probs.astype(LOW))
        return carry

    lax.fori_loop(low_block, near - 1, block_step, 0)
    for pair in range(pairs):
        qgrad_ref[:, pair * PAIR : (pair + 1) * PAIR] = (
            merge_heads(qgrad[pair]) * HD**-0.5
        ).astype(LOW)
        rest = jnp.sum(farsum[pair], 1, keepdims=True)
        for side in range(2):
            place = (2 * pair + side) * BUCKETS + BUCKETS - 1
            tgrad = tgrad + jnp.where(lane == place, rest[side * BQ : (side + 1) * BQ], 0.0)
    tgrad_ref[...] = tgrad.astype(LOW)

    @pl.when((stream == pl.num_programs(0) - 1) & (step == pl.num_programs(1) - 1))
    def _():
        for side in range(2):
            gbefore_ref[side] = wgrad[side, :, :rows].T.astype(LOW)
            ghere_ref[side] = wgrad[side, :, rows:].T


def whole_spec(shape):
    return pl.BlockSpec(shape, lambda stream, step, bounds: (0,) * len(shape))


def rows_spec(width):
    return pl.BlockSpec((None, BQ, width), lambda stream, step, bounds: (stream, step, 0))


def pair_rows_spec(width):
    return pl.BlockSpec((None, 2, BQ, width), lambda stream, step, bounds: (stream, 0, step, 0))


QDOC_SPEC = pl.BlockSpec((BQ, 1), lambda stream, step, bounds: (step, 0))


def shaped(shape, dtype):
    return jax.ShapeDtypeStruct(shape, dtype)


def local_call(kernel, grid, in_specs, out_specs, out_shape, scratch, cost):
    return pl.pallas_call(
        kernel,
        grid_spec=pltpu.PrefetchScalarGridSpec(
            num_scalar_prefetch=1,
            grid=grid,
            in_specs=in_specs,
            out_specs=out_specs,
            scratch_shapes=scratch,
        ),
        out_shape=out_shape,
        compiler_params=pltpu.CompilerParams(
            vmem_limit_bytes=VMEM_BYTES, dimension_semantics=("arbitrary", "arbitrary")
        ),
        cost_estimate=pl.CostEstimate(
            flops=int(cost), bytes_accessed=int(cost), transcendentals=0
        ),
    )


def full_forward(with_self, bounds, queries, before, here, after, qdoc, kdoc):
    streams, rows, width = queries.shape
    pairs = width // PAIR
    blocks = 3 * rows // BK
    kv_spec = whole_spec((2, rows, width))
    return local_call(
        functools.partial(full_forward_kernel, with_self),
        (streams, rows // BQ),
        [rows_spec(width), kv_spec, kv_spec, kv_spec, QDOC_SPEC, whole_spec((blocks, 1, BK))],
        [rows_spec(width), rows_spec(width), rows_spec(128)],
        [
            shaped((streams, rows, width), LOW),
            shaped((streams, rows, width), WIDE),
            shaped((streams, rows, 128), WIDE),
        ],
        [
            pltpu.VMEM((2, 3 * rows, width), LOW),
            pltpu.VMEM((blocks, pairs, 2 * BQ, BK), WIDE),
            pltpu.VMEM((pairs, 2 * BQ, 128), WIDE),
            pltpu.VMEM((pairs, 2 * BQ, 128), WIDE),
            pltpu.VMEM((pairs, 2 * BQ, 128), WIDE),
        ],
        1000,
    )(bounds, queries, before, here, after, qdoc, kdoc)


def full_backward(with_self, bounds, queries, grads, att, lse, before, here, after, qdoc, kdoc):
    streams, rows, width = queries.shape
    pairs = width // PAIR
    blocks = 3 * rows // BK
    kv_spec = whole_spec((2, rows, width))
    grad_spec = whole_spec((2, rows, width))
    return local_call(
        functools.partial(full_backward_kernel, with_self),
        (streams, rows // BQ),
        [rows_spec(width)] * 3
        + [rows_spec(128), kv_spec, kv_spec, kv_spec, QDOC_SPEC, whole_spec((blocks, 1, BK))],
        [rows_spec(width), grad_spec, grad_spec, grad_spec],
        [
            shaped((streams, rows, width), LOW),
            shaped((2, rows, width), LOW),
            shaped((2, rows, width), WIDE),
            shaped((2, rows, width), LOW),
        ],
        [
            pltpu.VMEM((2, 3 * rows, width), LOW),
            pltpu.VMEM((2, width, 3 * rows), WIDE),
            pltpu.VMEM((pairs, 2 * BQ, 128), WIDE),
        ],
        1000,
    )(bounds, queries, grads, att, lse, before, here, after, qdoc, kdoc)


def spread_index():
    row, lane = np.arange(BQ)[:, None], np.arange(128)[None, :]
    return bucket_table((row - lane) % 128).astype(np.int32)


def skew_index():
    row, lane = np.arange(BQ)[:, None], np.arange(128)[None, :]
    return ((row - lane) % 128).astype(np.int32)


def bucket_hot(heads):
    offsets = np.arange(128)
    hot = np.zeros((heads, 128, 128), np.float32)
    for head in range(heads):
        hot[head, offsets, head * BUCKETS + bucket_table(offsets)] = 1.0
    return hot


def causal_forward(own, bounds, queries, before, here, qdoc, kdoc, tables, own_pair):
    streams, rows, width = queries.shape
    pairs = width // PAIR
    blocks = 2 * rows // 128
    kv_spec = whole_spec((2, rows, width))
    specs = [rows_spec(width), kv_spec, kv_spec, QDOC_SPEC, whole_spec((blocks, 1, 128))]
    specs += [rows_spec(128), whole_spec((BQ, 128))]
    operands = [bounds, queries, before, here, qdoc, kdoc, tables, jnp.asarray(spread_index())]
    if own:
        specs.append(pair_rows_spec(width))
        operands.append(own_pair)
    return local_call(
        functools.partial(causal_forward_kernel, own),
        (streams, rows // BQ),
        specs,
        [rows_spec(width), rows_spec(width), rows_spec(128)],
        [
            shaped((streams, rows, width), LOW),
            shaped((streams, rows, width), WIDE),
            shaped((streams, rows, 128), WIDE),
        ],
        [
            pltpu.VMEM((2, 2 * rows, width), LOW),
            pltpu.VMEM((blocks, pairs, 2 * BQ, 128), WIDE),
            pltpu.VMEM((pairs, 2 * BQ, 128), WIDE),
            pltpu.VMEM((pairs, 2 * BQ, 128), WIDE),
            pltpu.VMEM((pairs, 2 * BQ, 128), WIDE),
        ],
        1000,
    )(*operands)


def causal_backward(
    own, bounds, queries, grads, att, lse, before, here, qdoc, kdoc, tables, own_pair
):
    streams, rows, width = queries.shape
    pairs = width // PAIR
    blocks = 2 * rows // 128
    kv_spec = whole_spec((2, rows, width))
    grad_spec = whole_spec((2, rows, width))
    specs = [rows_spec(width)] * 3 + [rows_spec(128), kv_spec, kv_spec, QDOC_SPEC]
    specs += [whole_spec((blocks, 1, 128)), rows_spec(128), whole_spec((BQ, 128))]
    specs += [whole_spec((BQ, 128)), whole_spec((2 * pairs, 128, 128))]
    operands = [bounds, queries, grads, att, lse, before, here, qdoc, kdoc, tables]
    operands += [jnp.asarray(spread_index()), jnp.asarray(skew_index())]
    operands += [jnp.asarray(bucket_hot(2 * pairs), LOW)]
    out_specs = [rows_spec(width), rows_spec(128), grad_spec, grad_spec]
    out_shape = [
        shaped((streams, rows, width), LOW),
        shaped((streams, rows, 128), LOW),
        shaped((2, rows, width), LOW),
        shaped((2, rows, width), WIDE),
    ]
    if own:
        specs.append(pair_rows_spec(width))
        operands.append(own_pair)
        out_specs.append(pair_rows_spec(width))
        out_shape.append(shaped((streams, 2, rows, width), LOW))
    return local_call(
        functools.partial(causal_backward_kernel, own),
        (streams, rows // BQ),
        specs,
        out_specs,
        out_shape,
        [
            pltpu.VMEM((2, 2 * rows, width), LOW),
            pltpu.VMEM((2, width, 2 * rows), WIDE),
            pltpu.VMEM((pairs, 2 * BQ, 128), WIDE),
            pltpu.VMEM((pairs, 2 * BQ, 128), WIDE),
        ],
        1000,
    )(*operands)


SUM_ROWS = 256
SUM_WIDTH = 256
SUM_DELAY = 3
MESH = pl.DeviceIdType.MESH


def blocks_of(shape):
    return [(shape[0], column) for column in range(0, shape[1], SUM_WIDTH)]


def tree_kernel(count, pieces, *refs):
    sources, targets, refs = refs[:pieces], refs[pieces : 2 * pieces], refs[2 * pieces :]
    x_ref, out_ref, total, part, landed, sent_up, came_up, sent_down, came_down, filled = refs
    chunks = x_ref.shape[0] // SUM_ROWS
    ring = part.shape[0]
    fills, drains, at = [], [], 0
    for place, (source, target) in enumerate(zip(sources, targets)):
        for rows, column in blocks_of(source.shape):
            columns = pl.ds(column, SUM_WIDTH)
            inside, outside = pl.ds(at, rows), filled.at[len(fills)]
            fills.append(pltpu.make_async_copy(source.at[:, columns], x_ref.at[inside], outside))
            drains.append(pltpu.make_async_copy(out_ref.at[inside], target.at[:, columns], outside))
            at += rows
    if at < x_ref.shape[0]:
        x_ref[at:, :] = jnp.zeros((x_ref.shape[0] - at, SUM_WIDTH), LOW)
    for fill in fills:
        fill.start()
    tall = count // 2
    place = lax.axis_index("seq")
    column = lax.rem(place, 2)
    row = place // 2
    beside = place + 1 - 2 * column

    def everyone(act):
        act(beside, None)
        act(place - 2, row > 0)
        act(place + 2, row < tall - 1)

    barrier = pltpu.get_barrier_semaphore()

    def greet(device, there):
        def signal():
            pl.semaphore_signal(barrier, inc=1, device_id={"seq": device}, device_id_type=MESH)

        if there is None:
            signal()
        else:
            pl.when(there)(signal)

    everyone(greet)
    friends = 1 + (row > 0).astype(jnp.int32) + (row < tall - 1).astype(jnp.int32)
    pl.semaphore_wait(barrier, friends)

    def role(chunk):
        kind = lax.rem(chunk, 6 + tall)
        spine = kind < 6
        top = jnp.where(spine, tall // 2 - 1 + lax.rem(kind // 2, 2), kind - 6)
        main = column == lax.rem(kind, 2)
        walks = main | jnp.logical_not(spine)
        here = row == top
        children = (
            main & (spine | here),
            walks & (row > 0) & (row <= top),
            walks & (row < tall - 1) & (row >= top),
        )
        reach = jnp.where(row < top, row, tall - 1 - row)
        reach = jnp.where(here, jnp.maximum(top, tall - 1 - top), reach)
        level = jnp.where(
            spine, jnp.where(main, 1 + reach, 0), reach + (here & main).astype(jnp.int32)
        )
        depth = jnp.abs(row - top) + jnp.logical_not(main).astype(jnp.int32)
        sideways = jnp.logical_not(main) & (spine | here)
        return children, level, depth, main & here, sideways, row < top

    devices = (beside, place - 2, place + 2)

    def rows_at(chunk):
        return pl.ds(pl.multiple_of(chunk * SUM_ROWS, SUM_ROWS), SUM_ROWS)

    def up_copy(chunk, slot, device):
        at = lax.rem(chunk, ring)
        return pltpu.make_async_remote_copy(
            src_ref=part.at[at],
            dst_ref=landed.at[at, slot],
            send_sem=sent_up.at[at],
            recv_sem=came_up.at[at, slot],
            device_id={"seq": device},
            device_id_type=MESH,
        )

    def down_copy(chunk, slot, device):
        at = lax.rem(chunk, ring)
        return pltpu.make_async_remote_copy(
            src_ref=out_ref.at[rows_at(chunk)],
            dst_ref=out_ref.at[rows_at(chunk)],
            send_sem=sent_down.at[at, slot],
            recv_sem=came_down.at[at],
            device_id={"seq": device},
            device_id_type=MESH,
        )

    def spread(chunk, children):
        for slot, child in enumerate(children):

            @pl.when(child)
            def _():
                down_copy(chunk, slot, devices[slot]).start()

    def climb(chunk, children, root, sideways, rising):
        at = lax.rem(chunk, ring)
        total[...] = x_ref[rows_at(chunk), :].astype(WIDE)
        for slot, child in enumerate(children):

            @pl.when(child)
            def _():
                up_copy(chunk, slot, devices[slot]).wait_recv()
                total[...] += landed[at, slot].astype(WIDE)

        @pl.when(root)
        def _():
            out_ref[rows_at(chunk), :] = total[...].astype(LOW)
            spread(chunk, children)

        @pl.when(jnp.logical_not(root))
        def _():
            part[at] = total[...].astype(LOW)

            @pl.when(sideways)
            def _():
                up_copy(chunk, 0, beside).start()

            @pl.when(jnp.logical_not(sideways) & rising)
            def _():
                up_copy(chunk, 1, place + 2).start()

            @pl.when(jnp.logical_not(sideways) & jnp.logical_not(rising))
            def _():
                up_copy(chunk, 2, place - 2).start()

    def fall(chunk, children):
        down_copy(chunk, 0, beside).wait_recv()
        up_copy(chunk, 0, beside).wait_send()
        spread(chunk, children)

    def finish(chunk, children):
        for slot, child in enumerate(children):

            @pl.when(child)
            def _():
                down_copy(chunk, slot, devices[slot]).wait_send()

    levels = tall + 1
    for fill in fills:
        fill.wait()

    def period(time, carry):
        def at_level(place_in_line, act):
            chunk = time - SUM_DELAY * place_in_line

            @pl.when((chunk >= 0) & (chunk < chunks))
            def _():
                act(chunk)

        def finish_step(chunk):
            finish(chunk, role(chunk)[0])

        at_level(2 * levels + 1, finish_step)
        for depth_now in range(levels, 0, -1):

            def fall_step(chunk, depth_now=depth_now):
                children, _, depth, root, _, _ = role(chunk)

                @pl.when((depth == depth_now) & jnp.logical_not(root))
                def _():
                    fall(chunk, children)

            at_level(levels + depth_now, fall_step)
        for level_now in range(levels - 1, -1, -1):

            def climb_step(chunk, level_now=level_now):
                children, level, _, root, sideways, rising = role(chunk)

                @pl.when(level == level_now)
                def _():
                    climb(chunk, children, root, sideways, rising)

            at_level(level_now, climb_step)
        return carry

    lax.fori_loop(0, chunks + SUM_DELAY * (2 * levels + 1), period, 0)
    for drain in drains:
        drain.start()
    for drain in drains:
        drain.wait()


def link_sum(pieces, count):
    levels = count // 2 + 1
    blocks = [block for piece in pieces for block in blocks_of(piece.shape)]
    chunks = -(-sum(rows for rows, _ in blocks) // SUM_ROWS)
    ring = min(chunks, SUM_DELAY * (2 * levels + 1) + 1)
    block = (SUM_ROWS, SUM_WIDTH)
    anywhere = [pl.BlockSpec(memory_space=pl.ANY)] * len(pieces)
    return pl.pallas_call(
        functools.partial(tree_kernel, count, len(pieces)),
        in_specs=anywhere,
        out_specs=anywhere,
        out_shape=[shaped(piece.shape, LOW) for piece in pieces],
        scratch_shapes=[
            pltpu.VMEM((chunks * SUM_ROWS, SUM_WIDTH), LOW),
            pltpu.VMEM((chunks * SUM_ROWS, SUM_WIDTH), LOW),
            pltpu.VMEM(block, WIDE),
            pltpu.VMEM((ring,) + block, LOW),
            pltpu.VMEM((ring, 3) + block, LOW),
            pltpu.SemaphoreType.DMA((ring,)),
            pltpu.SemaphoreType.DMA((ring, 3)),
            pltpu.SemaphoreType.DMA((ring, 3)),
            pltpu.SemaphoreType.DMA((ring,)),
            pltpu.SemaphoreType.DMA((len(blocks),)),
        ],
        compiler_params=pltpu.CompilerParams(
            collective_id=0, has_side_effects=True, vmem_limit_bytes=56 * 1024 * 1024
        ),
        cost_estimate=pl.CostEstimate(flops=1000, bytes_accessed=1000, transcendentals=0),
    )(*pieces)


PLAN = (
    "e012ee0eee10ee20102010112122020101212020",
    "101212F020011212e200Ce1e11Ce2eGe202ee100",
    "S122D00eeWWee",
)


class Kept:
    pass


class Order:
    def __init__(self):
        self.token = None

    def enter(self, *values):
        if self.token is None:
            return values
        values, _ = lax.optimization_barrier((values, self.token))
        return values

    def leave(self, value):
        self.token = value


def swap_core(value):
    count = lax.axis_size("tp")
    return lax.ppermute(value, "tp", [(place, place ^ 1) for place in range(count)])


def swap_chip(low):
    count = lax.axis_size("tp")
    hop = 2
    got = lax.ppermute(low, "tp", [(place, place ^ hop) for place in range(count)])
    while 2 * hop < count:
        hop *= 2
        low = (low.astype(WIDE) + got.astype(WIDE)).astype(LOW)
        got = lax.ppermute(low, "tp", [(place, place ^ hop) for place in range(count)])
    return low, got


def core_index():
    return lax.rem(lax.axis_index("tp"), 2)


def half_rows(rows, mine):
    half = rows.shape[1] // 2
    core = core_index() if mine else 1 - core_index()
    return lax.dynamic_slice_in_dim(rows, core * half, half, 1)


def natural_rows(mine, other):
    first = core_index() == 0
    return jnp.concatenate([jnp.where(first, mine, other), jnp.where(first, other, mine)], 1)


def project(rows, weight):
    return jnp.einsum("gsd,df->gsf", rows, weight, preferred_element_type=WIDE)


def back_project(grads, weight):
    return jnp.einsum("gsf,df->gsd", grads, weight, preferred_element_type=WIDE)


def weight_grad(rows, grads):
    return jnp.einsum("gsd,gsf->df", rows, grads, preferred_element_type=WIDE)


def split_rows(cells):
    if isinstance(cells, tuple):
        return list(cells)
    return [half_rows(cells, True), half_rows(cells, False)]


def rows_weight_grad(lefts, rights):
    lefts = [part for cells in lefts for part in split_rows(cells)]
    rights = [part for cells in rights for part in split_rows(cells)]
    return weight_grad(jnp.concatenate(lefts, 1), jnp.concatenate(rights, 1))


def norm_forward(resid, gain, shift):
    mean = jnp.mean(resid, -1, keepdims=True)
    centred = resid - mean
    inverse = lax.rsqrt(jnp.mean(centred * centred, -1, keepdims=True) + 1e-05)
    normed = centred * inverse
    return (normed * gain + shift, normed, inverse)


def norm_backward(grad_out, saved, gain):
    normed, inverse = saved
    grad_normed = grad_out * gain
    grad_resid = inverse * (
        grad_normed
        - jnp.mean(grad_normed, -1, keepdims=True)
        - normed * jnp.mean(grad_normed * normed, -1, keepdims=True)
    )
    sums = jnp.stack([jnp.sum(grad_out * normed, (0, 1)), jnp.sum(grad_out, (0, 1))])
    return (grad_resid, sums)


def gelu_both(hidden):
    scaled = hidden * (0.5**0.5)
    half = 0.5 * lax.erf(scaled) + 0.5
    slope = half + hidden * jnp.exp(-(scaled * scaled)) * ((2.0 * math.pi) ** -0.5)
    return ((hidden * half).astype(LOW), slope.astype(LOW))


def passed_along(value, steps):
    count = lax.axis_size("seq")
    if steps > 0:
        pairs = [(place, place + 1) for place in range(count - 1)]
    else:
        pairs = [(place + 1, place) for place in range(count - 1)]
    return lax.ppermute(value, "seq", pairs)


def doc_index(positions, ends):
    return jnp.sum((positions[:, None] >= ends[None, :]).astype(jnp.int32), 1)


def pick(owner, values):
    match = owner[:, None] == jnp.arange(values.shape[0], dtype=jnp.int32)[None, :]
    return jnp.sum(jnp.where(match, values[None, :], 0), 1)


def pad_tables(tables):
    missing = 128 - tables.shape[-1]
    return jnp.pad(tables, ((0, 0), (0, 0), (0, missing))) if missing else tables


def sum_seq(values, turn):
    places = list(range(lax.axis_size("seq")))
    return lax.psum(tuple(values), "seq", axis_index_groups=[places[turn:] + places[:turn]])


def per_device(
    enc_input,
    dec_input,
    enc_cotan,
    dec_cotan,
    doc_lengths,
    src_padding,
    enc_qkv,
    enc_wout,
    enc_gain,
    enc_bias,
    enc_up,
    enc_down,
    post_gain,
    post_bias,
    self_qkv,
    self_rel,
    self_wout,
    self_gain,
    self_bias,
    cross_wq,
    cross_wkv,
    cross_wout,
    cross_gain,
    cross_bias,
    ffn_up,
    ffn_down,
    ffn_gain,
    ffn_bias,
):
    rows = enc_input.shape[0]
    half = rows // 2
    streams = dec_input.shape[0]
    table_width = self_rel.shape[1]
    base = lax.axis_index("seq") * rows
    total_rows = rows * lax.axis_size("seq")
    ends = jnp.cumsum(doc_lengths)
    starts = ends - doc_lengths
    key_pos = base - rows + jnp.arange(3 * rows, dtype=jnp.int32)
    key_valid = (key_pos >= 0) & (key_pos < total_rows)
    key_owner = doc_index(key_pos, ends)
    key_doc = jnp.where(key_valid, key_owner, -1)
    key_pad = (
        lax.dynamic_slice_in_dim(jnp.pad(src_padding, (rows, rows)), base, 3 * rows) == 1
    )
    key_first = key_pos == pick(key_owner, starts)
    qdoc = key_doc[rows : 2 * rows][:, None]
    enc_kdoc = jnp.where(key_pad, key_doc, -1).reshape(-1, 1, BK)
    cross_kdoc = jnp.where(key_pad | key_first, key_doc, -1).reshape(-1, 1, BK)
    self_kdoc = key_doc[: 2 * rows].reshape(-1, 1, 128)
    owners = key_owner[rows : 2 * rows]
    block_first = pick(owners[::BQ], starts) - base + rows
    block_end = pick(owners[BQ - 1 :: BQ], ends) - base + rows
    full_bounds = jnp.stack([block_first // BK, (block_end + BK - 1) // BK])
    self_bounds = block_first // 128

    order = Order()
    enter, leave = order.enter, order.leave
    enc, cross = Kept(), Kept()
    dec = [Kept() for _ in range(streams)]
    straight_rows = enc_input[None]

    def halves(att, weight):
        other = project(half_rows(att, False), weight).astype(LOW)
        mine = project(half_rows(att, True), weight)
        return mine, other

    def back_halves(grads, weight):
        other = back_project(half_rows(grads, False), weight).astype(LOW)
        mine = back_project(half_rows(grads, True), weight)
        return mine, other

    def exchange(mine, other):
        got = swap_core(other)
        yield
        mine, got = enter(mine, got)
        low = (mine + got.astype(WIDE)).astype(LOW)
        leave(low)
        low, got = swap_chip(low)
        yield
        low, got = enter(low, got)
        return low.astype(WIDE) + got.astype(WIDE)

    def close_branch(resid, mine, other, gain, shift):
        total = yield from exchange(mine, other)
        output, normed, inverse = norm_forward(resid + total, gain, shift)
        low = output.astype(LOW)
        leave(low)
        return output, low, swap_core(low), (normed, inverse)

    def open_branch(grad, saved, gain):
        grad, sums = norm_backward(grad, saved, gain)
        low = grad.astype(LOW)
        leave(low)
        return grad, low, swap_core(low), sums

    def encoder():
        (enc_rows,) = enter(enc_input)
        pair = jnp.einsum("sd,cdf->csf", enc_rows, enc_qkv[1:], preferred_element_type=WIDE).astype(LOW)
        enc.pair = pair
        enc.before = passed_along(pair, 1)
        enc.after = passed_along(pair, -1)
        enc.query = project(enc_rows[None], enc_qkv[0]).astype(LOW)
        leave(enc.query)
        yield
        query, before, after = enter(enc.query, enc.before, enc.after)
        enc.query, enc.before, enc.after = query, before, after
        att, wide, lse = full_forward(
            True, full_bounds, query, before, enc.pair, after, qdoc, enc_kdoc
        )
        enc.att, enc.wide, enc.lse = att, wide, lse
        mine, other = halves(att, enc_wout)
        leave(mine)
        resid = half_rows(straight_rows, True).astype(WIDE)
        resid, mine, got, enc.saved_att = yield from close_branch(
            resid, mine, other, enc_gain, enc_bias
        )
        yield
        mine, got = enter(mine, got)
        middle = jnp.concatenate([mine, got], 1)
        act, slope = gelu_both(project(middle, enc_up))
        enc.middle, enc.act, enc.slope = middle, act, slope
        other = project(act[:, half:], enc_down).astype(LOW)
        mine = project(act[:, :half], enc_down)
        leave(mine)
        resid, mine, got, enc.saved_ffn = yield from close_branch(
            resid, mine, other, post_gain, post_bias
        )
        yield
        mine, got = enter(mine, got)
        enc.final = natural_rows(mine, got)
        pair = jnp.einsum(
            "sd,cdf->csf", enc.final[0], cross_wkv, preferred_element_type=WIDE
        ).astype(LOW)
        leave(pair)
        cross.pair = pair
        cross.before = passed_along(pair, 1)
        cross.after = passed_along(pair, -1)
        yield
        parts = enter(*[dec[stream].cross_parts for stream in range(streams)])
        to_before = sum(part[0].astype(WIDE) for part in parts).astype(LOW)
        to_after = sum(part[2].astype(WIDE) for part in parts).astype(LOW)
        here = sum(part[1] for part in parts)
        leave(to_after)
        from_next = passed_along(to_before, -1)
        from_last = passed_along(to_after, 1)
        yield
        here, from_next, from_last = enter(here, from_next, from_last)
        pair_grad = (here + from_next.astype(WIDE) + from_last.astype(WIDE)).astype(LOW)
        cross.pair_grad = pair_grad
        extra = jnp.einsum("csf,cdf->sd", pair_grad, cross_wkv, preferred_element_type=WIDE)[None]
        mine, other = half_rows(extra, True), half_rows(extra, False).astype(LOW)
        leave(other)
        total = yield from exchange(mine, other)
        grad = half_rows(enc_cotan[None], True).astype(WIDE) + total
        grad, mine, got, enc.post_sums = open_branch(grad, enc.saved_ffn, post_gain)
        yield
        mine, got = enter(mine, got)
        ffn_rows = jnp.concatenate([mine, got], 1)
        grad_act = jnp.einsum("gsd,fd->gsf", ffn_rows, enc_down, preferred_element_type=WIDE)
        hidden_grad = (grad_act * enc.slope.astype(WIDE)).astype(LOW)
        enc.ffn_rows, enc.hidden_grad = ffn_rows, hidden_grad
        other = back_project(hidden_grad[:, half:], enc_up).astype(LOW)
        mine = back_project(hidden_grad[:, :half], enc_up)
        leave(mine)
        total = yield from exchange(mine, other)
        grad, mine, got, enc.att_sums = open_branch(grad + total, enc.saved_att, enc_gain)
        yield
        mine, got = enter(mine, got)
        enc.att_rows = (mine, got)
        query_grad, to_before, here, to_after = full_backward(
            True,
            full_bounds,
            enc.query,
            att_grad(mine, got, enc_wout),
            enc.wide,
            enc.lse,
            enc.before,
            enc.pair,
            enc.after,
            qdoc,
            enc_kdoc,
        )
        leave(query_grad)
        from_next = passed_along(to_before, -1)
        from_last = passed_along(to_after, 1)
        yield
        here, from_next, from_last = enter(here, from_next, from_last)
        pair_grad = (here + from_next.astype(WIDE) + from_last.astype(WIDE)).astype(LOW)
        enc.query_grad, enc.pair_grad = query_grad, pair_grad
        partial_value = back_project(query_grad, enc_qkv[0]) + jnp.einsum(
            "csf,cdf->sd", pair_grad, enc_qkv[1:], preferred_element_type=WIDE
        )
        mine, other = half_rows(partial_value, True), half_rows(partial_value, False).astype(LOW)
        leave(other)
        total = yield from exchange(mine, other)
        low = (grad + total).astype(LOW)
        leave(low)
        got = swap_core(low)
        yield
        low, got = enter(low, got)
        enc.grad = natural_rows(low, got)[0]
        leave(enc.grad)
        yield

    def att_grad(mine, other, weight):
        return natural_rows(
            jnp.einsum("gsd,fd->gsf", mine, weight, preferred_element_type=WIDE).astype(LOW),
            jnp.einsum("gsd,fd->gsf", other, weight, preferred_element_type=WIDE).astype(LOW),
        )

    def decoder(stream):
        own = stream > 0
        kept = dec[stream]
        (dec_rows,) = enter(dec_input[stream : stream + 1])
        pair = jnp.einsum(
            "gsd,cdf->gcsf", dec_rows, self_qkv[1:], preferred_element_type=WIDE
        ).astype(LOW)
        query = project(dec_rows, self_qkv[0]).astype(LOW)
        table = pad_tables(project(dec_rows, self_rel))
        leave((pair, query, table))
        if stream == 0:
            cross.main = pair[0]
            cross.main_before = passed_along(pair[0], 1)
        yield
        main = cross.main
        query, main_before = enter(query, cross.main_before)
        cross.main_before = main_before
        own_pair = pair if own else None
        att, wide, lse = causal_forward(
            own, self_bounds, query, main_before, main, qdoc, self_kdoc, table, own_pair
        )
        kept.self_att = att
        mine, other = halves(att, self_wout)
        leave(mine)
        resid, mine, got, saved_self = yield from close_branch(
            half_rows(dec_rows, True).astype(WIDE), mine, other, self_gain, self_bias
        )
        yield
        mine, got = enter(mine, got)
        kept.first = (mine, got)
        cross_query = natural_rows(
            project(mine, cross_wq).astype(LOW), project(got, cross_wq).astype(LOW)
        )
        leave(cross_query)
        yield
        cross_query, before, after = enter(cross_query, cross.before, cross.after)
        cross.before, cross.after = before, after
        cross_att, cross_wide, cross_lse = full_forward(
            False, full_bounds, cross_query, before, cross.pair, after, qdoc, cross_kdoc
        )
        kept.cross_att = cross_att
        mine, other = halves(cross_att, cross_wout)
        leave(mine)
        resid, mine, got, saved_cross = yield from close_branch(
            resid, mine, other, cross_gain, cross_bias
        )
        yield
        mine, got = enter(mine, got)
        second = jnp.concatenate([mine, got], 1)
        act, slope = gelu_both(project(second, ffn_up))
        kept.second, kept.act = second, act
        other = project(act[:, half:], ffn_down).astype(LOW)
        mine = project(act[:, :half], ffn_down)
        leave(mine)
        total = yield from exchange(mine, other)
        output, normed, inverse = norm_forward(resid + total, ffn_gain, ffn_bias)
        final_mine = output.astype(LOW)
        final_got = swap_core(final_mine)
        grad = half_rows(dec_cotan[stream : stream + 1], True).astype(WIDE)
        grad, mine, got, kept.ffn_sums = open_branch(grad, (normed, inverse), ffn_gain)
        yield
        mine, got = enter(mine, got)
        ffn_rows = jnp.concatenate([mine, got], 1)
        grad_act = jnp.einsum("gsd,fd->gsf", ffn_rows, ffn_down, preferred_element_type=WIDE)
        hidden_grad = (grad_act * slope.astype(WIDE)).astype(LOW)
        kept.ffn_rows, kept.hidden_grad = ffn_rows, hidden_grad
        other = back_project(hidden_grad[:, half:], ffn_up).astype(LOW)
        mine = back_project(hidden_grad[:, :half], ffn_up)
        leave(mine)
        total = yield from exchange(mine, other)
        grad, mine, got, kept.cross_sums = open_branch(grad + total, saved_cross, cross_gain)
        kept.final = natural_rows(final_mine, final_got)
        yield
        mine, got = enter(mine, got)
        kept.cross_rows = (mine, got)
        query_grad, *kept.cross_parts = full_backward(
            False,
            full_bounds,
            cross_query,
            att_grad(mine, got, cross_wout),
            cross_wide,
            cross_lse,
            cross.before,
            cross.pair,
            cross.after,
            qdoc,
            cross_kdoc,
        )
        kept.cross_query_grad = query_grad
        mine, other = back_halves(query_grad, cross_wq)
        leave(mine)
        total = yield from exchange(mine, other)
        grad, mine, got, kept.self_sums = open_branch(grad + total, saved_self, self_gain)
        yield
        mine, got = enter(mine, got)
        kept.self_rows = (mine, got)
        query_grad, table_grad, to_before, here, *own_grad = causal_backward(
            own,
            self_bounds,
            query,
            att_grad(mine, got, self_wout),
            wide,
            lse,
            main_before,
            main,
            qdoc,
            self_kdoc,
            table,
            own_pair,
        )
        table_grad = table_grad[:, :, :table_width]
        kept.table_grad = table_grad
        kept.self_parts = (to_before, here)
        leave(query_grad)
        if own:
            pair_grad = own_grad[0][0]
        else:
            yield
            parts = enter(*[dec[item].self_parts for item in range(streams)])
            to_before = sum(part[0].astype(WIDE) for part in parts).astype(LOW)
            here = sum(part[1] for part in parts)
            leave(to_before)
            from_next = passed_along(to_before, -1)
            yield
            here, from_next = enter(here, from_next)
            pair_grad = (here + from_next.astype(WIDE)).astype(LOW)
        kept.query_grad, kept.pair_grad = query_grad, pair_grad
        partial_value = (
            back_project(query_grad, self_qkv[0])
            + jnp.einsum("csf,cdf->sd", pair_grad, self_qkv[1:], preferred_element_type=WIDE)
            + back_project(table_grad, self_rel)
        )
        mine, other = half_rows(partial_value, True), half_rows(partial_value, False).astype(LOW)
        leave(other)
        total = yield from exchange(mine, other)
        low = (grad + total).astype(LOW)
        leave(low)
        got = swap_core(low)
        yield
        low, got = enter(low, got)
        kept.grad = natural_rows(low, got)
        leave(kept.grad)
        yield

    weights = Kept()

    def ffn_weights():
        acts, grads = enter([kept.act for kept in dec], [kept.ffn_rows for kept in dec])
        down = weight_grad(jnp.concatenate(acts), jnp.concatenate(grads)).astype(LOW)
        seconds, grads = [kept.second for kept in dec], [kept.hidden_grad for kept in dec]
        up = weight_grad(jnp.concatenate(seconds), jnp.concatenate(grads)).astype(LOW)
        leave((down, up))
        weights.ffn = sum_seq((down, up), 0)
        yield

    def cross_weights():
        atts, grads = enter([kept.cross_att for kept in dec], [kept.cross_rows for kept in dec])
        wout = rows_weight_grad(atts, grads).astype(LOW)
        firsts = [kept.first for kept in dec]
        wq = rows_weight_grad(firsts, [kept.cross_query_grad for kept in dec]).astype(LOW)
        leave((wout, wq))
        weights.cross = (wout, wq)
        yield
        (final,) = enter(enc.final)
        wkv = jnp.einsum(
            "sd,csf->cdf", final[0], cross.pair_grad, preferred_element_type=WIDE
        ).astype(LOW)
        leave(wkv)
        weights.cross = sum_seq(weights.cross + (wkv,), 1)
        yield

    def enc_ffn_weights():
        act, grads = enter(enc.act, enc.ffn_rows)
        down = weight_grad(act, grads).astype(LOW)
        up = weight_grad(enc.middle, enc.hidden_grad).astype(LOW)
        leave((down, up))
        weights.enc = [down, up]
        yield

    def flat(cells):
        if cells.shape[-1] % SUM_WIDTH:
            cells = jnp.swapaxes(cells, -1, -2)
        return cells.reshape(-1, cells.shape[-1])

    def unflat(cells, shape):
        if shape[-1] % SUM_WIDTH:
            return jnp.swapaxes(cells.reshape(shape[:-2] + (shape[-1], shape[-2])), -1, -2)
        return cells.reshape(shape)

    def self_weights():
        atts, grads = enter([kept.self_att for kept in dec], [kept.self_rows for kept in dec])
        wout = rows_weight_grad(atts, grads).astype(LOW)
        tables = jnp.concatenate([kept.table_grad for kept in dec], 0)
        rel = weight_grad(dec_input, tables).astype(LOW)
        queries = jnp.concatenate([kept.query_grad for kept in dec])
        query = weight_grad(dec_input, queries).astype(LOW)
        sides = [jnp.stack([kept.pair_grad[side] for kept in dec]) for side in range(2)]
        key, value = [weight_grad(dec_input, side).astype(LOW) for side in sides]
        leave((wout, rel, query, key, value))
        weights.self = [wout, rel, query, key, value]
        yield

    def finished():
        (finals,) = enter([kept.final for kept in dec])
        weights.final = jnp.concatenate(finals, 0)
        leave(weights.final)
        yield

    def enc_weights():
        query_grad, pair_grad, grads = enter(enc.query_grad, enc.pair_grad, enc.att_rows)
        query = weight_grad(straight_rows, query_grad).astype(LOW)
        key = weight_grad(straight_rows, pair_grad[:1]).astype(LOW)
        value = weight_grad(straight_rows, pair_grad[1:]).astype(LOW)
        wout = rows_weight_grad([enc.att], [grads]).astype(LOW)
        sums = jnp.concatenate(
            [
                enc.att_sums,
                enc.post_sums,
                sum(kept.self_sums for kept in dec),
                sum(kept.cross_sums for kept in dec),
                sum(kept.ffn_sums for kept in dec),
            ],
            0,
        )
        sums = sums + swap_core(sums)
        sums = jnp.pad(sums, ((0, -sums.shape[0] % 16), (0, 0))).astype(LOW)
        parts = weights.enc + weights.self + [wout, query, key, value, sums]
        pieces = [flat(part) for part in parts]
        leave((wout, query, key, value, sums))
        yield
        pieces = enter(*pieces)
        summed = link_sum(pieces, lax.axis_size("seq"))
        leave(summed[0])
        weights.ffn, weights.cross = enter(weights.ffn, weights.cross)
        weights.last = [
            unflat(cells.astype(WIDE), part.shape) for cells, part in zip(summed, parts)
        ]
        yield

    tasks = {"e": encoder(), "F": ffn_weights(), "C": cross_weights()}
    tasks.update({"D": finished(), "G": enc_ffn_weights(), "S": self_weights(), "W": enc_weights()})
    tasks.update({str(stream): decoder(stream) for stream in range(streams)})
    for item in "".join(PLAN):
        next(tasks[item], None)
    for task in tasks.values():
        for _ in task:
            pass

    ffn_down_grad, ffn_up_grad = [value.astype(WIDE) for value in weights.ffn]
    cross_wout_grad, cross_wq_grad, cross_wkv_grad = [
        value.astype(WIDE) for value in weights.cross
    ]
    enc_down_grad, enc_up_grad, *found = weights.last
    self_wout_grad, self_rel_grad, *found = found
    self_qkv_grad = jnp.stack(found[:3])
    enc_wout_grad, sums = found[3], found[7]
    enc_qkv_grad = jnp.stack(found[4:7])
    return (
        enc.final[0],
        weights.final,
        enc.grad,
        jnp.concatenate([kept.grad for kept in dec], 0),
        enc_qkv_grad,
        enc_wout_grad,
        sums[0],
        sums[1],
        enc_up_grad,
        enc_down_grad,
        sums[2],
        sums[3],
        self_qkv_grad,
        self_rel_grad,
        self_wout_grad,
        sums[4],
        sums[5],
        cross_wq_grad,
        cross_wkv_grad,
        cross_wout_grad,
        sums[6],
        sums[7],
        ffn_up_grad,
        ffn_down_grad,
        sums[8],
        sums[9],
    )


def solution(mesh):
    in_specs = (
        P("seq", None),
        P(None, "seq", None),
        P("seq", None),
        P(None, "seq", None),
        P(),
        P(),
        P(None, None, "tp"),
        P("tp", None),
        P(),
        P(),
        P(None, "tp"),
        P("tp", None),
        P(),
        P(),
        P(None, None, "tp"),
        P(None, "tp"),
        P("tp", None),
        P(),
        P(),
        P(None, "tp"),
        P(None, None, "tp"),
        P("tp", None),
        P(),
        P(),
        P(None, "tp"),
        P("tp", None),
        P(),
        P(),
    )
    out_specs = (
        P("seq", None),
        P(None, "seq", None),
        P("seq", None),
        P(None, "seq", None),
        P(None, None, "tp"),
        P("tp", None),
        P(),
        P(),
        P(None, "tp"),
        P("tp", None),
        P(),
        P(),
        P(None, None, "tp"),
        P(None, "tp"),
        P("tp", None),
        P(),
        P(),
        P(None, "tp"),
        P(None, None, "tp"),
        P("tp", None),
        P(),
        P(),
        P(None, "tp"),
        P("tp", None),
        P(),
        P(),
    )
    return jax.shard_map(
        per_device, mesh=mesh, in_specs=in_specs, out_specs=out_specs, check_vma=False
    )
```

```python
import functools
import math

import jax
import jax.numpy as jnp
import numpy as np
from jax import lax
from jax.experimental import pallas as pl
from jax.experimental.pallas import tpu as pltpu
from jax.sharding import PartitionSpec as P

HD = 64
BUCKETS = 32
DOC_MAX = 512
PAIR = 2 * HD
BQ = 128
BK = 256
NEG = -1e30
VMEM_BYTES = 40 * 1024 * 1024

LOW = jnp.bfloat16
WIDE = jnp.float32


def bucket_bounds():
    exact = BUCKETS // 2
    bounds = []
    for level in range(1, BUCKETS):
        if level < exact:
            bounds.append(level)
        else:
            bounds.append(int(math.ceil(exact * (128.0 / exact) ** ((level - exact) / exact))))
    return bounds


def bucket_table(offsets):
    return sum((offsets >= bound).astype(np.int32) for bound in bucket_bounds())


def dot_nt(left, right):
    return lax.dot_general(left, right, (((1,), (1,)), ((), ())), preferred_element_type=WIDE)


def dot_nn(left, right):
    return lax.dot_general(left, right, (((1,), (0,)), ((), ())), preferred_element_type=WIDE)


def stack_heads(cells):
    lane = lax.broadcasted_iota(jnp.int32, cells.shape, 1)
    wide = cells.astype(WIDE)
    first = jnp.where(lane < HD, wide, 0.0)
    return jnp.concatenate([first, wide - first], 0)


def merge_heads(cells):
    half = cells.shape[0] // 2
    lane = lax.broadcasted_iota(jnp.int32, (half, cells.shape[1]), 1)
    return jnp.where(lane < HD, cells[:half], cells[half:])


def both_heads(mask, cells):
    return jnp.where(mask[None], cells.reshape(2, BQ, cells.shape[1]), NEG).reshape(cells.shape)


def pair_columns(cells, pair):
    return jnp.concatenate([cells[:, 2 * pair : 2 * pair + 1], cells[:, 2 * pair + 1 : 2 * pair + 2]], 0)


def put_columns(store, pair, column):
    lane = lax.broadcasted_iota(jnp.int32, store.shape, 1)
    store = jnp.where(lane == 2 * pair, column[:BQ], store)
    return jnp.where(lane == 2 * pair + 1, column[BQ:], store)


def fill_window(window, parts):
    rows = parts[0].shape[1]
    for place, part in enumerate(parts):
        window[:, place * rows : (place + 1) * rows, :] = part[...]


def full_mask(with_self, qdoc, kdoc_ref, block, query_at):
    allowed = qdoc == kdoc_ref[block]
    if with_self:
        row = lax.broadcasted_iota(jnp.int32, allowed.shape, 0) + query_at
        column = lax.broadcasted_iota(jnp.int32, allowed.shape, 1) + block * BK
        allowed = allowed | (row == column)
    return allowed


def full_forward_kernel(
    with_self,
    bounds_ref,
    q_ref,
    before_ref,
    here_ref,
    after_ref,
    qdoc_ref,
    kdoc_ref,
    att_ref,
    wide_ref,
    lse_ref,
    window,
    scores,
    top,
    total,
    gathered,
):
    stream, step = pl.program_id(0), pl.program_id(1)
    rows = here_ref.shape[1]
    pairs = here_ref.shape[2] // PAIR

    @pl.when((stream == 0) & (step == 0))
    def _():
        fill_window(window, (before_ref, here_ref, after_ref))

    low_block, high_block = bounds_ref[0, step], bounds_ref[1, step]
    qdoc = qdoc_ref[...]
    queries = [
        (stack_heads(q_ref[:, pair * PAIR : (pair + 1) * PAIR]) * HD**-0.5).astype(LOW)
        for pair in range(pairs)
    ]
    top[...] = jnp.full(top.shape, NEG, WIDE)
    total[...] = jnp.zeros(total.shape, WIDE)
    gathered[...] = jnp.zeros(gathered.shape, WIDE)

    def score_step(block, carry):
        allowed = full_mask(with_self, qdoc, kdoc_ref, block, rows + step * BQ)
        at = pl.ds(pl.multiple_of(block * BK, BK), BK)
        for pair in range(pairs):
            keys = window[0, at, pair * PAIR : (pair + 1) * PAIR]
            found = both_heads(allowed, dot_nt(queries[pair], keys))
            scores[block, pair] = found
            top[pair] = jnp.maximum(top[pair], jnp.maximum(found[:, :128], found[:, 128:]))
        return carry

    lax.fori_loop(low_block, high_block, score_step, 0)
    peaks = [jnp.max(top[pair], 1, keepdims=True) for pair in range(pairs)]

    def value_step(block, carry):
        at = pl.ds(pl.multiple_of(block * BK, BK), BK)
        for pair in range(pairs):
            values = window[1, at, pair * PAIR : (pair + 1) * PAIR]
            weights = jnp.exp(scores[block, pair] - peaks[pair])
            total[pair] += weights[:, :128] + weights[:, 128:]
            gathered[pair] += dot_nn(weights.astype(LOW), values)
        return carry

    lax.fori_loop(low_block, high_block, value_step, 0)
    lse = jnp.zeros((BQ, 128), WIDE)
    for pair in range(pairs):
        weight = jnp.sum(total[pair], 1, keepdims=True)
        result = merge_heads(gathered[pair] / weight)
        att_ref[:, pair * PAIR : (pair + 1) * PAIR] = result.astype(LOW)
        wide_ref[:, pair * PAIR : (pair + 1) * PAIR] = result
        lse = put_columns(lse, pair, peaks[pair] + jnp.log(weight))
    lse_ref[...] = lse


def full_backward_kernel(
    with_self,
    bounds_ref,
    q_ref,
    grad_ref,
    att_ref,
    lse_ref,
    before_ref,
    here_ref,
    after_ref,
    qdoc_ref,
    kdoc_ref,
    qgrad_ref,
    gbefore_ref,
    ghere_ref,
    gafter_ref,
    window,
    wgrad,
    qgrad,
):
    stream, step = pl.program_id(0), pl.program_id(1)
    rows = here_ref.shape[1]
    pairs = here_ref.shape[2] // PAIR

    @pl.when((stream == 0) & (step == 0))
    def _():
        fill_window(window, (before_ref, here_ref, after_ref))
        wgrad[...] = jnp.zeros(wgrad.shape, WIDE)

    low_block, high_block = bounds_ref[0, step], bounds_ref[1, step]
    qdoc = qdoc_ref[...]
    lse_all = lse_ref[...]
    queries, grads, queries_t, grads_t, deltas, logs = [], [], [], [], [], []
    for pair in range(pairs):
        cut = slice(pair * PAIR, (pair + 1) * PAIR)
        query = stack_heads(q_ref[:, cut]) * HD**-0.5
        grad = stack_heads(grad_ref[:, cut])
        att = att_ref[:, cut]
        deltas.append(jnp.sum(grad * jnp.concatenate([att, att], 0), 1, keepdims=True))
        logs.append(pair_columns(lse_all, pair))
        queries.append(query.astype(LOW))
        grads.append(grad.astype(LOW))
        queries_t.append(query.T.astype(LOW))
        grads_t.append(grad.T.astype(LOW))
    qgrad[...] = jnp.zeros(qgrad.shape, WIDE)

    def block_step(block, carry):
        allowed = full_mask(with_self, qdoc, kdoc_ref, block, rows + step * BQ)
        at = pl.ds(pl.multiple_of(block * BK, BK), BK)
        for pair in range(pairs):
            cut = slice(pair * PAIR, (pair + 1) * PAIR)
            keys = window[0, at, cut]
            values = window[1, at, cut]
            probs = jnp.exp(both_heads(allowed, dot_nt(queries[pair], keys)) - logs[pair])
            slopes = probs * (dot_nt(grads[pair], values) - deltas[pair])
            slopes = slopes.astype(LOW)
            qgrad[pair] += dot_nn(slopes, keys)
            wgrad[0, cut, at] += dot_nn(queries_t[pair], slopes)
            wgrad[1, cut, at] += dot_nn(grads_t[pair], probs.astype(LOW))
        return carry

    lax.fori_loop(low_block, high_block, block_step, 0)
    for pair in range(pairs):
        qgrad_ref[:, pair * PAIR : (pair + 1) * PAIR] = (
            merge_heads(qgrad[pair]) * HD**-0.5
        ).astype(LOW)

    @pl.when((stream == pl.num_programs(0) - 1) & (step == pl.num_programs(1) - 1))
    def _():
        for side in range(2):
            gbefore_ref[side] = wgrad[side, :, :rows].T.astype(LOW)
            ghere_ref[side] = wgrad[side, :, rows : 2 * rows].T
            gafter_ref[side] = wgrad[side, :, 2 * rows :].T.astype(LOW)


def causal_parts(own, table, gidx, pair):
    lane = lax.broadcasted_iota(jnp.int32, (BQ, 128), 1)
    row = lax.broadcasted_iota(jnp.int32, (BQ, 128), 0)
    near, far = [], []
    for head in (2 * pair, 2 * pair + 1):
        spread = jnp.take_along_axis(
            table, gidx + head * BUCKETS, axis=1, mode="promise_in_bounds"
        )
        last = table[:, head * BUCKETS + BUCKETS - 1 : head * BUCKETS + BUCKETS]
        near.append((jnp.where(lane > row, spread, last), spread))
        far.append(last)
    bias_before = jnp.concatenate([near[0][0], near[1][0]], 0)
    bias_here = jnp.concatenate([near[0][1], near[1][1]], 0)
    return bias_before, bias_here, jnp.concatenate(far, 0)


def own_column(table, pair):
    first, second = 2 * pair * BUCKETS, (2 * pair + 1) * BUCKETS
    return jnp.concatenate([table[:, first : first + 1], table[:, second : second + 1]], 0)


def causal_masks(own, qdoc, kdoc_ref, near):
    lane = lax.broadcasted_iota(jnp.int32, (BQ, 128), 1)
    row = lax.broadcasted_iota(jnp.int32, (BQ, 128), 0)
    earlier = (lane < row) if own else (lane <= row)
    return qdoc == kdoc_ref[near - 1], (qdoc == kdoc_ref[near]) & earlier


def causal_forward_kernel(own, *refs):
    bounds_ref, q_ref, before_ref, here_ref, qdoc_ref, kdoc_ref, table_ref, gidx_ref = refs[:8]
    refs = refs[8:]
    if own:
        own_ref, refs = refs[0], refs[1:]
    att_ref, wide_ref, lse_ref, window, scores, top, total, gathered = refs
    stream, step = pl.program_id(0), pl.program_id(1)
    rows = here_ref.shape[1]
    pairs = here_ref.shape[2] // PAIR

    @pl.when((stream == 0) & (step == 0))
    def _():
        fill_window(window, (before_ref, here_ref))

    near = rows // 128 + step
    low_block = bounds_ref[step]
    qdoc = qdoc_ref[...]
    table = table_ref[...]
    gidx = gidx_ref[...]
    queries, fars, peaks, owns = [], [], [], []
    mask_before, mask_here = causal_masks(own, qdoc, kdoc_ref, near)
    near_at = pl.ds(pl.multiple_of((near - 1) * 128, 128), 256)
    for pair in range(pairs):
        cut = slice(pair * PAIR, (pair + 1) * PAIR)
        query = stack_heads(q_ref[:, cut]) * HD**-0.5
        queries.append(query.astype(LOW))
        bias_before, bias_here, far = causal_parts(own, table, gidx, pair)
        fars.append(far)
        found = dot_nt(queries[pair], window[0, near_at, cut])
        found_before = both_heads(mask_before, found[:, :128] + bias_before)
        found_here = both_heads(mask_here, found[:, 128:] + bias_here)
        scores[near - 1, pair] = found_before
        scores[near, pair] = found_here
        top[pair] = jnp.maximum(found_before, found_here)
        if own:
            keys = own_ref[0, :, cut].astype(WIDE)
            owns.append(
                jnp.sum(query * jnp.concatenate([keys, keys], 0), 1, keepdims=True)
                + own_column(table, pair)
            )

    def score_step(block, carry):
        allowed = qdoc == kdoc_ref[block]
        at = pl.ds(pl.multiple_of(block * 128, 128), 128)
        for pair in range(pairs):
            keys = window[0, at, pair * PAIR : (pair + 1) * PAIR]
            found = both_heads(allowed, dot_nt(queries[pair], keys) + fars[pair])
            scores[block, pair] = found
            top[pair] = jnp.maximum(top[pair], found)
        return carry

    lax.fori_loop(low_block, near - 1, score_step, 0)
    for pair in range(pairs):
        cut = slice(pair * PAIR, (pair + 1) * PAIR)
        peak = jnp.max(top[pair], 1, keepdims=True)
        if own:
            peak = jnp.maximum(peak, owns[pair])
        peaks.append(peak)
        weights_before = jnp.exp(scores[near - 1, pair] - peak)
        weights_here = jnp.exp(scores[near, pair] - peak)
        total[pair] = weights_before + weights_here
        weights = jnp.concatenate([weights_before, weights_here], 1).astype(LOW)
        gathered[pair] = dot_nn(weights, window[1, near_at, cut])

    def value_step(block, carry):
        at = pl.ds(pl.multiple_of(block * 128, 128), 128)
        for pair in range(pairs):
            values = window[1, at, pair * PAIR : (pair + 1) * PAIR]
            weights = jnp.exp(scores[block, pair] - peaks[pair])
            total[pair] += weights
            gathered[pair] += dot_nn(weights.astype(LOW), values)
        return carry

    lax.fori_loop(low_block, near - 1, value_step, 0)
    lse = jnp.zeros((BQ, 128), WIDE)
    for pair in range(pairs):
        cut = slice(pair * PAIR, (pair + 1) * PAIR)
        weight = jnp.sum(total[pair], 1, keepdims=True)
        result = gathered[pair]
        if own:
            own_weight = jnp.exp(owns[pair] - peaks[pair])
            weight = weight + own_weight
            values = own_ref[1, :, cut].astype(WIDE)
            result = result + own_weight * jnp.concatenate([values, values], 0)
        result = merge_heads(result / weight)
        att_ref[:, cut] = result.astype(LOW)
        wide_ref[:, cut] = result
        lse = put_columns(lse, pair, peaks[pair] + jnp.log(weight))
    lse_ref[...] = lse


def causal_backward_kernel(own, *refs):
    bounds_ref, q_ref, grad_ref, att_ref, lse_ref, before_ref, here_ref = refs[:7]
    qdoc_ref, kdoc_ref, table_ref, gidx_ref, sidx_ref, hot_ref = refs[7:13]
    refs = refs[13:]
    if own:
        own_ref, refs = refs[0], refs[1:]
    qgrad_ref, tgrad_ref, gbefore_ref, ghere_ref = refs[:4]
    refs = refs[4:]
    if own:
        ograd_ref, refs = refs[0], refs[1:]
    window, wgrad, qgrad, farsum = refs
    stream, step = pl.program_id(0), pl.program_id(1)
    rows = here_ref.shape[1]
    pairs = here_ref.shape[2] // PAIR

    @pl.when((stream == 0) & (step == 0))
    def _():
        fill_window(window, (before_ref, here_ref))
        wgrad[...] = jnp.zeros(wgrad.shape, WIDE)

    near = rows // 128 + step
    low_block = bounds_ref[step]
    qdoc = qdoc_ref[...]
    table = table_ref[...]
    gidx = gidx_ref[...]
    sidx = sidx_ref[...]
    lse_all = lse_ref[...]
    lane = lax.broadcasted_iota(jnp.int32, (BQ, 128), 1)
    row = lax.broadcasted_iota(jnp.int32, (BQ, 128), 0)
    mask_before, mask_here = causal_masks(own, qdoc, kdoc_ref, near)
    near_at = pl.ds(pl.multiple_of((near - 1) * 128, 128), 256)
    queries, grads, queries_t, grads_t, deltas, logs, fars = [], [], [], [], [], [], []
    tgrad = jnp.zeros((BQ, 128), WIDE)
    for pair in range(pairs):
        cut = slice(pair * PAIR, (pair + 1) * PAIR)
        query = stack_heads(q_ref[:, cut]) * HD**-0.5
        grad = stack_heads(grad_ref[:, cut])
        att = att_ref[:, cut]
        delta = jnp.sum(grad * jnp.concatenate([att, att], 0), 1, keepdims=True)
        log_total = pair_columns(lse_all, pair)
        deltas.append(delta)
        logs.append(log_total)
        queries.append(query.astype(LOW))
        grads.append(grad.astype(LOW))
        queries_t.append(query.T.astype(LOW))
        grads_t.append(grad.T.astype(LOW))
        bias_before, bias_here, far = causal_parts(own, table, gidx, pair)
        fars.append(far)
        keys = window[0, near_at, cut]
        values = window[1, near_at, cut]
        found = dot_nt(queries[pair], keys)
        found_before = both_heads(mask_before, found[:, :128] + bias_before)
        found_here = both_heads(mask_here, found[:, 128:] + bias_here)
        probs = jnp.exp(jnp.concatenate([found_before, found_here], 1) - log_total)
        slopes = probs * (dot_nt(grads[pair], values) - delta)
        slopes_low = slopes.astype(LOW)
        qgrad[pair] = dot_nn(slopes_low, keys)
        wgrad[0, cut, near_at] += dot_nn(queries_t[pair], slopes_low)
        wgrad[1, cut, near_at] += dot_nn(grads_t[pair], probs.astype(LOW))
        rest = []
        for side in range(2):
            part_before = slopes[side * BQ : (side + 1) * BQ, :128]
            part_here = slopes[side * BQ : (side + 1) * BQ, 128:]
            merged = jnp.where(lane <= row, part_here, part_before)
            skewed = jnp.take_along_axis(merged, sidx, axis=1, mode="promise_in_bounds")
            tgrad = tgrad + dot_nn(skewed.astype(LOW), hot_ref[2 * pair + side])
            rest.append(jnp.where(lane <= row, part_before, 0.0))
        farsum[pair] = jnp.concatenate(rest, 0)
        if own:
            own_keys = own_ref[0, :, cut].astype(WIDE)
            own_values = own_ref[1, :, cut].astype(WIDE)
            own_keys = jnp.concatenate([own_keys, own_keys], 0)
            own_values = jnp.concatenate([own_values, own_values], 0)
            own_score = jnp.sum(query * own_keys, 1, keepdims=True) + own_column(table, pair)
            own_prob = jnp.exp(own_score - log_total)
            own_slope = own_prob * (jnp.sum(grad * own_values, 1, keepdims=True) - delta)
            qgrad[pair] += own_slope * own_keys
            key_part = own_slope * query
            value_part = own_prob * grad
            ograd_ref[0, :, cut] = (key_part[:BQ] + key_part[BQ:]).astype(LOW)
            ograd_ref[1, :, cut] = (value_part[:BQ] + value_part[BQ:]).astype(LOW)
            for side in range(2):
                place = (2 * pair + side) * BUCKETS
                tgrad = tgrad + jnp.where(lane == place, own_slope[side * BQ : (side + 1) * BQ], 0.0)

    def block_step(block, carry):
        allowed = qdoc == kdoc_ref[block]
        at = pl.ds(pl.multiple_of(block * 128, 128), 128)
        for pair in range(pairs):
            cut = slice(pair * PAIR, (pair + 1) * PAIR)
            keys = window[0, at, cut]
            values = window[1, at, cut]
            found = both_heads(allowed, dot_nt(queries[pair], keys) + fars[pair])
            probs = jnp.exp(found - logs[pair])
            slopes = probs * (dot_nt(grads[pair], values) - deltas[pair])
            farsum[pair] += slopes
            slopes = slopes.astype(LOW)
            qgrad[pair] += dot_nn(slopes, keys)
            wgrad[0, cut, at] += dot_nn(queries_t[pair], slopes)
            wgrad[1, cut, at] += dot_nn(grads_t[pair], probs.astype(LOW))
        return carry

    lax.fori_loop(low_block, near - 1, block_step, 0)
    for pair in range(pairs):
        qgrad_ref[:, pair * PAIR : (pair + 1) * PAIR] = (
            merge_heads(qgrad[pair]) * HD**-0.5
        ).astype(LOW)
        rest = jnp.sum(farsum[pair], 1, keepdims=True)
        for side in range(2):
            place = (2 * pair + side) * BUCKETS + BUCKETS - 1
            tgrad = tgrad + jnp.where(lane == place, rest[side * BQ : (side + 1) * BQ], 0.0)
    tgrad_ref[...] = tgrad.astype(LOW)

    @pl.when((stream == pl.num_programs(0) - 1) & (step == pl.num_programs(1) - 1))
    def _():
        for side in range(2):
            gbefore_ref[side] = wgrad[side, :, :rows].T.astype(LOW)
            ghere_ref[side] = wgrad[side, :, rows:].T


def whole_spec(shape):
    return pl.BlockSpec(shape, lambda stream, step, bounds: (0,) * len(shape))


def rows_spec(width):
    return pl.BlockSpec((None, BQ, width), lambda stream, step, bounds: (stream, step, 0))


def pair_rows_spec(width):
    return pl.BlockSpec((None, 2, BQ, width), lambda stream, step, bounds: (stream, 0, step, 0))


QDOC_SPEC = pl.BlockSpec((BQ, 1), lambda stream, step, bounds: (step, 0))


def shaped(shape, dtype):
    return jax.ShapeDtypeStruct(shape, dtype)


def local_call(kernel, grid, in_specs, out_specs, out_shape, scratch, cost):
    return pl.pallas_call(
        kernel,
        grid_spec=pltpu.PrefetchScalarGridSpec(
            num_scalar_prefetch=1,
            grid=grid,
            in_specs=in_specs,
            out_specs=out_specs,
            scratch_shapes=scratch,
        ),
        out_shape=out_shape,
        compiler_params=pltpu.CompilerParams(
            vmem_limit_bytes=VMEM_BYTES, dimension_semantics=("arbitrary", "arbitrary")
        ),
        cost_estimate=pl.CostEstimate(
            flops=int(cost), bytes_accessed=int(cost), transcendentals=0
        ),
    )


def full_forward(with_self, bounds, queries, before, here, after, qdoc, kdoc):
    streams, rows, width = queries.shape
    pairs = width // PAIR
    blocks = 3 * rows // BK
    kv_spec = whole_spec((2, rows, width))
    return local_call(
        functools.partial(full_forward_kernel, with_self),
        (streams, rows // BQ),
        [rows_spec(width), kv_spec, kv_spec, kv_spec, QDOC_SPEC, whole_spec((blocks, 1, BK))],
        [rows_spec(width), rows_spec(width), rows_spec(128)],
        [
            shaped((streams, rows, width), LOW),
            shaped((streams, rows, width), WIDE),
            shaped((streams, rows, 128), WIDE),
        ],
        [
            pltpu.VMEM((2, 3 * rows, width), LOW),
            pltpu.VMEM((blocks, pairs, 2 * BQ, BK), WIDE),
            pltpu.VMEM((pairs, 2 * BQ, 128), WIDE),
            pltpu.VMEM((pairs, 2 * BQ, 128), WIDE),
            pltpu.VMEM((pairs, 2 * BQ, 128), WIDE),
        ],
        1000,
    )(bounds, queries, before, here, after, qdoc, kdoc)


def full_backward(with_self, bounds, queries, grads, att, lse, before, here, after, qdoc, kdoc):
    streams, rows, width = queries.shape
    pairs = width // PAIR
    blocks = 3 * rows // BK
    kv_spec = whole_spec((2, rows, width))
    grad_spec = whole_spec((2, rows, width))
    return local_call(
        functools.partial(full_backward_kernel, with_self),
        (streams, rows // BQ),
        [rows_spec(width)] * 3
        + [rows_spec(128), kv_spec, kv_spec, kv_spec, QDOC_SPEC, whole_spec((blocks, 1, BK))],
        [rows_spec(width), grad_spec, grad_spec, grad_spec],
        [
            shaped((streams, rows, width), LOW),
            shaped((2, rows, width), LOW),
            shaped((2, rows, width), WIDE),
            shaped((2, rows, width), LOW),
        ],
        [
            pltpu.VMEM((2, 3 * rows, width), LOW),
            pltpu.VMEM((2, width, 3 * rows), WIDE),
            pltpu.VMEM((pairs, 2 * BQ, 128), WIDE),
        ],
        1000,
    )(bounds, queries, grads, att, lse, before, here, after, qdoc, kdoc)


def spread_index():
    row, lane = np.arange(BQ)[:, None], np.arange(128)[None, :]
    return bucket_table((row - lane) % 128).astype(np.int32)


def skew_index():
    row, lane = np.arange(BQ)[:, None], np.arange(128)[None, :]
    return ((row - lane) % 128).astype(np.int32)


def bucket_hot(heads):
    offsets = np.arange(128)
    hot = np.zeros((heads, 128, 128), np.float32)
    for head in range(heads):
        hot[head, offsets, head * BUCKETS + bucket_table(offsets)] = 1.0
    return hot


def causal_forward(own, bounds, queries, before, here, qdoc, kdoc, tables, own_pair):
    streams, rows, width = queries.shape
    pairs = width // PAIR
    blocks = 2 * rows // 128
    kv_spec = whole_spec((2, rows, width))
    specs = [rows_spec(width), kv_spec, kv_spec, QDOC_SPEC, whole_spec((blocks, 1, 128))]
    specs += [rows_spec(128), whole_spec((BQ, 128))]
    operands = [bounds, queries, before, here, qdoc, kdoc, tables, jnp.asarray(spread_index())]
    if own:
        specs.append(pair_rows_spec(width))
        operands.append(own_pair)
    return local_call(
        functools.partial(causal_forward_kernel, own),
        (streams, rows // BQ),
        specs,
        [rows_spec(width), rows_spec(width), rows_spec(128)],
        [
            shaped((streams, rows, width), LOW),
            shaped((streams, rows, width), WIDE),
            shaped((streams, rows, 128), WIDE),
        ],
        [
            pltpu.VMEM((2, 2 * rows, width), LOW),
            pltpu.VMEM((blocks, pairs, 2 * BQ, 128), WIDE),
            pltpu.VMEM((pairs, 2 * BQ, 128), WIDE),
            pltpu.VMEM((pairs, 2 * BQ, 128), WIDE),
            pltpu.VMEM((pairs, 2 * BQ, 128), WIDE),
        ],
        1000,
    )(*operands)


def causal_backward(
    own, bounds, queries, grads, att, lse, before, here, qdoc, kdoc, tables, own_pair
):
    streams, rows, width = queries.shape
    pairs = width // PAIR
    blocks = 2 * rows // 128
    kv_spec = whole_spec((2, rows, width))
    grad_spec = whole_spec((2, rows, width))
    specs = [rows_spec(width)] * 3 + [rows_spec(128), kv_spec, kv_spec, QDOC_SPEC]
    specs += [whole_spec((blocks, 1, 128)), rows_spec(128), whole_spec((BQ, 128))]
    specs += [whole_spec((BQ, 128)), whole_spec((2 * pairs, 128, 128))]
    operands = [bounds, queries, grads, att, lse, before, here, qdoc, kdoc, tables]
    operands += [jnp.asarray(spread_index()), jnp.asarray(skew_index())]
    operands += [jnp.asarray(bucket_hot(2 * pairs), LOW)]
    out_specs = [rows_spec(width), rows_spec(128), grad_spec, grad_spec]
    out_shape = [
        shaped((streams, rows, width), LOW),
        shaped((streams, rows, 128), LOW),
        shaped((2, rows, width), LOW),
        shaped((2, rows, width), WIDE),
    ]
    if own:
        specs.append(pair_rows_spec(width))
        operands.append(own_pair)
        out_specs.append(pair_rows_spec(width))
        out_shape.append(shaped((streams, 2, rows, width), LOW))
    return local_call(
        functools.partial(causal_backward_kernel, own),
        (streams, rows // BQ),
        specs,
        out_specs,
        out_shape,
        [
            pltpu.VMEM((2, 2 * rows, width), LOW),
            pltpu.VMEM((2, width, 2 * rows), WIDE),
            pltpu.VMEM((pairs, 2 * BQ, 128), WIDE),
            pltpu.VMEM((pairs, 2 * BQ, 128), WIDE),
        ],
        1000,
    )(*operands)


SUM_ROWS = 256
SUM_WIDTH = 256
SUM_DELAY = 3
MESH = pl.DeviceIdType.MESH


def blocks_of(shape):
    return [(shape[0], column) for column in range(0, shape[1], SUM_WIDTH)]


def tree_kernel(count, pieces, *refs):
    sources, targets, refs = refs[:pieces], refs[pieces : 2 * pieces], refs[2 * pieces :]
    x_ref, out_ref, total, part, landed, sent_up, came_up, sent_down, came_down, filled = refs
    chunks = x_ref.shape[0] // SUM_ROWS
    ring = part.shape[0]
    fills, drains, at = [], [], 0
    for place, (source, target) in enumerate(zip(sources, targets)):
        for rows, column in blocks_of(source.shape):
            columns = pl.ds(column, SUM_WIDTH)
            inside, outside = pl.ds(at, rows), filled.at[len(fills)]
            fills.append(pltpu.make_async_copy(source.at[:, columns], x_ref.at[inside], outside))
            drains.append(pltpu.make_async_copy(out_ref.at[inside], target.at[:, columns], outside))
            at += rows
    if at < x_ref.shape[0]:
        x_ref[at:, :] = jnp.zeros((x_ref.shape[0] - at, SUM_WIDTH), LOW)
    for fill in fills:
        fill.start()
    tall = count // 2
    place = lax.axis_index("seq")
    column = lax.rem(place, 2)
    row = place // 2
    beside = place + 1 - 2 * column

    def everyone(act):
        act(beside, None)
        act(place - 2, row > 0)
        act(place + 2, row < tall - 1)

    barrier = pltpu.get_barrier_semaphore()

    def greet(device, there):
        def signal():
            pl.semaphore_signal(barrier, inc=1, device_id={"seq": device}, device_id_type=MESH)

        if there is None:
            signal()
        else:
            pl.when(there)(signal)

    everyone(greet)
    friends = 1 + (row > 0).astype(jnp.int32) + (row < tall - 1).astype(jnp.int32)
    pl.semaphore_wait(barrier, friends)

    def role(chunk):
        kind = lax.rem(chunk, 6 + tall)
        spine = kind < 6
        top = jnp.where(spine, tall // 2 - 1 + lax.rem(kind // 2, 2), kind - 6)
        main = column == lax.rem(kind, 2)
        walks = main | jnp.logical_not(spine)
        here = row == top
        children = (
            main & (spine | here),
            walks & (row > 0) & (row <= top),
            walks & (row < tall - 1) & (row >= top),
        )
        reach = jnp.where(row < top, row, tall - 1 - row)
        reach = jnp.where(here, jnp.maximum(top, tall - 1 - top), reach)
        level = jnp.where(
            spine, jnp.where(main, 1 + reach, 0), reach + (here & main).astype(jnp.int32)
        )
        depth = jnp.abs(row - top) + jnp.logical_not(main).astype(jnp.int32)
        sideways = jnp.logical_not(main) & (spine | here)
        return children, level, depth, main & here, sideways, row < top

    devices = (beside, place - 2, place + 2)

    def rows_at(chunk):
        return pl.ds(pl.multiple_of(chunk * SUM_ROWS, SUM_ROWS), SUM_ROWS)

    def up_copy(chunk, slot, device):
        at = lax.rem(chunk, ring)
        return pltpu.make_async_remote_copy(
            src_ref=part.at[at],
            dst_ref=landed.at[at, slot],
            send_sem=sent_up.at[at],
            recv_sem=came_up.at[at, slot],
            device_id={"seq": device},
            device_id_type=MESH,
        )

    def down_copy(chunk, slot, device):
        at = lax.rem(chunk, ring)
        return pltpu.make_async_remote_copy(
            src_ref=out_ref.at[rows_at(chunk)],
            dst_ref=out_ref.at[rows_at(chunk)],
            send_sem=sent_down.at[at, slot],
            recv_sem=came_down.at[at],
            device_id={"seq": device},
            device_id_type=MESH,
        )

    def spread(chunk, children):
        for slot, child in enumerate(children):

            @pl.when(child)
            def _():
                down_copy(chunk, slot, devices[slot]).start()

    def climb(chunk, children, root, sideways, rising):
        at = lax.rem(chunk, ring)
        total[...] = x_ref[rows_at(chunk), :].astype(WIDE)
        for slot, child in enumerate(children):

            @pl.when(child)
            def _():
                up_copy(chunk, slot, devices[slot]).wait_recv()
                total[...] += landed[at, slot].astype(WIDE)

        @pl.when(root)
        def _():
            out_ref[rows_at(chunk), :] = total[...].astype(LOW)
            spread(chunk, children)

        @pl.when(jnp.logical_not(root))
        def _():
            part[at] = total[...].astype(LOW)

            @pl.when(sideways)
            def _():
                up_copy(chunk, 0, beside).start()

            @pl.when(jnp.logical_not(sideways) & rising)
            def _():
                up_copy(chunk, 1, place + 2).start()

            @pl.when(jnp.logical_not(sideways) & jnp.logical_not(rising))
            def _():
                up_copy(chunk, 2, place - 2).start()

    def fall(chunk, children):
        down_copy(chunk, 0, beside).wait_recv()
        up_copy(chunk, 0, beside).wait_send()
        spread(chunk, children)

    def finish(chunk, children):
        for slot, child in enumerate(children):

            @pl.when(child)
            def _():
                down_copy(chunk, slot, devices[slot]).wait_send()

    levels = tall + 1
    for fill in fills:
        fill.wait()

    def period(time, carry):
        def at_level(place_in_line, act):
            chunk = time - SUM_DELAY * place_in_line

            @pl.when((chunk >= 0) & (chunk < chunks))
            def _():
                act(chunk)

        def finish_step(chunk):
            finish(chunk, role(chunk)[0])

        at_level(2 * levels + 1, finish_step)
        for depth_now in range(levels, 0, -1):

            def fall_step(chunk, depth_now=depth_now):
                children, _, depth, root, _, _ = role(chunk)

                @pl.when((depth == depth_now) & jnp.logical_not(root))
                def _():
                    fall(chunk, children)

            at_level(levels + depth_now, fall_step)
        for level_now in range(levels - 1, -1, -1):

            def climb_step(chunk, level_now=level_now):
                children, level, _, root, sideways, rising = role(chunk)

                @pl.when(level == level_now)
                def _():
                    climb(chunk, children, root, sideways, rising)

            at_level(level_now, climb_step)
        return carry

    lax.fori_loop(0, chunks + SUM_DELAY * (2 * levels + 1), period, 0)
    for drain in drains:
        drain.start()
    for drain in drains:
        drain.wait()


def link_sum(pieces, count):
    levels = count // 2 + 1
    blocks = [block for piece in pieces for block in blocks_of(piece.shape)]
    chunks = -(-sum(rows for rows, _ in blocks) // SUM_ROWS)
    ring = min(chunks, SUM_DELAY * (2 * levels + 1) + 1)
    block = (SUM_ROWS, SUM_WIDTH)
    anywhere = [pl.BlockSpec(memory_space=pl.ANY)] * len(pieces)
    return pl.pallas_call(
        functools.partial(tree_kernel, count, len(pieces)),
        in_specs=anywhere,
        out_specs=anywhere,
        out_shape=[shaped(piece.shape, LOW) for piece in pieces],
        scratch_shapes=[
            pltpu.VMEM((chunks * SUM_ROWS, SUM_WIDTH), LOW),
            pltpu.VMEM((chunks * SUM_ROWS, SUM_WIDTH), LOW),
            pltpu.VMEM(block, WIDE),
            pltpu.VMEM((ring,) + block, LOW),
            pltpu.VMEM((ring, 3) + block, LOW),
            pltpu.SemaphoreType.DMA((ring,)),
            pltpu.SemaphoreType.DMA((ring, 3)),
            pltpu.SemaphoreType.DMA((ring, 3)),
            pltpu.SemaphoreType.DMA((ring,)),
            pltpu.SemaphoreType.DMA((len(blocks),)),
        ],
        compiler_params=pltpu.CompilerParams(
            collective_id=0, has_side_effects=True, vmem_limit_bytes=56 * 1024 * 1024
        ),
        cost_estimate=pl.CostEstimate(flops=1000, bytes_accessed=1000, transcendentals=0),
    )(*pieces)


PLAN = (
    "e012ee0eee10ee20102010112122020101212020",
    "101212F020011212e200Ce1e11Ce2eGe202ee100",
    "S122D00WeeWWee",
)


class Kept:
    pass


class Order:
    def __init__(self):
        self.token = None

    def enter(self, *values):
        if self.token is None:
            return values
        values, _ = lax.optimization_barrier((values, self.token))
        return values

    def leave(self, value):
        self.token = value


def swap_core(value):
    count = lax.axis_size("tp")
    return lax.ppermute(value, "tp", [(place, place ^ 1) for place in range(count)])


def swap_chip(low):
    count = lax.axis_size("tp")
    hop = 2
    got = lax.ppermute(low, "tp", [(place, place ^ hop) for place in range(count)])
    while 2 * hop < count:
        hop *= 2
        low = (low.astype(WIDE) + got.astype(WIDE)).astype(LOW)
        got = lax.ppermute(low, "tp", [(place, place ^ hop) for place in range(count)])
    return low, got


def core_index():
    return lax.rem(lax.axis_index("tp"), 2)


def half_rows(rows, mine):
    half = rows.shape[1] // 2
    core = core_index() if mine else 1 - core_index()
    return lax.dynamic_slice_in_dim(rows, core * half, half, 1)


def natural_rows(mine, other):
    first = core_index() == 0
    return jnp.concatenate([jnp.where(first, mine, other), jnp.where(first, other, mine)], 1)


def project(rows, weight):
    return jnp.einsum("gsd,df->gsf", rows, weight, preferred_element_type=WIDE)


def back_project(grads, weight):
    return jnp.einsum("gsf,df->gsd", grads, weight, preferred_element_type=WIDE)


def weight_grad(rows, grads):
    return jnp.einsum("gsd,gsf->df", rows, grads, preferred_element_type=WIDE)


def split_rows(cells):
    if isinstance(cells, tuple):
        return list(cells)
    return [half_rows(cells, True), half_rows(cells, False)]


def rows_weight_grad(lefts, rights):
    lefts = [part for cells in lefts for part in split_rows(cells)]
    rights = [part for cells in rights for part in split_rows(cells)]
    return weight_grad(jnp.concatenate(lefts, 1), jnp.concatenate(rights, 1))


def norm_forward(resid, gain, shift):
    mean = jnp.mean(resid, -1, keepdims=True)
    centred = resid - mean
    inverse = lax.rsqrt(jnp.mean(centred * centred, -1, keepdims=True) + 1e-05)
    normed = centred * inverse
    return (normed * gain + shift, normed, inverse)


def norm_backward(grad_out, saved, gain):
    normed, inverse = saved
    grad_normed = grad_out * gain
    grad_resid = inverse * (
        grad_normed
        - jnp.mean(grad_normed, -1, keepdims=True)
        - normed * jnp.mean(grad_normed * normed, -1, keepdims=True)
    )
    sums = jnp.stack([jnp.sum(grad_out * normed, (0, 1)), jnp.sum(grad_out, (0, 1))])
    return (grad_resid, sums)


def gelu_both(hidden):
    scaled = hidden * (0.5**0.5)
    half = 0.5 * lax.erf(scaled) + 0.5
    slope = half + hidden * jnp.exp(-(scaled * scaled)) * ((2.0 * math.pi) ** -0.5)
    return ((hidden * half).astype(LOW), slope.astype(LOW))


def passed_along(value, steps):
    count = lax.axis_size("seq")
    if steps > 0:
        pairs = [(place, place + 1) for place in range(count - 1)]
    else:
        pairs = [(place + 1, place) for place in range(count - 1)]
    return lax.ppermute(value, "seq", pairs)


def doc_index(positions, ends):
    return jnp.sum((positions[:, None] >= ends[None, :]).astype(jnp.int32), 1)


def pick(owner, values):
    match = owner[:, None] == jnp.arange(values.shape[0], dtype=jnp.int32)[None, :]
    return jnp.sum(jnp.where(match, values[None, :], 0), 1)


def pad_tables(tables):
    missing = 128 - tables.shape[-1]
    return jnp.pad(tables, ((0, 0), (0, 0), (0, missing))) if missing else tables


def sum_seq(values, turn):
    places = list(range(lax.axis_size("seq")))
    return lax.psum(tuple(values), "seq", axis_index_groups=[places[turn:] + places[:turn]])


def per_device(
    enc_input,
    dec_input,
    enc_cotan,
    dec_cotan,
    doc_lengths,
    src_padding,
    enc_qkv,
    enc_wout,
    enc_gain,
    enc_bias,
    enc_up,
    enc_down,
    post_gain,
    post_bias,
    self_qkv,
    self_rel,
    self_wout,
    self_gain,
    self_bias,
    cross_wq,
    cross_wkv,
    cross_wout,
    cross_gain,
    cross_bias,
    ffn_up,
    ffn_down,
    ffn_gain,
    ffn_bias,
):
    rows = enc_input.shape[0]
    half = rows // 2
    streams = dec_input.shape[0]
    table_width = self_rel.shape[1]
    base = lax.axis_index("seq") * rows
    total_rows = rows * lax.axis_size("seq")
    ends = jnp.cumsum(doc_lengths)
    starts = ends - doc_lengths
    key_pos = base - rows + jnp.arange(3 * rows, dtype=jnp.int32)
    key_valid = (key_pos >= 0) & (key_pos < total_rows)
    key_owner = doc_index(key_pos, ends)
    key_doc = jnp.where(key_valid, key_owner, -1)
    key_pad = (
        lax.dynamic_slice_in_dim(jnp.pad(src_padding, (rows, rows)), base, 3 * rows) == 1
    )
    key_first = key_pos == pick(key_owner, starts)
    qdoc = key_doc[rows : 2 * rows][:, None]
    enc_kdoc = jnp.where(key_pad, key_doc, -1).reshape(-1, 1, BK)
    cross_kdoc = jnp.where(key_pad | key_first, key_doc, -1).reshape(-1, 1, BK)
    self_kdoc = key_doc[: 2 * rows].reshape(-1, 1, 128)
    owners = key_owner[rows : 2 * rows]
    block_first = pick(owners[::BQ], starts) - base + rows
    block_end = pick(owners[BQ - 1 :: BQ], ends) - base + rows
    full_bounds = jnp.stack([block_first // BK, (block_end + BK - 1) // BK])
    self_bounds = block_first // 128

    order = Order()
    enter, leave = order.enter, order.leave
    enc, cross = Kept(), Kept()
    dec = [Kept() for _ in range(streams)]
    straight_rows = enc_input[None]

    def halves(att, weight):
        other = project(half_rows(att, False), weight).astype(LOW)
        mine = project(half_rows(att, True), weight)
        return mine, other

    def back_halves(grads, weight):
        other = back_project(half_rows(grads, False), weight).astype(LOW)
        mine = back_project(half_rows(grads, True), weight)
        return mine, other

    def exchange(mine, other):
        got = swap_core(other)
        yield
        mine, got = enter(mine, got)
        low = (mine + got.astype(WIDE)).astype(LOW)
        leave(low)
        low, got = swap_chip(low)
        yield
        low, got = enter(low, got)
        return low.astype(WIDE) + got.astype(WIDE)

    def close_branch(resid, mine, other, gain, shift):
        total = yield from exchange(mine, other)
        output, normed, inverse = norm_forward(resid + total, gain, shift)
        low = output.astype(LOW)
        leave(low)
        return output, low, swap_core(low), (normed, inverse)

    def open_branch(grad, saved, gain):
        grad, sums = norm_backward(grad, saved, gain)
        low = grad.astype(LOW)
        leave(low)
        return grad, low, swap_core(low), sums

    def encoder():
        (enc_rows,) = enter(enc_input)
        pair = jnp.einsum("sd,cdf->csf", enc_rows, enc_qkv[1:], preferred_element_type=WIDE).astype(LOW)
        enc.pair = pair
        enc.before = passed_along(pair, 1)
        enc.after = passed_along(pair, -1)
        enc.query = project(enc_rows[None], enc_qkv[0]).astype(LOW)
        leave(enc.query)
        yield
        query, before, after = enter(enc.query, enc.before, enc.after)
        enc.query, enc.before, enc.after = query, before, after
        att, wide, lse = full_forward(
            True, full_bounds, query, before, enc.pair, after, qdoc, enc_kdoc
        )
        enc.att, enc.wide, enc.lse = att, wide, lse
        mine, other = halves(att, enc_wout)
        leave(mine)
        resid = half_rows(straight_rows, True).astype(WIDE)
        resid, mine, got, enc.saved_att = yield from close_branch(
            resid, mine, other, enc_gain, enc_bias
        )
        yield
        mine, got = enter(mine, got)
        middle = jnp.concatenate([mine, got], 1)
        act, slope = gelu_both(project(middle, enc_up))
        enc.middle, enc.act, enc.slope = middle, act, slope
        other = project(act[:, half:], enc_down).astype(LOW)
        mine = project(act[:, :half], enc_down)
        leave(mine)
        resid, mine, got, enc.saved_ffn = yield from close_branch(
            resid, mine, other, post_gain, post_bias
        )
        yield
        mine, got = enter(mine, got)
        enc.final = natural_rows(mine, got)
        pair = jnp.einsum(
            "sd,cdf->csf", enc.final[0], cross_wkv, preferred_element_type=WIDE
        ).astype(LOW)
        leave(pair)
        cross.pair = pair
        cross.before = passed_along(pair, 1)
        cross.after = passed_along(pair, -1)
        yield
        parts = enter(*[dec[stream].cross_parts for stream in range(streams)])
        to_before = sum(part[0].astype(WIDE) for part in parts).astype(LOW)
        to_after = sum(part[2].astype(WIDE) for part in parts).astype(LOW)
        here = sum(part[1] for part in parts)
        leave(to_after)
        from_next = passed_along(to_before, -1)
        from_last = passed_along(to_after, 1)
        yield
        here, from_next, from_last = enter(here, from_next, from_last)
        pair_grad = (here + from_next.astype(WIDE) + from_last.astype(WIDE)).astype(LOW)
        cross.pair_grad = pair_grad
        extra = jnp.einsum("csf,cdf->sd", pair_grad, cross_wkv, preferred_element_type=WIDE)[None]
        mine, other = half_rows(extra, True), half_rows(extra, False).astype(LOW)
        leave(other)
        total = yield from exchange(mine, other)
        grad = half_rows(enc_cotan[None], True).astype(WIDE) + total
        grad, mine, got, enc.post_sums = open_branch(grad, enc.saved_ffn, post_gain)
        yield
        mine, got = enter(mine, got)
        ffn_rows = jnp.concatenate([mine, got], 1)
        grad_act = jnp.einsum("gsd,fd->gsf", ffn_rows, enc_down, preferred_element_type=WIDE)
        hidden_grad = (grad_act * enc.slope.astype(WIDE)).astype(LOW)
        enc.ffn_rows, enc.hidden_grad = ffn_rows, hidden_grad
        other = back_project(hidden_grad[:, half:], enc_up).astype(LOW)
        mine = back_project(hidden_grad[:, :half], enc_up)
        leave(mine)
        total = yield from exchange(mine, other)
        grad, mine, got, enc.att_sums = open_branch(grad + total, enc.saved_att, enc_gain)
        yield
        mine, got = enter(mine, got)
        enc.att_rows = (mine, got)
        query_grad, to_before, here, to_after = full_backward(
            True,
            full_bounds,
            enc.query,
            att_grad(mine, got, enc_wout),
            enc.wide,
            enc.lse,
            enc.before,
            enc.pair,
            enc.after,
            qdoc,
            enc_kdoc,
        )
        leave(query_grad)
        enc.query_grad = query_grad
        from_next = passed_along(to_before, -1)
        from_last = passed_along(to_after, 1)
        yield
        here, from_next, from_last = enter(here, from_next, from_last)
        pair_grad = (here + from_next.astype(WIDE) + from_last.astype(WIDE)).astype(LOW)
        enc.pair_grad = pair_grad
        partial_value = back_project(query_grad, enc_qkv[0]) + jnp.einsum(
            "csf,cdf->sd", pair_grad, enc_qkv[1:], preferred_element_type=WIDE
        )
        mine, other = half_rows(partial_value, True), half_rows(partial_value, False).astype(LOW)
        leave(other)
        total = yield from exchange(mine, other)
        low = (grad + total).astype(LOW)
        leave(low)
        got = swap_core(low)
        yield
        low, got = enter(low, got)
        enc.grad = natural_rows(low, got)[0]
        leave(enc.grad)
        yield

    def att_grad(mine, other, weight):
        return natural_rows(
            jnp.einsum("gsd,fd->gsf", mine, weight, preferred_element_type=WIDE).astype(LOW),
            jnp.einsum("gsd,fd->gsf", other, weight, preferred_element_type=WIDE).astype(LOW),
        )

    def decoder(stream):
        own = stream > 0
        kept = dec[stream]
        (dec_rows,) = enter(dec_input[stream : stream + 1])
        pair = jnp.einsum(
            "gsd,cdf->gcsf", dec_rows, self_qkv[1:], preferred_element_type=WIDE
        ).astype(LOW)
        query = project(dec_rows, self_qkv[0]).astype(LOW)
        table = pad_tables(project(dec_rows, self_rel))
        leave((pair, query, table))
        if stream == 0:
            cross.main = pair[0]
            cross.main_before = passed_along(pair[0], 1)
        yield
        main = cross.main
        query, main_before = enter(query, cross.main_before)
        cross.main_before = main_before
        own_pair = pair if own else None
        att, wide, lse = causal_forward(
            own, self_bounds, query, main_before, main, qdoc, self_kdoc, table, own_pair
        )
        kept.self_att = att
        mine, other = halves(att, self_wout)
        leave(mine)
        resid, mine, got, saved_self = yield from close_branch(
            half_rows(dec_rows, True).astype(WIDE), mine, other, self_gain, self_bias
        )
        yield
        mine, got = enter(mine, got)
        kept.first = (mine, got)
        cross_query = natural_rows(
            project(mine, cross_wq).astype(LOW), project(got, cross_wq).astype(LOW)
        )
        leave(cross_query)
        yield
        cross_query, before, after = enter(cross_query, cross.before, cross.after)
        cross.before, cross.after = before, after
        cross_att, cross_wide, cross_lse = full_forward(
            False, full_bounds, cross_query, before, cross.pair, after, qdoc, cross_kdoc
        )
        kept.cross_att = cross_att
        mine, other = halves(cross_att, cross_wout)
        leave(mine)
        resid, mine, got, saved_cross = yield from close_branch(
            resid, mine, other, cross_gain, cross_bias
        )
        yield
        mine, got = enter(mine, got)
        second = jnp.concatenate([mine, got], 1)
        act, slope = gelu_both(project(second, ffn_up))
        kept.second, kept.act = second, act
        other = project(act[:, half:], ffn_down).astype(LOW)
        mine = project(act[:, :half], ffn_down)
        leave(mine)
        total = yield from exchange(mine, other)
        output, normed, inverse = norm_forward(resid + total, ffn_gain, ffn_bias)
        final_mine = output.astype(LOW)
        final_got = swap_core(final_mine)
        grad = half_rows(dec_cotan[stream : stream + 1], True).astype(WIDE)
        grad, mine, got, kept.ffn_sums = open_branch(grad, (normed, inverse), ffn_gain)
        yield
        mine, got = enter(mine, got)
        ffn_rows = jnp.concatenate([mine, got], 1)
        grad_act = jnp.einsum("gsd,fd->gsf", ffn_rows, ffn_down, preferred_element_type=WIDE)
        hidden_grad = (grad_act * slope.astype(WIDE)).astype(LOW)
        kept.ffn_rows, kept.hidden_grad = ffn_rows, hidden_grad
        other = back_project(hidden_grad[:, half:], ffn_up).astype(LOW)
        mine = back_project(hidden_grad[:, :half], ffn_up)
        leave(mine)
        total = yield from exchange(mine, other)
        grad, mine, got, kept.cross_sums = open_branch(grad + total, saved_cross, cross_gain)
        kept.final = natural_rows(final_mine, final_got)
        yield
        mine, got = enter(mine, got)
        kept.cross_rows = (mine, got)
        query_grad, *kept.cross_parts = full_backward(
            False,
            full_bounds,
            cross_query,
            att_grad(mine, got, cross_wout),
            cross_wide,
            cross_lse,
            cross.before,
            cross.pair,
            cross.after,
            qdoc,
            cross_kdoc,
        )
        kept.cross_query_grad = query_grad
        mine, other = back_halves(query_grad, cross_wq)
        leave(mine)
        total = yield from exchange(mine, other)
        grad, mine, got, kept.self_sums = open_branch(grad + total, saved_self, self_gain)
        yield
        mine, got = enter(mine, got)
        kept.self_rows = (mine, got)
        query_grad, table_grad, to_before, here, *own_grad = causal_backward(
            own,
            self_bounds,
            query,
            att_grad(mine, got, self_wout),
            wide,
            lse,
            main_before,
            main,
            qdoc,
            self_kdoc,
            table,
            own_pair,
        )
        table_grad = table_grad[:, :, :table_width]
        kept.table_grad = table_grad
        kept.self_parts = (to_before, here)
        leave(query_grad)
        if own:
            pair_grad = own_grad[0][0]
        else:
            yield
            parts = enter(*[dec[item].self_parts for item in range(streams)])
            to_before = sum(part[0].astype(WIDE) for part in parts).astype(LOW)
            here = sum(part[1] for part in parts)
            leave(to_before)
            from_next = passed_along(to_before, -1)
            yield
            here, from_next = enter(here, from_next)
            pair_grad = (here + from_next.astype(WIDE)).astype(LOW)
        kept.query_grad, kept.pair_grad = query_grad, pair_grad
        partial_value = (
            back_project(query_grad, self_qkv[0])
            + jnp.einsum("csf,cdf->sd", pair_grad, self_qkv[1:], preferred_element_type=WIDE)
            + back_project(table_grad, self_rel)
        )
        mine, other = half_rows(partial_value, True), half_rows(partial_value, False).astype(LOW)
        leave(other)
        total = yield from exchange(mine, other)
        low = (grad + total).astype(LOW)
        leave(low)
        got = swap_core(low)
        yield
        low, got = enter(low, got)
        kept.grad = natural_rows(low, got)
        leave(kept.grad)
        yield

    weights = Kept()

    def ffn_weights():
        acts, grads = enter([kept.act for kept in dec], [kept.ffn_rows for kept in dec])
        down = weight_grad(jnp.concatenate(acts), jnp.concatenate(grads)).astype(LOW)
        seconds, grads = [kept.second for kept in dec], [kept.hidden_grad for kept in dec]
        up = weight_grad(jnp.concatenate(seconds), jnp.concatenate(grads)).astype(LOW)
        leave((down, up))
        weights.ffn = sum_seq((down, up), 0)
        yield

    def cross_weights():
        atts, grads = enter([kept.cross_att for kept in dec], [kept.cross_rows for kept in dec])
        wout = rows_weight_grad(atts, grads).astype(LOW)
        firsts = [kept.first for kept in dec]
        wq = rows_weight_grad(firsts, [kept.cross_query_grad for kept in dec]).astype(LOW)
        leave((wout, wq))
        weights.cross = (wout, wq)
        yield
        (final,) = enter(enc.final)
        wkv = jnp.einsum(
            "sd,csf->cdf", final[0], cross.pair_grad, preferred_element_type=WIDE
        ).astype(LOW)
        leave(wkv)
        weights.cross = list(weights.cross) + [wkv]
        yield

    def enc_ffn_weights():
        act, grads = enter(enc.act, enc.ffn_rows)
        down = weight_grad(act, grads).astype(LOW)
        up = weight_grad(enc.middle, enc.hidden_grad).astype(LOW)
        leave((down, up))
        weights.enc = [down, up]
        yield

    def flat(cells):
        if cells.shape[-1] % SUM_WIDTH:
            cells = jnp.swapaxes(cells, -1, -2)
        return cells.reshape(-1, cells.shape[-1])

    def unflat(cells, shape):
        if shape[-1] % SUM_WIDTH:
            return jnp.swapaxes(cells.reshape(shape[:-2] + (shape[-1], shape[-2])), -1, -2)
        return cells.reshape(shape)

    def self_weights():
        atts, grads = enter([kept.self_att for kept in dec], [kept.self_rows for kept in dec])
        wout = rows_weight_grad(atts, grads).astype(LOW)
        tables = jnp.concatenate([kept.table_grad for kept in dec], 0)
        rel = weight_grad(dec_input, tables).astype(LOW)
        queries = jnp.concatenate([kept.query_grad for kept in dec])
        query = weight_grad(dec_input, queries).astype(LOW)
        sides = [jnp.stack([kept.pair_grad[side] for kept in dec]) for side in range(2)]
        key, value = [weight_grad(dec_input, side).astype(LOW) for side in sides]
        leave((wout, rel, query, key, value))
        weights.self = [wout, rel, query, key, value]
        yield

    def finished():
        (finals,) = enter([kept.final for kept in dec])
        weights.final = jnp.concatenate(finals, 0)
        leave(weights.final)
        yield

    def enc_weights():
        query_grad, grads = enter(enc.query_grad, enc.att_rows)
        query = weight_grad(straight_rows, query_grad).astype(LOW)
        wout = rows_weight_grad([enc.att], [grads]).astype(LOW)
        leave((query, wout))
        yield
        (pair_grad,) = enter(enc.pair_grad)
        key = weight_grad(straight_rows, pair_grad[:1]).astype(LOW)
        value = weight_grad(straight_rows, pair_grad[1:]).astype(LOW)
        sums = jnp.concatenate(
            [
                enc.att_sums,
                enc.post_sums,
                sum(kept.self_sums for kept in dec),
                sum(kept.cross_sums for kept in dec),
                sum(kept.ffn_sums for kept in dec),
            ],
            0,
        )
        sums = sums + swap_core(sums)
        sums = jnp.pad(sums, ((0, -sums.shape[0] % 16), (0, 0))).astype(LOW)
        parts = weights.cross + weights.enc + weights.self + [wout, query, key, value, sums]
        pieces = [flat(part) for part in parts]
        leave((wout, query, key, value, sums))
        yield
        pieces = enter(*pieces)
        summed = link_sum(pieces, lax.axis_size("seq"))
        leave(summed[0])
        (weights.ffn,) = enter(weights.ffn)
        weights.last = [
            unflat(cells.astype(WIDE), part.shape) for cells, part in zip(summed, parts)
        ]
        yield

    tasks = {"e": encoder(), "F": ffn_weights(), "C": cross_weights()}
    tasks.update({"D": finished(), "G": enc_ffn_weights(), "S": self_weights(), "W": enc_weights()})
    tasks.update({str(stream): decoder(stream) for stream in range(streams)})
    for item in "".join(PLAN):
        next(tasks[item], None)
    for task in tasks.values():
        for _ in task:
            pass

    ffn_down_grad, ffn_up_grad = [value.astype(WIDE) for value in weights.ffn]
    cross_wout_grad, cross_wq_grad, cross_wkv_grad, *found = weights.last
    enc_down_grad, enc_up_grad, *found = found
    self_wout_grad, self_rel_grad, *found = found
    self_qkv_grad = jnp.stack(found[:3])
    enc_wout_grad, sums = found[3], found[7]
    enc_qkv_grad = jnp.stack(found[4:7])
    return (
        enc.final[0],
        weights.final,
        enc.grad,
        jnp.concatenate([kept.grad for kept in dec], 0),
        enc_qkv_grad,
        enc_wout_grad,
        sums[0],
        sums[1],
        enc_up_grad,
        enc_down_grad,
        sums[2],
        sums[3],
        self_qkv_grad,
        self_rel_grad,
        self_wout_grad,
        sums[4],
        sums[5],
        cross_wq_grad,
        cross_wkv_grad,
        cross_wout_grad,
        sums[6],
        sums[7],
        ffn_up_grad,
        ffn_down_grad,
        sums[8],
        sums[9],
    )


def solution(mesh):
    in_specs = (
        P("seq", None),
        P(None, "seq", None),
        P("seq", None),
        P(None, "seq", None),
        P(),
        P(),
        P(None, None, "tp"),
        P("tp", None),
        P(),
        P(),
        P(None, "tp"),
        P("tp", None),
        P(),
        P(),
        P(None, None, "tp"),
        P(None, "tp"),
        P("tp", None),
        P(),
        P(),
        P(None, "tp"),
        P(None, None, "tp"),
        P("tp", None),
        P(),
        P(),
        P(None, "tp"),
        P("tp", None),
        P(),
        P(),
    )
    out_specs = (
        P("seq", None),
        P(None, "seq", None),
        P("seq", None),
        P(None, "seq", None),
        P(None, None, "tp"),
        P("tp", None),
        P(),
        P(),
        P(None, "tp"),
        P("tp", None),
        P(),
        P(),
        P(None, None, "tp"),
        P(None, "tp"),
        P("tp", None),
        P(),
        P(),
        P(None, "tp"),
        P(None, None, "tp"),
        P("tp", None),
        P(),
        P(),
        P(None, "tp"),
        P("tp", None),
        P(),
        P(),
    )
    return jax.shard_map(
        per_device, mesh=mesh, in_specs=in_specs, out_specs=out_specs, check_vma=False
    )
```
